256 devices in a mesh: gx: 16 (over y, x), gy: 8 (over z_lo, core), gz: 2 (over z_hi).
Axes of the slice: x: 4, y: 4, z: 8 (z_hi: 2, z_lo: 4; z = z_hi * 4 + z_lo), core: 2. Of those that a mesh axis runs over, the one named last changes fastest.
Arguments:
- adjoint_source: float32 [2, 128, 256, 256], P(None, 'gx', 'gy', 'gz'), may hold values from -6 to 6
- velocity: float32 [128, 256, 256], P('gx', 'gy', 'gz'), may hold values from 1.5 to 4.5
- damping: float32 [128, 256, 256], P('gx', 'gy', 'gz'), may hold values from 0.02 to 0.6
- face_rounds: int32 [16, 8, 2, 6], P('gx', 'gy', 'gz'), may hold values from 0 to 5, as said below
- aggregates: int32 [32, 32, 2], P('gx', 'gy', 'gz'), may hold values from 0 to 511, as said below
Outputs:
- adjoint_field: float32 [2, 128, 256, 256], P(None, 'gx', 'gy', 'gz')
The draws below stay inside these ranges and needn't reach their ends.
Inputs may be any that keep to these rules, and one draw needn't show every extreme that they name: `face_rounds`: entry k of subdomain (i, j, l) is the round of its k-th face in the order low first dimension, high first dimension, low second, high second, low depth, high depth. Two subdomains that share a face give it the same round, the six faces of a subdomain have six different rounds, and the faces along one dimension use the same two rounds in every subdomain. Faces on the grid's outer boundary carry a round too. `aggregates`: every aggregate holds exactly 4 coarse cells.
All inputs are finite; a program needn't handle non-finite values.
Results may differ from the reference program's by a relative error of at most 0.0003.
Values sent between devices are 32-bit elements; how exact they have to be, the bound alone decides.
A program may use at most 128 MiB of HBM per device.

```python
import math
import jax
import jax.numpy as jnp
from jax import lax

CX = 8
CY = 32
CZ = 128
KX = 4
KY = 8
SWEEPS = 3
SMOOTH = 4
NX = 128
NY = 256
NZ = 256
NBX = 16
NBY = 8
NBZ = 2
NQX = 32
NQY = 32
N_AGG = 512


def draw_adjoint_source(key, part):
    key = jax.random.fold_in(key, 5)
    keys = jax.random.split(key, 2)
    rough = jax.random.truncated_normal(keys[0], -4.5, 4.5, (2, NX, NY, NZ), jnp.float32)
    levels = jax.random.uniform(keys[1], (2, NQX, 1, NQY, 1, NBZ, 1), jnp.float32, -0.5, 1.5)
    offsets = jnp.broadcast_to(levels, (2, NQX, KX, NQY, KY, NBZ, CZ)).reshape(2, NX, NY, NZ)
    return rough + offsets


def draw_face_rounds(key, part):
    key = jax.random.fold_in(key, 11)
    keys = jax.random.split(key, 4)
    order = jax.random.permutation(keys[0], 6).astype(jnp.int32)
    flip_x = jax.random.randint(keys[1], (1, NBY, NBZ), 0, 2)
    flip_y = jax.random.randint(keys[2], (NBX, 1, NBZ), 0, 2)
    flip_z = jax.random.randint(keys[3], (NBX, NBY, 1), 0, 2)
    coord_x = jnp.arange(NBX, dtype=jnp.int32)[:, None, None]
    coord_y = jnp.arange(NBY, dtype=jnp.int32)[None, :, None]
    coord_z = jnp.arange(NBZ, dtype=jnp.int32)[None, None, :]
    faces = [jnp.take(order, (coord_x - 1 + flip_x) % 2), jnp.take(order, (coord_x + flip_x) % 2), jnp.take(order, 2 + (coord_y - 1 + flip_y) % 2), jnp.take(order, 2 + (coord_y + flip_y) % 2), jnp.take(order, 4 + (coord_z - 1 + flip_z) % 2), jnp.take(order, 4 + (coord_z + flip_z) % 2)]
    faces = [jnp.broadcast_to(face, (NBX, NBY, NBZ)) for face in faces]
    return jnp.stack(faces, axis=-1).astype(jnp.int32)


def draw_aggregates(key, part):
    key = jax.random.fold_in(key, 23)
    shuffled = jax.random.permutation(key, NQX * NQY * NBZ).astype(jnp.int32)
    return (shuffled % N_AGG).reshape(NQX, NQY, NBZ).astype(jnp.int32)


def level_of(own_key, extent, cuts, least, high):
    def one(axis_at, blocks):
        steps = jax.random.uniform(jax.random.fold_in(jax.random.fold_in(own_key, 6), axis_at), (blocks,), jnp.float32, least / len(cuts), high / len(cuts))
        return jnp.repeat(jnp.exp(steps), extent[axis_at] // blocks).reshape((-1,) + (1,) * (len(extent) - axis_at - 1))

    level = one(*cuts[0])
    for cut in cuts[1:]:
        level = level * one(*cut)
    return level


def setup_inputs(seed: int = 0) -> dict:
    arg_keys = jax.random.split(jax.random.key(seed), 6)
    adjoint_source = draw_adjoint_source(jax.random.fold_in(arg_keys[5], 71), 0)
    velocity = jnp.clip(1.5 + 3.0 * jax.random.uniform(arg_keys[1], (NX, NY, NZ), jnp.float32) ** level_of(arg_keys[1], (NX, NY, NZ), ((0, 16), (1, 8), (2, 2)), -0.2, 0.2), 1.5, 4.5)
    damping = jnp.clip(jnp.exp(math.log(0.6) - 3.4011974 * jax.random.uniform(arg_keys[2], (NX, NY, NZ), jnp.float32) ** level_of(arg_keys[2], (NX, NY, NZ), ((0, 16), (1, 8), (2, 2)), -0.2, 0.2)), 0.02, 0.6)
    face_rounds = draw_face_rounds(jax.random.fold_in(arg_keys[5], 71), 0)
    aggregates = draw_aggregates(jax.random.fold_in(arg_keys[5], 71), 0)
    return dict(adjoint_source=adjoint_source, velocity=velocity, damping=damping, face_rounds=face_rounds, aggregates=aggregates)


GAMMA_RE = 0.6
GAMMA_IM = 0.25
RELAX = 0.8
OMEGA_SQ = 9.0


def smooth_axis(padded, dimension):
    length = padded.shape[dimension] - 2
    below_part = lax.slice_in_dim(padded, 0, length, axis=dimension)
    middle = lax.slice_in_dim(padded, 1, length + 1, axis=dimension)
    above_part = lax.slice_in_dim(padded, 2, length + 2, axis=dimension)
    return 0.5 * below_part + middle + 0.5 * above_part


def apply_operator(padded, state_field, kappa_cell, kappa_damp, dims):
    smoothed = padded
    for dimension in dims:
        smoothed = smooth_axis(smoothed, dimension)
    laplace = 16.0 * state_field - 2.0 * smoothed
    real_part = laplace[0] - kappa_cell * state_field[0] - kappa_damp * state_field[1]
    imag_part = laplace[1] - kappa_cell * state_field[1] + kappa_damp * state_field[0]
    return jnp.stack([real_part, imag_part])


def jacobi_local(residual, kappa_cell, kappa_damp, inv_re, inv_im, widths, dims):
    correction = jnp.zeros_like(residual)
    for step_index in range(SMOOTH):
        padded = jnp.pad(correction, widths)
        misfit = residual - apply_operator(padded, correction, kappa_cell, kappa_damp, dims)
        step_re = inv_re * misfit[0] - inv_im * misfit[1]
        step_im = inv_re * misfit[1] + inv_im * misfit[0]
        correction = correction + RELAX * jnp.stack([step_re, step_im])
    return correction


def blend_trace(own_plane, other_plane, active):
    diff_re = other_plane[0] - own_plane[0]
    diff_im = other_plane[1] - own_plane[1]
    blended = jnp.stack([own_plane[0] + GAMMA_RE * diff_re - GAMMA_IM * diff_im,
                         own_plane[1] + GAMMA_RE * diff_im + GAMMA_IM * diff_re])
    return jnp.where(active, blended, own_plane)


def trace_rounds(blocks, face_rounds):
    for round_now in range(6):
        for dimension in range(3):
            moved = jnp.moveaxis(blocks, (1 + 2 * dimension, 2 + 2 * dimension), (1, 2))
            colours = jnp.moveaxis(face_rounds[..., 2 * dimension + 1], dimension, 0)[:, :, None, :, None]
            active = colours[:-1] == round_now
            high_side = moved[:, :-1, -1]
            low_side = moved[:, 1:, 0]
            moved = moved.at[:, :-1, -1].set(blend_trace(high_side, low_side, active))
            moved = moved.at[:, 1:, 0].set(blend_trace(low_side, high_side, active))
            blocks = jnp.moveaxis(moved, (1, 2), (1 + 2 * dimension, 2 + 2 * dimension))
    return blocks


def reference(adjoint_source, velocity, damping, face_rounds, aggregates):
    kappa_cell = OMEGA_SQ / (velocity * velocity)
    kappa_damp = kappa_cell * damping
    diag_re = 14.0 - kappa_cell
    diag_norm = diag_re * diag_re + kappa_damp * kappa_damp
    inv_re = diag_re / diag_norm
    inv_im = -kappa_damp / diag_norm
    agg_ids = aggregates.reshape(-1).astype(jnp.int32)
    kappa_sums = kappa_cell.reshape(NQX, KX, NQY, KY, NBZ, CZ).sum(axis=(1, 3, 5)).reshape(-1)
    damp_sums = kappa_damp.reshape(NQX, KX, NQY, KY, NBZ, CZ).sum(axis=(1, 3, 5)).reshape(-1)
    kappa_total = jax.ops.segment_sum(kappa_sums, agg_ids, num_segments=N_AGG)
    damp_total = jax.ops.segment_sum(damp_sums, agg_ids, num_segments=N_AGG)
    coarse_norm = kappa_total * kappa_total + damp_total * damp_total
    block_shape = (NBX, CX, NBY, CY, NBZ, CZ)
    kappa_blocks = kappa_cell.reshape(block_shape)
    damp_blocks = kappa_damp.reshape(block_shape)
    inv_re_blocks = inv_re.reshape(block_shape)
    inv_im_blocks = inv_im.reshape(block_shape)
    block_widths = ((0, 0), (0, 0), (1, 1), (0, 0), (1, 1), (0, 0), (1, 1))
    adjoint_field = jnp.zeros_like(adjoint_source)
    for sweep_index in range(SWEEPS):
        padded = jnp.pad(adjoint_field, ((0, 0), (1, 1), (1, 1), (1, 1)))
        residual = adjoint_source - apply_operator(padded, adjoint_field, kappa_cell, kappa_damp, (1, 2, 3))
        cell_sums = residual.reshape(2, NQX, KX, NQY, KY, NBZ, CZ).sum(axis=(2, 4, 6)).reshape(2, -1)
        totals = jax.ops.segment_sum(cell_sums.T, agg_ids, num_segments=N_AGG).T
        coarse_re = (-totals[0] * kappa_total + totals[1] * damp_total) / coarse_norm
        coarse_im = (-totals[0] * damp_total - totals[1] * kappa_total) / coarse_norm
        coarse_values = jnp.stack([coarse_re, coarse_im])
        per_cell = coarse_values[:, agg_ids].reshape(2, NQX, 1, NQY, 1, NBZ, 1)
        coarse_term = jnp.broadcast_to(per_cell, (2, NQX, KX, NQY, KY, NBZ, CZ)).reshape(2, NX, NY, NZ)
        residual_blocks = residual.reshape((2,) + block_shape)
        correction = jacobi_local(residual_blocks, kappa_blocks, damp_blocks, inv_re_blocks, inv_im_blocks, block_widths, (2, 4, 6))
        correction = trace_rounds(correction, face_rounds)
        adjoint_field = adjoint_field + correction.reshape(2, NX, NY, NZ) + coarse_term
    return adjoint_field
```

```python
import functools

import jax
import jax.numpy as jnp
from jax import lax
from jax.experimental import pallas as pl
from jax.experimental.pallas import tpu as pltpu
from jax.sharding import PartitionSpec as P

MESH = pl.DeviceIdType.MESH
F32 = jnp.float32
BF16 = jnp.bfloat16

CX, CY, CZ = 8, 32, 128
PY = 48
TILES = CY // 8
SWEEPS = 3
SMOOTH = 4
GAMMA_RE = 0.6
GAMMA_IM = 0.25
RELAX = 0.8
OMEGA_SQ = 9.0

OFFSETS = [(ox, oy) for ox in (-1, 0, 1) for oy in (-1, 0, 1)]
NEIGHBOURS = [(ox, oy, 1) for ox, oy in OFFSETS if ox and oy]
NEIGHBOURS += [(ox, oy, 1) for ox, oy in OFFSETS if not (ox and oy)]
NEIGHBOURS += [(ox, oy, 0) for ox, oy in OFFSETS if ox and not oy]
NEIGHBOURS += [(ox, oy, 0) for ox, oy in OFFSETS if ox and oy]
NEIGHBOURS += [(ox, oy, 0) for ox, oy in OFFSETS if oy and not ox]


def slot_of(ox, oy):
    return (ox + 1) * 3 + (oy + 1)


def corner_of(ox, oy):
    return (1 if ox > 0 else 0) * 2 + (1 if oy > 0 else 0)


def iota(dim, shape=(8, 128)):
    return lax.broadcasted_iota(jnp.int32, shape, dim)


def roll(v, lanes, subs=0):
    if isinstance(lanes, int):
        lanes = lanes % 128
    if not isinstance(lanes, int) or lanes:
        v = pltpu.roll(v, lanes, 1)
    if subs % 8:
        v = pltpu.roll(v, subs % 8, 0)
    return v


def blend(a, b, mask):
    d_re = b[0] - a[0]
    d_im = b[1] - a[1]
    t_re = GAMMA_RE * d_re - GAMMA_IM * d_im
    t_im = GAMMA_RE * d_im + GAMMA_IM * d_re
    if mask is not None:
        t_re = jnp.where(mask, t_re, 0.0)
        t_im = jnp.where(mask, t_im, 0.0)
    return (a[0] + t_re, a[1] + t_im), (b[0] - t_re, b[1] - t_im)


def kernel(
    nx, ny,
    src, vel, dmp, rounds, aggs, out,
    kap, kdm, mre, mim, res, ping, pong, cor, fld, fz,
    coltile, edgecol, onehot, ktile,
    info_send, info_recv, stage, rz, ry, rd, ar_src1, ar_src2, ar1, ar2,
    info_ss, info_rs, h_ss, h_rs, x_ss, x_rs, ar_ss, ar_rs,
):
    ix, iy, iz = lax.axis_index("gx"), lax.axis_index("gy"), lax.axis_index("gz")
    lane, sub = iota(1), iota(0)
    lx, lt = lane % 8, (lane // 8) % TILES
    zf = jnp.where(iz == 0, 127, 0).astype(jnp.int32)
    at_face = lane == zf
    first_lane, last_lane = lane == 0, lane == 127
    lane32 = iota(1, (32, 128))
    first32, last32 = lane32 == 0, lane32 == 127

    has_x = {-1: ix > 0, 1: ix < nx - 1}
    has_y = {-1: iy > 0, 1: iy < ny - 1}

    def exists(ox, oy):
        if ox and oy:
            return jnp.logical_and(has_x[ox], has_y[oy])
        if ox:
            return has_x[ox]
        if oy:
            return has_y[oy]
        return None

    def guarded(cond, fn):
        if cond is None:
            fn()
        else:
            pl.when(cond)(fn)

    def device(ox, oy, oz):
        return (ix + ox, iy + oy, (1 - iz) if oz else iz)

    group1 = [(lax.rem(ix + d, nx), iy, iz) for d in range(1, nx)]
    here = iz * ny + iy
    group2 = []
    for d in range(1, 2 * ny):
        there = lax.rem(here + d, 2 * ny)
        group2.append((ix, lax.rem(there, ny), there // ny))

    zero = jnp.zeros((8, 128), F32)
    for k in range(SWEEPS):
        for p in range(2):
            for x in range(10):
                tiles = range(6) if x in (0, 9) else (0, 5)
                for t in tiles:
                    cor[k, p, pl.ds(x * PY + 8 * t, 8), :] = zero
        for s in range(2):
            for o in range(9):
                rz[k, s, o] = zero
        for o in range(2):
            for j in range(3):
                ry[k, o, j] = zero
        for o in range(4):
            for j in range(2):
                rd[k, o, j] = zero
    for s in range(2):
        for o in range(9):
            info_recv[s, o] = zero - 1.0

    barrier = pltpu.get_barrier_semaphore()
    count = jnp.int32(nx - 1 + 2 * ny - 1 + 1)
    for ox, oy, oz in NEIGHBOURS:
        def tell(ox=ox, oy=oy, oz=oz):
            pl.semaphore_signal(barrier, inc=1, device_id=device(ox, oy, oz), device_id_type=MESH)
        guarded(exists(ox, oy), tell)
        if exists(ox, oy) is not None:
            count = count + jnp.where(exists(ox, oy), 1, 0)
    for target in group2 + group1:
        pl.semaphore_signal(barrier, inc=1, device_id=target, device_id_type=MESH)

    for buf in (ping, pong):
        for p in range(2):
            for x in range(8):
                buf[p, pl.ds(x * PY, 8), :] = zero
                buf[p, pl.ds(x * PY + 40, 8), :] = zero
    for p in range(2):
        for x in range(10):
            for t in range(6):
                fld[p, pl.ds(x * PY + 8 * t, 8), :] = zero
        for role in range(4):
            fz[role, p] = zero

    for x in range(CX):
        v = vel[x]
        kappa = OMEGA_SQ / (v * v)
        damp = kappa * dmp[x]
        d_re = 14.0 - kappa
        scale = RELAX / (d_re * d_re + damp * damp)
        kap[x] = 16.0 - kappa
        kdm[x] = damp
        mre[x] = d_re * scale
        mim[x] = -damp * scale

    def face(i, inside):
        return jnp.where(inside, rounds[0, 0, 0, i].astype(F32), -1.0)

    low_x, high_x = face(0, ix > 0), face(1, ix < nx - 1)
    low_y, high_y = face(2, iy > 0), face(3, iy < ny - 1)
    depth = jnp.where(iz == 0, rounds[0, 0, 0, 5].astype(F32), rounds[0, 0, 0, 4].astype(F32))
    ids = [[aggs[qx, qy, 0].astype(F32) for qy in range(TILES)] for qx in range(2)]
    info = jnp.where(lx == 0, low_x, jnp.where(lx == 7, high_x, -1.0))
    col_y = jnp.where((lt == 0) & (sub == 0), low_y, jnp.where((lt == TILES - 1) & (sub == 7), high_y, -1.0))
    info = jnp.where(lane >= 32, col_y, info)
    info = jnp.where(lane >= 64, depth, info)
    for qx in range(2):
        for qy in range(TILES):
            info = jnp.where((lane >= 96) & (lx // 4 == qx) & (lt == qy), ids[qx][qy], info)
    info_send[...] = info

    agg_of = ((sub % 4) * 128 + lane).astype(F32)
    low_rows = sub < 4

    def bucket(sums):
        rows = [jnp.sum(sums[p][qx][t], axis=0, keepdims=True) for p in range(2) for qx in range(2) for t in range(TILES)]
        total = jnp.sum(jnp.concatenate(rows, axis=0), axis=1, keepdims=True)
        tile = zero
        for qx in range(2):
            for t in range(TILES):
                q = qx * TILES + t
                s_re = jnp.broadcast_to(total[q:q + 1], (8, 128))
                s_im = jnp.broadcast_to(total[8 + q:9 + q], (8, 128))
                tile = jnp.where(agg_of == ids[qx][t], tile + jnp.where(low_rows, s_re, s_im), tile)
        return tile

    def rows_of(v, t):
        return v[8 * t:8 * t + 8]

    sums = [[[zero] * TILES for _ in range(2)] for _ in range(2)]
    for x in range(CX):
        kappa, damp = 16.0 - kap[x], kdm[x]
        for t in range(TILES):
            sums[0][x // 4][t] = sums[0][x // 4][t] + rows_of(kappa, t)
            sums[1][x // 4][t] = sums[1][x // 4][t] + rows_of(damp, t)
    ar_src1[SWEEPS] = bucket(sums)

    def assemble(tiles, default):
        def pick(parts):
            value = jnp.full((8, 128), default, F32)
            for mask, tile in parts:
                value = jnp.where(mask, tile, value)
            return value
        t0, t3 = (lt == 0) & (sub == 0), (lt == TILES - 1) & (sub == 7)
        x0, x7 = lx == 0, lx == 7
        across_x = pick([(x0, roll(tiles[(-1, 0)], -7)), (x7, roll(tiles[(1, 0)], 7))])
        across_y = pick([(t0, roll(tiles[(0, -1)], -24, 1)), (t3, roll(tiles[(0, 1)], 24, -1))])
        across_xy = pick([
            (x0 & t0, roll(tiles[(-1, -1)], -31, 1)),
            (x0 & t3, roll(tiles[(-1, 1)], 17, -1)),
            (x7 & t0, roll(tiles[(1, -1)], -17, 1)),
            (x7 & t3, roll(tiles[(1, 1)], 31, -1)),
        ])
        return [tiles[(0, 0)], across_x, across_y, across_xy]

    def smooth_z(v):
        return 2.0 * v + jnp.where(first32, 0.0, pltpu.roll(v, 1, 1)) + jnp.where(last32, 0.0, pltpu.roll(v, 127, 1))

    def residual_pass():
        lefts = []
        for p in range(2):
            c0, px, py, pxy = (fz[role, p] for role in range(4))
            t0, t3 = (lt == 0) & (sub == 0), (lt == TILES - 1) & (sub == 7)

            def smooth_y(v, across):
                up = pltpu.roll(v, 1, 0)
                up = jnp.where(sub == 0, roll(up, 8), up)
                up = jnp.where(t0, across, up)
                down = pltpu.roll(v, 7, 0)
                down = jnp.where(sub == 7, roll(down, -8), down)
                down = jnp.where(t3, across, down)
                return up + 2.0 * v + down

            yc, yx = smooth_y(c0, py), smooth_y(px, pxy)
            w = 2.0 * yc + jnp.where(lx == 0, yx, roll(yc, 1)) + jnp.where(lx == 7, yx, roll(yc, -1))
            lefts.append(pltpu.roll(w, zf, 1))
        sums = [[[zero] * TILES for _ in range(2)] for _ in range(2)]
        ys = [[None] * 10 for _ in range(2)]

        def y_smoothed(p, x):
            if ys[p][x] is None:
                base = x * PY
                ys[p][x] = (fld[p, pl.ds(base + 7, 32), :] + fld[p, pl.ds(base + 9, 32), :]
                            + 2.0 * fld[p, pl.ds(base + 8, 32), :])
            return ys[p][x]

        for x in range(CX):
            smoothed = []
            for p in range(2):
                v = y_smoothed(p, x) + 2.0 * y_smoothed(p, x + 1) + y_smoothed(p, x + 2)
                halo = jnp.concatenate([roll(lefts[p], -(8 * t + x)) for t in range(TILES)], axis=0)
                smoothed.append(smooth_z(v) + jnp.where(lane32 == zf, halo, 0.0))
            f_re = fld[0, pl.ds((x + 1) * PY + 8, 32), :]
            f_im = fld[1, pl.ds((x + 1) * PY + 8, 32), :]
            a, b = kap[x], kdm[x]
            r_re = src[0, x] + 0.25 * smoothed[0] - a * f_re + b * f_im
            r_im = src[1, x] + 0.25 * smoothed[1] - a * f_im - b * f_re
            res[0, x] = r_re
            res[1, x] = r_im
            for t in range(TILES):
                sums[0][x // 4][t] = sums[0][x // 4][t] + rows_of(r_re, t)
                sums[1][x // 4][t] = sums[1][x // 4][t] + rows_of(r_im, t)
        return sums

    def first_pass():
        sums = [[[zero] * TILES for _ in range(2)] for _ in range(2)]
        for x in range(CX):
            for p in range(2):
                v = src[p, x]
                res[p, x] = v
                for t in range(TILES):
                    sums[p][x // 4][t] = sums[p][x // 4][t] + rows_of(v, t)
        return sums

    def jacobi(k):
        for x in range(CX):
            a, b = mre[x], mim[x]
            r_re, r_im = res[0, x], res[1, x]
            ping[0, pl.ds(x * PY + 8, 32), :] = a * r_re - b * r_im
            ping[1, pl.ds(x * PY + 8, 32), :] = a * r_im + b * r_re
        buffers = [ping, pong]
        for step in range(1, SMOOTH):
            now, later = buffers[(step - 1) % 2], buffers[step % 2]
            last = step == SMOOTH - 1
            ys = [[None] * CX for _ in range(2)]

            def y_smoothed(p, x):
                if x < 0 or x >= CX:
                    return None
                if ys[p][x] is None:
                    base = x * PY
                    ys[p][x] = (now[p, pl.ds(base + 7, 32), :] + now[p, pl.ds(base + 9, 32), :]
                                + 2.0 * now[p, pl.ds(base + 8, 32), :])
                return ys[p][x]

            for x in range(CX):
                misfit, old = [], []
                for p in range(2):
                    v = 2.0 * y_smoothed(p, x)
                    for near in (y_smoothed(p, x - 1), y_smoothed(p, x + 1)):
                        if near is not None:
                            v = v + near
                    c = now[p, pl.ds(x * PY + 8, 32), :]
                    old.append(c)
                    misfit.append(res[p, x] + 0.25 * smooth_z(v) - 2.0 * c)
                a, b = mre[x], mim[x]
                new_re = 0.2 * old[0] + (a * misfit[0] - b * misfit[1])
                new_im = 0.2 * old[1] + (a * misfit[1] + b * misfit[0])
                if last:
                    cor[k, 0, pl.ds((x + 1) * PY + 8, 32), :] = new_re
                    cor[k, 1, pl.ds((x + 1) * PY + 8, 32), :] = new_im
                else:
                    later[0, pl.ds(x * PY + 8, 32), :] = new_re
                    later[1, pl.ds(x * PY + 8, 32), :] = new_im

    def remote(src_ref, dst_ref, ssem, rsem, target):
        return pltpu.make_async_remote_copy(
            src_ref=src_ref, dst_ref=dst_ref, send_sem=ssem, recv_sem=rsem,
            device_id=target, device_id_type=MESH)

    def halo_copies(k, ox, oy, oz, incoming):
        mine, theirs = oz * 9 + slot_of(ox, oy), oz * 9 + slot_of(-ox, -oy)
        target = device(ox, oy, oz)
        if oz == 0 and ox and oy:
            part = stage.at[k, pl.ds(5, 2)]
            there, at_home = rd.at[k, corner_of(-ox, -oy)], rd.at[k, corner_of(ox, oy)]
        elif oz == 0 and oy:
            part = stage.at[k, pl.ds(0, 3)] if oy < 0 else stage.at[k, pl.ds(2, 3)]
            there, at_home = ry.at[k, 1 if oy < 0 else 0], ry.at[k, 0 if oy < 0 else 1]
        else:
            part = stage.at[k, 2]
            there, at_home = rz.at[k, oz, slot_of(-ox, -oy)], rz.at[k, oz, slot_of(ox, oy)]
        if incoming:
            return remote(part, at_home, h_ss.at[k, mine], h_rs.at[k, mine], target)
        return remote(part, there, h_ss.at[k, mine], h_rs.at[k, theirs], target)

    def plane_copies(k, ox, incoming):
        own, halo = (1, 9) if ox < 0 else (8, 0)
        part = cor.at[k, :, pl.ds(own * PY + 8, 32), :]
        there = cor.at[k, :, pl.ds(halo * PY + 8, 32), :]
        at_home = cor.at[k, :, pl.ds((0 if ox < 0 else 9) * PY + 8, 32), :]
        mine, theirs = (0, 1) if ox < 0 else (1, 0)
        if incoming:
            return remote(part, at_home, x_ss.at[k, mine], x_rs.at[k, mine], device(ox, 0, 0))
        return remote(part, there, x_ss.at[k, mine], x_rs.at[k, theirs], device(ox, 0, 0))

    def for_halo(k, fn, incoming=False):
        for ox, oy, oz in NEIGHBOURS:
            guarded(exists(ox, oy), lambda ox=ox, oy=oy, oz=oz: fn(halo_copies(k, ox, oy, oz, incoming)))
        for ox in (-1, 1):
            guarded(exists(ox, 0), lambda ox=ox: fn(plane_copies(k, ox, incoming)))

    def info_copies(ox, oy, oz, incoming):
        mine, theirs = oz * 9 + slot_of(ox, oy), oz * 9 + slot_of(-ox, -oy)
        target = device(ox, oy, oz)
        if incoming:
            return remote(info_send, info_recv.at[oz, slot_of(ox, oy)], info_ss.at[mine], info_rs.at[mine], target)
        return remote(info_send, info_recv.at[oz, slot_of(-ox, -oy)], info_ss.at[mine], info_rs.at[theirs], target)

    def for_info(fn, incoming=False):
        for ox, oy, oz in NEIGHBOURS:
            guarded(exists(ox, oy), lambda ox=ox, oy=oy, oz=oz: fn(info_copies(ox, oy, oz, incoming)))

    def pack_halo(k):
        packed = zero
        for p in range(2):
            for x in range(CX):
                for t in range(TILES):
                    v = cor[k, p, pl.ds((x + 1) * PY + 8 + 8 * t, 8), :]
                    to = p * 32 + t * 8 + x
                    packed = jnp.where(lane == to, pltpu.roll(v, jnp.where(iz == 0, to + 1, to), 1), packed)
        stage[k, 2] = packed
        stage[k, 5] = packed
        for p in range(2):
            stage[k, p] = cor[k, p, pl.ds(PY + 8, 8, stride=PY), :]
            stage[k, 3 + p] = cor[k, p, pl.ds(PY + 39, 8, stride=PY), :]
        lines = [cor[k, p, pl.ds(x * PY + y, 1), :] for p in range(2) for x in (1, 8) for y in (8, 39)]
        stage[k, 6] = jnp.concatenate(lines, axis=0)

    def reduce_copies(k, stage_no, every=True):
        bufs, srcs, targets = ((ar1, ar_src1, group1), (ar2, ar_src2, group2))[stage_no]
        sem = 2 * k + stage_no
        if every:
            return remote(bufs.at[k], bufs.at[k], ar_ss.at[sem], ar_rs.at[sem], targets[0])
        return [remote(srcs.at[k], bufs.at[k, d], ar_ss.at[sem], ar_rs.at[sem], target)
                for d, target in enumerate(targets)]

    def reduce_start(k, stage_no):
        for send in reduce_copies(k, stage_no, False):
            send.start()

    def reduce_finish(k, stage_no):
        bufs, srcs, targets = ((ar1, ar_src1, group1), (ar2, ar_src2, group2))[stage_no]
        reduce_copies(k, stage_no).wait_recv()
        total = srcs[k]
        for d in range(len(targets)):
            total = total + bufs[k, d]
        return total

    def setup_rounds():
        rows = []
        for s in range(2):
            tiles = {o: info_recv[s, slot_of(*o)] for o in OFFSETS}
            if s == 0:
                tiles[(0, 0)] = info_send[...]
            roles = assemble(tiles, -1.0)
            coltile[4 * s + 0] = roles[0]
            coltile[4 * s + 1] = roles[2]
            coltile[4 * s + 2] = roll(roles[0], -32)
            coltile[4 * s + 3] = roll(roles[1], -32)
            if s == 0:
                for role in range(4):
                    coltile[8 + role] = roll(roles[role], -64)
                corner = [jnp.full((4, 128), -1.0, F32) for _ in range(4)]
                row4 = iota(0, (4, 128))
                for j, tile in enumerate((roles[0], roles[2], roll(roles[0], -32), roll(roles[1], -32))):
                    for c in range(4):
                        sx, sy = c // 2, c % 2
                        spot = (lane == (3 * sy) * 8 + 7 * sx) & (sub == 7 * sy)
                        value = jnp.max(jnp.max(jnp.where(spot, tile, -1.0), axis=1, keepdims=True), axis=0, keepdims=True)
                        corner[j] = jnp.where(row4 == c, value, corner[j])
                    edgecol[j] = corner[j]
            ids_row = jnp.full((8, 128), -1.0, F32)
            for role in range(4):
                spread = jnp.broadcast_to(jnp.max(roles[role], axis=0, keepdims=True), (8, 128))
                ids_row = jnp.where(lane // 32 == role, roll(spread, 32 * (role + 1)), ids_row)
            rows.append(ids_row[0:1])
        number = iota(0, (128, 128)).astype(F32)
        for s in range(2):
            wide = jnp.broadcast_to(rows[s], (128, 128))
            for j in range(4):
                onehot[:, pl.ds((4 * s + j) * 128, 128)] = jnp.where(wide - 128.0 * j == number, 1.0, 0.0).astype(BF16)

    def coarse_rows(totals):
        kt = ktile[...]
        swapped = pltpu.roll(totals, 4, 0)
        k_swap = pltpu.roll(kt, 4, 0)
        k_all = jnp.where(low_rows, kt, k_swap)
        d_all = jnp.where(low_rows, k_swap, kt)
        norm = k_all * k_all + d_all * d_all
        norm = jnp.where(norm > 0.0, norm, 1.0)
        c = (jnp.where(low_rows, swapped, -swapped) * d_all - totals * k_all) / norm
        high = c.astype(BF16)
        rest = c - high.astype(F32)
        middle = rest.astype(BF16)
        low = (rest - middle.astype(F32)).astype(BF16)
        split = jnp.concatenate([high.astype(F32), middle.astype(F32), low.astype(F32), zero], axis=0).astype(BF16)
        found = jnp.dot(split, onehot[...], preferred_element_type=F32)
        found = found[0:8] + found[8:16] + found[16:24]
        rows = []
        for s in range(2):
            spread = zero
            for j in range(4):
                spread = spread + jnp.where(sub % 4 == j, found[:, (4 * s + j) * 128:(4 * s + j + 1) * 128], 0.0)
            rows.append([jnp.sum(spread[0:4], axis=0, keepdims=True), jnp.sum(spread[4:8], axis=0, keepdims=True)])
        return rows

    def sides_rounds(k):
        cells = []
        for s in range(2):
            tiles = {}
            for ox, oy in OFFSETS:
                if s == 0 and ox == 0 and oy == 0:
                    tiles[(ox, oy)] = stage[k, 2]
                elif s == 0 and ox and oy:
                    tiles[(ox, oy)] = rd[k, corner_of(ox, oy), 0]
                elif s == 0 and oy:
                    tiles[(ox, oy)] = ry[k, 0, 0] if oy < 0 else ry[k, 1, 2]
                else:
                    tiles[(ox, oy)] = rz[k, s, slot_of(ox, oy)]
            roles = assemble(tiles, 0.0)
            cells.append([(role, roll(role, -32)) for role in roles])
        for r in range(6):
            now = float(r)
            for s in range(2):
                c = cells[s]
                c[0], c[1] = blend(c[0], c[1], coltile[4 * s + 0] == now)
                c[2], c[3] = blend(c[2], c[3], coltile[4 * s + 1] == now)
                c[0], c[2] = blend(c[0], c[2], coltile[4 * s + 2] == now)
                c[1], c[3] = blend(c[1], c[3], coltile[4 * s + 3] == now)
            for role in range(4):
                cells[0][role], cells[1][role] = blend(cells[0][role], cells[1][role], coltile[8 + role] == now)
        return cells

    def main_rounds(k):
        def lines(planes, rows):
            return tuple(
                jnp.concatenate([cor[k, p, pl.ds(x * PY + y, 1), :] for x in planes for y in rows], axis=0) for p in range(2))

        c0 = lines((1, 8), (8, 39))
        px = lines((0, 9), (8, 39))
        halo_rows = []
        for p in range(2):
            parts = []
            for x_at in (0, 7):
                parts += [ry[k, 0, 1 + p, pl.ds(x_at, 1), :], ry[k, 1, p, pl.ds(x_at, 1), :]]
            halo_rows.append(jnp.concatenate(parts, axis=0))
        py = tuple(halo_rows)
        diagonal = []
        for p in range(2):
            parts = []
            for c in range(4):
                parts.append(rd[k, c, 1, pl.ds(p * 4 + (3 - c), 1), :])
            diagonal.append(jnp.concatenate(parts, axis=0))
        pxy = tuple(diagonal)
        for r in range(6):
            now = float(r)
            c0, px = blend(c0, px, edgecol[0] == now)
            py, pxy = blend(py, pxy, edgecol[1] == now)
            c0, py = blend(c0, py, edgecol[2] == now)
            px, pxy = blend(px, pxy, edgecol[3] == now)
        for own, halo, ox in ((1, 0, -1), (8, 9, 1)):
            a = tuple(cor[k, p, pl.ds(own * PY + 8, 32), :] for p in range(2))
            b = tuple(cor[k, p, pl.ds(halo * PY + 8, 32), :] for p in range(2))
            a, b = blend(a, b, jnp.broadcast_to(has_x[ox], (32, 128)))
            for p in range(2):
                cor[k, p, pl.ds(own * PY + 8, 32), :] = a[p]
                cor[k, p, pl.ds(halo * PY + 8, 32), :] = b[p]
        for own, halo, oy in ((8, 7, -1), (39, 40, 1)):
            a = tuple(stage[k, p if oy < 0 else 3 + p] for p in range(2))
            b = tuple(ry[k, 0, 1 + p] if oy < 0 else ry[k, 1, p] for p in range(2))
            a, b = blend(a, b, jnp.broadcast_to(has_y[oy], (8, 128)))
            for p in range(2):
                cor[k, p, pl.ds(PY + own, 8, stride=PY), :] = a[p]
                cor[k, p, pl.ds(PY + halo, 8, stride=PY), :] = b[p]
        for c in range(4):
            sx, sy = c // 2, c % 2
            own_x, halo_x = (1, 8)[sx], (0, 9)[sx]
            own_y, halo_y = (8, 39)[sy], (7, 40)[sy]
            for p in range(2):
                cor[k, p, pl.ds(own_x * PY + own_y, 1), :] = c0[p][c:c + 1]
                cor[k, p, pl.ds(halo_x * PY + own_y, 1), :] = px[p][c:c + 1]
                cor[k, p, pl.ds(own_x * PY + halo_y, 1), :] = py[p][c:c + 1]
                cor[k, p, pl.ds(halo_x * PY + halo_y, 1), :] = pxy[p][c:c + 1]

    def update(k, cells, coarse):
        last = k == SWEEPS - 1
        for p in range(2):
            turned = [pltpu.roll(cells[0][role][p], zf, 1) for role in range(4)]
            row = coarse[0][p]

            def term(role, t, x):
                at = 32 * role + 8 * t + x
                return jnp.broadcast_to(row[:, at:at + 1], (8, 128))

            for x in range(10):
                if last and x in (0, 9):
                    continue
                role = 1 if x in (0, 9) else 0
                near = min(max(x - 1, 0), 7)
                for t in range(TILES):
                    value = term(role, t, (near // 4) * 4 if role == 0 else near)
                    column = roll(turned[role], -(8 * t + near))
                    rows = pl.ds(x * PY + 8 + 8 * t, 8)
                    value = value + fld[p, rows, :] + jnp.where(at_face, column, cor[k, p, rows, :])
                    if last:
                        out[p, x - 1, pl.ds(8 * t, 8), :] = value
                    else:
                        fld[p, rows, :] = value
                if last:
                    continue
                for t, at, y in ((0, 0, 7), (TILES - 1, 7, 40)):
                    column = roll(turned[2 + role], -(8 * t + near))[at:at + 1]
                    place = pl.ds(x * PY + y, 1)
                    value = term(2 + role, t, near)[0:1] + fld[p, place, :]
                    fld[p, place, :] = value + jnp.where(at_face[0:1], column, cor[k, p, place, :])
            if not last:
                for role in range(4):
                    here_row = jnp.broadcast_to(coarse[1][p], (8, 128))
                    fz[role, p] = fz[role, p] + cells[1][role][p] + roll(here_row, -32 * role)

    for k in range(SWEEPS):
        sums = first_pass() if k == 0 else residual_pass()
        ar_src1[k] = bucket(sums)
        if k == 0:
            jacobi(k)
            pack_halo(k)
            pl.semaphore_wait(barrier, count)
            reduce_start(k, 0)
            reduce_start(SWEEPS, 0)
            for_info(lambda copy: copy.start())
            for_halo(k, lambda copy: copy.start())
        else:
            reduce_start(k, 0)
            jacobi(k)
            pack_halo(k)
            for_halo(k, lambda copy: copy.start())
        ar_src2[k] = reduce_finish(k, 0)
        reduce_start(k, 1)
        if k == 0:
            ar_src2[SWEEPS] = reduce_finish(SWEEPS, 0)
            reduce_start(SWEEPS, 1)
            for_info(lambda copy: copy.wait_recv(), True)
            setup_rounds()
        for_halo(k, lambda copy: copy.wait_recv(), True)
        cells = sides_rounds(k)
        for_halo(k, lambda copy: copy.wait_send())
        main_rounds(k)
        reduce_copies(k, 0).wait_send()
        if k == 0:
            reduce_copies(SWEEPS, 0).wait_send()
            for_info(lambda copy: copy.wait_send())
            ktile[...] = reduce_finish(SWEEPS, 1)
            reduce_copies(SWEEPS, 1).wait_send()
        coarse = coarse_rows(reduce_finish(k, 1))
        update(k, cells, coarse)
        reduce_copies(k, 1).wait_send()


def solution(mesh):
    nx, ny = mesh.shape["gx"], mesh.shape["gy"]

    def step(adjoint_source, velocity, damping, face_rounds, aggregates):
        vmem = pl.BlockSpec(memory_space=pltpu.VMEM)
        smem = pl.BlockSpec(memory_space=pltpu.SMEM)
        dma = pltpu.SemaphoreType.DMA
        tile = (8, 128)
        block = (CX, CY, CZ)
        return pl.pallas_call(
            functools.partial(kernel, nx, ny),
            out_shape=jax.ShapeDtypeStruct((2,) + block, F32),
            in_specs=[vmem, vmem, vmem, smem, smem],
            out_specs=vmem,
            scratch_shapes=[
                pltpu.VMEM(block, F32), pltpu.VMEM(block, F32), pltpu.VMEM(block, F32), pltpu.VMEM(block, F32),
                pltpu.VMEM((2,) + block, F32),
                pltpu.VMEM((2, CX * PY, CZ), F32), pltpu.VMEM((2, CX * PY, CZ), F32),
                pltpu.VMEM((SWEEPS, 2, 10 * PY, CZ), F32),
                pltpu.VMEM((2, 10 * PY, CZ), F32),
                pltpu.VMEM((4, 2) + tile, F32),
                pltpu.VMEM((12,) + tile, F32), pltpu.VMEM((4, 4, 128), F32),
                pltpu.VMEM((128, 1024), BF16), pltpu.VMEM(tile, F32),
                pltpu.VMEM(tile, F32), pltpu.VMEM((2, 9) + tile, F32),
                pltpu.VMEM((SWEEPS, 7) + tile, F32), pltpu.VMEM((SWEEPS, 2, 9) + tile, F32),
                pltpu.VMEM((SWEEPS, 2, 3) + tile, F32), pltpu.VMEM((SWEEPS, 4, 2) + tile, F32),
                pltpu.VMEM((SWEEPS + 1,) + tile, F32), pltpu.VMEM((SWEEPS + 1,) + tile, F32),
                pltpu.VMEM((SWEEPS + 1, nx - 1) + tile, F32), pltpu.VMEM((SWEEPS + 1, 2 * ny - 1) + tile, F32),
                dma((18,)), dma((18,)), dma((SWEEPS, 18)), dma((SWEEPS, 18)),
                dma((SWEEPS, 2)), dma((SWEEPS, 2)), dma((2 * SWEEPS + 2,)), dma((2 * SWEEPS + 2,)),
            ],
            compiler_params=pltpu.CompilerParams(
                collective_id=0, has_side_effects=True, vmem_limit_bytes=32 * 1024 * 1024
            ),
        )(adjoint_source, velocity, damping, face_rounds, aggregates)

    placed = (
        P(None, "gx", "gy", "gz"),
        P("gx", "gy", "gz"),
        P("gx", "gy", "gz"),
        P("gx", "gy", "gz", None),
        P("gx", "gy", "gz"),
    )
    return jax.shard_map(
        step, mesh=mesh, in_specs=placed, out_specs=P(None, "gx", "gy", "gz"), check_vma=False
    )
```

```python
import functools

import jax
import jax.numpy as jnp
from jax import lax
from jax.experimental import pallas as pl
from jax.experimental.pallas import tpu as pltpu
from jax.sharding import PartitionSpec as P

MESH = pl.DeviceIdType.MESH
F32 = jnp.float32
BF16 = jnp.bfloat16

CX, CY, CZ = 8, 32, 128
PY = 48
TILES = CY // 8
SWEEPS = 3
SMOOTH = 4
GAMMA_RE = 0.6
GAMMA_IM = 0.25
RELAX = 0.8
OMEGA_SQ = 9.0

OFFSETS = [(ox, oy) for ox in (-1, 0, 1) for oy in (-1, 0, 1)]
NEIGHBOURS = [(ox, oy, 1) for ox, oy in OFFSETS if ox and oy]
NEIGHBOURS += [(ox, oy, 1) for ox, oy in OFFSETS if not (ox and oy)]
NEIGHBOURS += [(ox, oy, 0) for ox, oy in OFFSETS if ox and not oy]
NEIGHBOURS += [(ox, oy, 0) for ox, oy in OFFSETS if ox and oy]
NEIGHBOURS += [(ox, oy, 0) for ox, oy in OFFSETS if oy and not ox]


def slot_of(ox, oy):
    return (ox + 1) * 3 + (oy + 1)


def corner_of(ox, oy):
    return (1 if ox > 0 else 0) * 2 + (1 if oy > 0 else 0)


def iota(dim, shape=(8, 128)):
    return lax.broadcasted_iota(jnp.int32, shape, dim)


def roll(v, lanes, subs=0):
    if isinstance(lanes, int):
        lanes = lanes % 128
    if not isinstance(lanes, int) or lanes:
        v = pltpu.roll(v, lanes, 1)
    if subs % 8:
        v = pltpu.roll(v, subs % 8, 0)
    return v


def blend(a, b, mask):
    d_re = b[0] - a[0]
    d_im = b[1] - a[1]
    t_re = GAMMA_RE * d_re - GAMMA_IM * d_im
    t_im = GAMMA_RE * d_im + GAMMA_IM * d_re
    if mask is not None:
        t_re = jnp.where(mask, t_re, 0.0)
        t_im = jnp.where(mask, t_im, 0.0)
    return (a[0] + t_re, a[1] + t_im), (b[0] - t_re, b[1] - t_im)


def kernel(
    nx, ny,
    src_in, vel_in, dmp_in, rounds, aggs, out,
    src, vel, dmp, in_sem,
    kap, kdm, mre, mim, res, ping, pong, cor, fld, fz,
    coltile, edgecol, onehot, ksum, cval, zmask,
    info_send, info_recv, stage, rz, ry, rd, row_send, pair_recv, chip_send, gath,
    info_ss, info_rs, h_ss, h_rs, x_ss, x_rs, pair_ss, pair_rs, ga_ss, ga_rs,
):
    ix, iy, iz = lax.axis_index("gx"), lax.axis_index("gy"), lax.axis_index("gz")
    lane, sub = iota(1), iota(0)
    lx, lt = lane % 8, (lane // 8) % TILES
    zf = jnp.where(iz == 0, 127, 0).astype(jnp.int32)
    at_face = lane == zf
    first_lane, last_lane = lane == 0, lane == 127
    lane32 = iota(1, (32, 128))
    first32, last32 = lane32 == 0, lane32 == 127

    has_x = {-1: ix > 0, 1: ix < nx - 1}
    has_y = {-1: iy > 0, 1: iy < ny - 1}

    def exists(ox, oy):
        if ox and oy:
            return jnp.logical_and(has_x[ox], has_y[oy])
        if ox:
            return has_x[ox]
        if oy:
            return has_y[oy]
        return None

    def guarded(cond, fn):
        if cond is None:
            fn()
        else:
            pl.when(cond)(fn)

    def device(ox, oy, oz):
        return (ix + ox, iy + oy, (1 - iz) if oz else iz)

    core = lax.rem(iy, 2)
    at_x, at_y, at_z = lax.rem(ix, 4), ix // 4, iz * (ny // 2) + iy // 2
    nz = ny
    pair = (ix, iy + 1 - 2 * core, iz)
    across = sorted(((dx, dy) for dx in range(4) for dy in range(4)), key=lambda d: -min(d[0], 4 - d[0]) - min(d[1], 4 - d[1]))
    across_x = [lax.rem(at_y + dy, 4) * 4 + lax.rem(at_x + dx, 4) for dx, dy in across]

    def for_chips(fn):
        def layer(i, carry):
            step = (i + 1) // 2
            there = lax.rem(at_z + nz // 2 + jnp.where(lax.rem(i, 2) == 1, nz - step, step), nz)
            ty, tz = lax.rem(there, ny // 2) * 2 + core, there // (ny // 2)
            for j in range(16):
                fn(i * 16 + j, (across_x[j], ty, tz))
            return carry
        lax.fori_loop(0, nz - 1, layer, 0)
        for j in range(15):
            fn((nz - 1) * 16 + j, (across_x[j], iy, iz))

    loads = [pltpu.make_async_copy(whole, local, in_sem.at[i])
             for i, (whole, local) in enumerate(((vel_in, vel), (dmp_in, dmp), (src_in, src)))]
    for load in loads:
        load.start()

    zero = jnp.zeros((8, 128), F32)
    for k in range(SWEEPS):
        for p in range(2):
            for x in range(10):
                tiles = range(6) if x in (0, 9) else (0, 5)
                for t in tiles:
                    cor[k, p, pl.ds(x * PY + 8 * t, 8), :] = zero
        for s in range(2):
            for o in range(9):
                rz[k, s, o] = zero
        for o in range(2):
            for j in range(3):
                ry[k, o, j] = zero
        for o in range(4):
            for j in range(2):
                rd[k, o, j] = zero
    for s in range(2):
        for o in range(9):
            info_recv[s, o] = zero - 1.0

    barrier = pltpu.get_barrier_semaphore()
    count = jnp.int32(16 * nz - 1 + 1)
    for ox, oy, oz in NEIGHBOURS:
        if oy == 0:
            continue
        def tell(ox=ox, oy=oy, oz=oz):
            pl.semaphore_signal(barrier, inc=1, device_id=device(ox, oy, oz), device_id_type=MESH)
        guarded(exists(ox, oy), tell)
        count = count + jnp.where(exists(ox, oy), 1, 0)

    def tell_chip(slot, target):
        pl.semaphore_signal(barrier, inc=1, device_id=target, device_id_type=MESH)

    for_chips(tell_chip)
    tell_chip(0, pair)

    for buf in (ping, pong):
        for p in range(2):
            for x in range(8):
                buf[p, pl.ds(x * PY, 8), :] = zero
                buf[p, pl.ds(x * PY + 40, 8), :] = zero
    for p in range(2):
        for x in range(10):
            for t in range(6):
                fld[p, pl.ds(x * PY + 8 * t, 8), :] = zero
        for role in range(4):
            fz[role, p] = zero

    for load in loads:
        load.wait()
    for x in range(CX):
        v = vel[x]
        kappa = OMEGA_SQ / (v * v)
        damp = kappa * dmp[x]
        d_re = 14.0 - kappa
        scale = RELAX / (d_re * d_re + damp * damp)
        kap[x] = 16.0 - kappa
        kdm[x] = damp
        mre[x] = d_re * scale
        mim[x] = -damp * scale

    def face(i, inside):
        return jnp.where(inside, rounds[0, 0, 0, i].astype(F32), -1.0)

    low_x, high_x = face(0, ix > 0), face(1, ix < nx - 1)
    low_y, high_y = face(2, iy > 0), face(3, iy < ny - 1)
    depth = jnp.where(iz == 0, rounds[0, 0, 0, 5].astype(F32), rounds[0, 0, 0, 4].astype(F32))
    ids = [[aggs[qx, 0, qy].astype(F32) for qy in range(TILES)] for qx in range(2)]
    info = jnp.where(lx == 0, low_x, jnp.where(lx == 7, high_x, -1.0))
    col_y = jnp.where((lt == 0) & (sub == 0), low_y, jnp.where((lt == TILES - 1) & (sub == 7), high_y, -1.0))
    info = jnp.where(lane >= 32, col_y, info)
    info = jnp.where(lane >= 64, depth, info)
    for qx in range(2):
        for qy in range(TILES):
            info = jnp.where((lane >= 96) & (lx // 4 == qx) & (lt == qy), ids[qx][qy], info)
    info_send[...] = info

    low_rows = sub < 4
    lane1 = iota(1, (1, 128))

    def row_of(sums, first):
        rows = [jnp.sum(sums[p][qx][t], axis=0, keepdims=True) for p in range(2) for qx in range(2) for t in range(TILES)]
        total = jnp.sum(jnp.concatenate(rows, axis=0), axis=1, keepdims=True)
        spread = jnp.where(iota(1, (16, 128)) == iota(0, (16, 128)) + first, jnp.broadcast_to(total, (16, 128)), 0.0)
        return jnp.sum(spread, axis=0, keepdims=True)

    def rows_of(v, t):
        return v[8 * t:8 * t + 8]

    sums = [[[zero] * TILES for _ in range(2)] for _ in range(2)]
    for x in range(CX):
        kappa, damp = 16.0 - kap[x], kdm[x]
        for t in range(TILES):
            sums[0][x // 4][t] = sums[0][x // 4][t] + rows_of(kappa, t)
            sums[1][x // 4][t] = sums[1][x // 4][t] + rows_of(damp, t)
    fixed_row = row_of(sums, 32 + 16 * core)
    for qx in range(2):
        for t in range(TILES):
            fixed_row = fixed_row + jnp.where(lane1 == 64 + 8 * core + qx * TILES + t, ids[qx][t], 0.0)

    def assemble(tiles, default):
        def pick(parts):
            value = jnp.full((8, 128), default, F32)
            for mask, tile in parts:
                value = jnp.where(mask, tile, value)
            return value
        t0, t3 = (lt == 0) & (sub == 0), (lt == TILES - 1) & (sub == 7)
        x0, x7 = lx == 0, lx == 7
        across_x = pick([(x0, roll(tiles[(-1, 0)], -7)), (x7, roll(tiles[(1, 0)], 7))])
        across_y = pick([(t0, roll(tiles[(0, -1)], -24, 1)), (t3, roll(tiles[(0, 1)], 24, -1))])
        across_xy = pick([
            (x0 & t0, roll(tiles[(-1, -1)], -31, 1)),
            (x0 & t3, roll(tiles[(-1, 1)], 17, -1)),
            (x7 & t0, roll(tiles[(1, -1)], -17, 1)),
            (x7 & t3, roll(tiles[(1, 1)], 31, -1)),
        ])
        return [tiles[(0, 0)], across_x, across_y, across_xy]

    def smooth_z(v):
        return 2.0 * v + jnp.where(first32, 0.0, pltpu.roll(v, 1, 1)) + jnp.where(last32, 0.0, pltpu.roll(v, 127, 1))

    def residual_pass():
        lefts = []
        for p in range(2):
            c0, px, py, pxy = (fz[role, p] for role in range(4))
            t0, t3 = (lt == 0) & (sub == 0), (lt == TILES - 1) & (sub == 7)

            def smooth_y(v, across):
                up = pltpu.roll(v, 1, 0)
                up = jnp.where(sub == 0, roll(up, 8), up)
                up = jnp.where(t0, across, up)
                down = pltpu.roll(v, 7, 0)
                down = jnp.where(sub == 7, roll(down, -8), down)
                down = jnp.where(t3, across, down)
                return up + 2.0 * v + down

            yc, yx = smooth_y(c0, py), smooth_y(px, pxy)
            w = 2.0 * yc + jnp.where(lx == 0, yx, roll(yc, 1)) + jnp.where(lx == 7, yx, roll(yc, -1))
            lefts.append(pltpu.roll(w, zf, 1))
        sums = [[[zero] * TILES for _ in range(2)] for _ in range(2)]
        ys = [[None] * 10 for _ in range(2)]

        def y_smoothed(p, x):
            if ys[p][x] is None:
                base = x * PY
                ys[p][x] = (fld[p, pl.ds(base + 7, 32), :] + fld[p, pl.ds(base + 9, 32), :]
                            + 2.0 * fld[p, pl.ds(base + 8, 32), :])
            return ys[p][x]

        for x in range(CX):
            smoothed = []
            for p in range(2):
                v = y_smoothed(p, x) + 2.0 * y_smoothed(p, x + 1) + y_smoothed(p, x + 2)
                halo = jnp.concatenate([roll(lefts[p], -(8 * t + x)) for t in range(TILES)], axis=0)
                smoothed.append(smooth_z(v) + jnp.where(lane32 == zf, halo, 0.0))
            f_re = fld[0, pl.ds((x + 1) * PY + 8, 32), :]
            f_im = fld[1, pl.ds((x + 1) * PY + 8, 32), :]
            a, b = kap[x], kdm[x]
            r_re = src[0, x] + 0.25 * smoothed[0] - a * f_re + b * f_im
            r_im = src[1, x] + 0.25 * smoothed[1] - a * f_im - b * f_re
            res[0, x] = r_re
            res[1, x] = r_im
            for t in range(TILES):
                sums[0][x // 4][t] = sums[0][x // 4][t] + rows_of(r_re, t)
                sums[1][x // 4][t] = sums[1][x // 4][t] + rows_of(r_im, t)
        return sums

    def first_pass():
        sums = [[[zero] * TILES for _ in range(2)] for _ in range(2)]
        for x in range(CX):
            for p in range(2):
                v = src[p, x]
                res[p, x] = v
                for t in range(TILES):
                    sums[p][x // 4][t] = sums[p][x // 4][t] + rows_of(v, t)
        return sums

    def jacobi(k):
        for x in range(CX):
            a, b = mre[x], mim[x]
            r_re, r_im = res[0, x], res[1, x]
            ping[0, pl.ds(x * PY + 8, 32), :] = a * r_re - b * r_im
            ping[1, pl.ds(x * PY + 8, 32), :] = a * r_im + b * r_re
        buffers = [ping, pong]
        for step in range(1, SMOOTH):
            now, later = buffers[(step - 1) % 2], buffers[step % 2]
            last = step == SMOOTH - 1
            ys = [[None] * CX for _ in range(2)]

            def y_smoothed(p, x):
                if x < 0 or x >= CX:
                    return None
                if ys[p][x] is None:
                    base = x * PY
                    ys[p][x] = (now[p, pl.ds(base + 7, 32), :] + now[p, pl.ds(base + 9, 32), :]
                                + 2.0 * now[p, pl.ds(base + 8, 32), :])
                return ys[p][x]

            for x in range(CX):
                misfit, old = [], []
                for p in range(2):
                    v = 2.0 * y_smoothed(p, x)
                    for near in (y_smoothed(p, x - 1), y_smoothed(p, x + 1)):
                        if near is not None:
                            v = v + near
                    c = now[p, pl.ds(x * PY + 8, 32), :]
                    old.append(c)
                    misfit.append(res[p, x] + 0.25 * smooth_z(v) - 2.0 * c)
                a, b = mre[x], mim[x]
                new_re = 0.2 * old[0] + (a * misfit[0] - b * misfit[1])
                new_im = 0.2 * old[1] + (a * misfit[1] + b * misfit[0])
                if last:
                    cor[k, 0, pl.ds((x + 1) * PY + 8, 32), :] = new_re
                    cor[k, 1, pl.ds((x + 1) * PY + 8, 32), :] = new_im
                else:
                    later[0, pl.ds(x * PY + 8, 32), :] = new_re
                    later[1, pl.ds(x * PY + 8, 32), :] = new_im

    def remote(src_ref, dst_ref, ssem, rsem, target):
        return pltpu.make_async_remote_copy(
            src_ref=src_ref, dst_ref=dst_ref, send_sem=ssem, recv_sem=rsem,
            device_id=target, device_id_type=MESH)

    def halo_copies(k, ox, oy, oz, incoming):
        mine, theirs = oz * 9 + slot_of(ox, oy), oz * 9 + slot_of(-ox, -oy)
        target = device(ox, oy, oz)
        if oz == 0 and ox and oy:
            part = stage.at[k, pl.ds(5, 2)]
            there, at_home = rd.at[k, corner_of(-ox, -oy)], rd.at[k, corner_of(ox, oy)]
        elif oz == 0 and oy:
            part = stage.at[k, pl.ds(0, 3)] if oy < 0 else stage.at[k, pl.ds(2, 3)]
            there, at_home = ry.at[k, 1 if oy < 0 else 0], ry.at[k, 0 if oy < 0 else 1]
        else:
            part = stage.at[k, 2]
            there, at_home = rz.at[k, oz, slot_of(-ox, -oy)], rz.at[k, oz, slot_of(ox, oy)]
        if incoming:
            return remote(part, at_home, h_ss.at[k, mine], h_rs.at[k, mine], target)
        return remote(part, there, h_ss.at[k, mine], h_rs.at[k, theirs], target)

    def plane_copies(k, ox, incoming):
        own, halo = (1, 9) if ox < 0 else (8, 0)
        part = cor.at[k, :, pl.ds(own * PY + 8, 32), :]
        there = cor.at[k, :, pl.ds(halo * PY + 8, 32), :]
        at_home = cor.at[k, :, pl.ds((0 if ox < 0 else 9) * PY + 8, 32), :]
        mine, theirs = (0, 1) if ox < 0 else (1, 0)
        if incoming:
            return remote(part, at_home, x_ss.at[k, mine], x_rs.at[k, mine], device(ox, 0, 0))
        return remote(part, there, x_ss.at[k, mine], x_rs.at[k, theirs], device(ox, 0, 0))

    def for_halo(k, fn, incoming=False):
        for ox, oy, oz in NEIGHBOURS:
            guarded(exists(ox, oy), lambda ox=ox, oy=oy, oz=oz: fn(halo_copies(k, ox, oy, oz, incoming)))
        for ox in (-1, 1):
            guarded(exists(ox, 0), lambda ox=ox: fn(plane_copies(k, ox, incoming)))

    def info_copies(ox, oy, oz, incoming):
        mine, theirs = oz * 9 + slot_of(ox, oy), oz * 9 + slot_of(-ox, -oy)
        target = device(ox, oy, oz)
        if incoming:
            return remote(info_send, info_recv.at[oz, slot_of(ox, oy)], info_ss.at[mine], info_rs.at[mine], target)
        return remote(info_send, info_recv.at[oz, slot_of(-ox, -oy)], info_ss.at[mine], info_rs.at[theirs], target)

    def for_info(fn, incoming=False):
        for ox, oy, oz in NEIGHBOURS:
            guarded(exists(ox, oy), lambda ox=ox, oy=oy, oz=oz: fn(info_copies(ox, oy, oz, incoming)))

    def pack_halo(k):
        packed = zero
        for p in range(2):
            for x in range(CX):
                for t in range(TILES):
                    v = cor[k, p, pl.ds((x + 1) * PY + 8 + 8 * t, 8), :]
                    to = p * 32 + t * 8 + x
                    packed = jnp.where(lane == to, pltpu.roll(v, jnp.where(iz == 0, to + 1, to), 1), packed)
        stage[k, 2] = packed
        stage[k, 5] = packed
        for p in range(2):
            stage[k, p] = cor[k, p, pl.ds(PY + 8, 8, stride=PY), :]
            stage[k, 3 + p] = cor[k, p, pl.ds(PY + 39, 8, stride=PY), :]
        lines = [cor[k, p, pl.ds(x * PY + y, 1), :] for p in range(2) for x in (1, 8) for y in (8, 39)]
        stage[k, 6] = jnp.concatenate(lines, axis=0)

    first_row = pl.ds(0, 1)
    others = pl.ds(0, 16 * nz - 1)

    def pair_copy(k):
        return remote(row_send.at[k, first_row], pair_recv.at[k, first_row], pair_ss.at[k], pair_rs.at[k], pair)

    def gather_start(k):
        chip = row_send[k, first_row] + pair_recv[k, first_row]
        chip_send[k, first_row] = chip
        gath[k, pl.ds(16 * nz - 1, 1)] = chip
        for_chips(lambda slot, target: remote(
            chip_send.at[k, first_row], gath.at[k, pl.ds(slot, 1)], ga_ss.at[k], ga_rs.at[k], target).start())

    def gather_every(k):
        return remote(gath.at[k, others], gath.at[k, others], ga_ss.at[k], ga_rs.at[k], pair)

    lane_n = iota(1, (128, 128))

    def by_aggregate(values):
        whole = jnp.where(lane_n < 32, values, 0.0)
        high = whole.astype(BF16).astype(F32)
        rest = whole - high
        middle = rest.astype(BF16).astype(F32)
        split = high + pltpu.roll(middle, 32, 1) + pltpu.roll(rest - middle, 64, 1)
        found = jnp.dot(onehot[...], split.astype(BF16), preferred_element_type=F32)
        lane64 = iota(1, (64, 128))
        total = jnp.zeros((64, 128), F32)
        for b in range(16):
            mine = (lane64 % 8 == b % 8) & ((lane64 // 16) % 2 == b // 8)
            total = jnp.where(mine, found[64 * b:64 * b + 64], total)
        total = jnp.where(lane64 < 96, total, 0.0)
        real = (lane64 // 8) % 2 == 0
        return (jnp.sum(jnp.where(real, total, 0.0), axis=1, keepdims=True),
                jnp.sum(jnp.where(real, 0.0, total), axis=1, keepdims=True))

    row64 = iota(0, (64, 128))

    def place_of(row):
        return row // 24, (row % 24) // 6, row % 6

    def setup_rounds():
        found = jnp.full((64, 128), -1.0, F32)
        for s in range(2):
            tiles = {o: info_recv[s, slot_of(*o)] for o in OFFSETS}
            if s == 0:
                tiles[(0, 0)] = info_send[...]
            roles = assemble(tiles, -1.0)
            coltile[4 * s + 0] = roles[0]
            coltile[4 * s + 1] = roles[2]
            coltile[4 * s + 2] = roll(roles[0], -32)
            coltile[4 * s + 3] = roll(roles[1], -32)
            if s == 0:
                for role in range(4):
                    coltile[8 + role] = roll(roles[role], -64)
                corner = [jnp.full((4, 128), -1.0, F32) for _ in range(4)]
                row4 = iota(0, (4, 128))
                for j, tile in enumerate((roles[0], roles[2], roll(roles[0], -32), roll(roles[1], -32))):
                    for c in range(4):
                        sx, sy = c // 2, c % 2
                        spot = (lane == (3 * sy) * 8 + 7 * sx) & (sub == 7 * sy)
                        value = jnp.max(jnp.max(jnp.where(spot, tile, -1.0), axis=1, keepdims=True), axis=0, keepdims=True)
                        corner[j] = jnp.where(row4 == c, value, corner[j])
                    edgecol[j] = corner[j]
            lane64 = iota(1, (64, 128))
            side, at_qx, at_qy = place_of(row64)
            role_at = jnp.where((at_qx == 0) | (at_qx == 3), 1, 0) + jnp.where((at_qy == 0) | (at_qy == 5), 2, 0)
            x_at = jnp.where(at_qx == 2, 4, jnp.where(at_qx == 3, 7, 0))
            spot = 96 + 8 * jnp.clip(at_qy - 1, 0, TILES - 1) + x_at
            for role in range(4):
                spread = jnp.broadcast_to(jnp.max(roles[role], axis=0, keepdims=True), (64, 128))
                found = jnp.where((side == s) & (role_at == role) & (lane64 == spot), spread, found)
        wanted = jnp.broadcast_to(jnp.max(found, axis=1, keepdims=True), (64, 128))
        cval[0] = wanted
        row24 = iota(0, (24, 128))
        lane24 = iota(1, (24, 128))
        x24, t24 = lane24 % 8, (lane24 // 8) % TILES
        for role in range(4):
            if role % 2:
                want_x = jnp.where(x24 == 0, 0, jnp.where(x24 == 7, 3, -1))
            else:
                want_x = 1 + x24 // 4
            if role // 2:
                want_y = jnp.where(t24 == 0, 0, jnp.where(t24 == TILES - 1, 5, -1))
            else:
                want_y = 1 + t24
            zmask[role] = jnp.where((row24 // 6 == want_x) & (row24 % 6 == want_y), 1.0, 0.0)

    def setup_aggregates():
        wanted = cval[0]
        cells = jnp.transpose(gath[0])
        for b in range(16):
            row = jnp.broadcast_to(cells[64 + b:65 + b], (64, 128))
            onehot[pl.ds(64 * b, 64), :] = jnp.where(wanted == row, 1.0, 0.0).astype(BF16)
        for p, total in enumerate(by_aggregate(pltpu.roll(gath[0], 96, 1))):
            ksum[p] = jnp.broadcast_to(total, (64, 128))

    def coarse_values(k):
        r_re, r_im = by_aggregate(gath[k])
        k_re, k_im = ksum[0], ksum[1]
        norm = k_re * k_re + k_im * k_im
        norm = jnp.where(norm > 0.0, norm, 1.0)
        cval[0] = (r_im * k_im - r_re * k_re) / norm
        cval[1] = (-r_re * k_im - r_im * k_re) / norm

    def sides_rounds(k):
        cells = []
        for s in range(2):
            tiles = {}
            for ox, oy in OFFSETS:
                if s == 0 and ox == 0 and oy == 0:
                    tiles[(ox, oy)] = stage[k, 2]
                elif s == 0 and ox and oy:
                    tiles[(ox, oy)] = rd[k, corner_of(ox, oy), 0]
                elif s == 0 and oy:
                    tiles[(ox, oy)] = ry[k, 0, 0] if oy < 0 else ry[k, 1, 2]
                else:
                    tiles[(ox, oy)] = rz[k, s, slot_of(ox, oy)]
            roles = assemble(tiles, 0.0)
            cells.append([(role, roll(role, -32)) for role in roles])
        for r in range(6):
            now = float(r)
            for s in range(2):
                c = cells[s]
                c[0], c[1] = blend(c[0], c[1], coltile[4 * s + 0] == now)
                c[2], c[3] = blend(c[2], c[3], coltile[4 * s + 1] == now)
                c[0], c[2] = blend(c[0], c[2], coltile[4 * s + 2] == now)
                c[1], c[3] = blend(c[1], c[3], coltile[4 * s + 3] == now)
            for role in range(4):
                cells[0][role], cells[1][role] = blend(cells[0][role], cells[1][role], coltile[8 + role] == now)
        return cells

    def main_rounds(k):
        def lines(planes, rows):
            return tuple(
                jnp.concatenate([cor[k, p, pl.ds(x * PY + y, 1), :] for x in planes for y in rows], axis=0) for p in range(2))

        c0 = lines((1, 8), (8, 39))
        px = lines((0, 9), (8, 39))
        halo_rows = []
        for p in range(2):
            parts = []
            for x_at in (0, 7):
                parts += [ry[k, 0, 1 + p, pl.ds(x_at, 1), :], ry[k, 1, p, pl.ds(x_at, 1), :]]
            halo_rows.append(jnp.concatenate(parts, axis=0))
        py = tuple(halo_rows)
        diagonal = []
        for p in range(2):
            parts = []
            for c in range(4):
                parts.append(rd[k, c, 1, pl.ds(p * 4 + (3 - c), 1), :])
            diagonal.append(jnp.concatenate(parts, axis=0))
        pxy = tuple(diagonal)
        for r in range(6):
            now = float(r)
            c0, px = blend(c0, px, edgecol[0] == now)
            py, pxy = blend(py, pxy, edgecol[1] == now)
            c0, py = blend(c0, py, edgecol[2] == now)
            px, pxy = blend(px, pxy, edgecol[3] == now)
        for own, halo, ox in ((1, 0, -1), (8, 9, 1)):
            a = tuple(cor[k, p, pl.ds(own * PY + 8, 32), :] for p in range(2))
            b = tuple(cor[k, p, pl.ds(halo * PY + 8, 32), :] for p in range(2))
            a, b = blend(a, b, jnp.broadcast_to(has_x[ox], (32, 128)))
            for p in range(2):
                cor[k, p, pl.ds(own * PY + 8, 32), :] = a[p]
                cor[k, p, pl.ds(halo * PY + 8, 32), :] = b[p]
        for own, halo, oy in ((8, 7, -1), (39, 40, 1)):
            a = tuple(stage[k, p if oy < 0 else 3 + p] for p in range(2))
            b = tuple(ry[k, 0, 1 + p] if oy < 0 else ry[k, 1, p] for p in range(2))
            a, b = blend(a, b, jnp.broadcast_to(has_y[oy], (8, 128)))
            for p in range(2):
                cor[k, p, pl.ds(PY + own, 8, stride=PY), :] = a[p]
                cor[k, p, pl.ds(PY + halo, 8, stride=PY), :] = b[p]
        for c in range(4):
            sx, sy = c // 2, c % 2
            own_x, halo_x = (1, 8)[sx], (0, 9)[sx]
            own_y, halo_y = (8, 39)[sy], (7, 40)[sy]
            for p in range(2):
                cor[k, p, pl.ds(own_x * PY + own_y, 1), :] = c0[p][c:c + 1]
                cor[k, p, pl.ds(halo_x * PY + own_y, 1), :] = px[p][c:c + 1]
                cor[k, p, pl.ds(own_x * PY + halo_y, 1), :] = py[p][c:c + 1]
                cor[k, p, pl.ds(halo_x * PY + halo_y, 1), :] = pxy[p][c:c + 1]

    def update(k, cells):
        last = k == SWEEPS - 1
        for p in range(2):
            turned = [pltpu.roll(cells[0][role][p], zf, 1) for role in range(4)]

            def term(role, t, x):
                at_qx = (0 if x == 0 else 3) if role % 2 else 1 + x // 4
                at_qy = (0 if t == 0 else 5) if role // 2 else 1 + t
                return jnp.broadcast_to(cval[p, pl.ds(at_qx * 6 + at_qy, 1), :], (8, 128))

            for x in range(10):
                if last and x in (0, 9):
                    continue
                role = 1 if x in (0, 9) else 0
                near = min(max(x - 1, 0), 7)
                for t in range(TILES):
                    value = term(role, t, (near // 4) * 4 if role == 0 else near)
                    column = roll(turned[role], -(8 * t + near))
                    rows = pl.ds(x * PY + 8 + 8 * t, 8)
                    value = value + fld[p, rows, :] + jnp.where(at_face, column, cor[k, p, rows, :])
                    if last:
                        out[p, x - 1, pl.ds(8 * t, 8), :] = value
                    else:
                        fld[p, rows, :] = value
                if last:
                    continue
                for t, at, y in ((0, 0, 7), (TILES - 1, 7, 40)):
                    column = roll(turned[2 + role], -(8 * t + near))[at:at + 1]
                    place = pl.ds(x * PY + y, 1)
                    value = term(2 + role, t, near)[0:1] + fld[p, place, :]
                    fld[p, place, :] = value + jnp.where(at_face[0:1], column, cor[k, p, place, :])
            if not last:
                other = cval[p, pl.ds(24, 24), :]
                for role in range(4):
                    halo = jnp.broadcast_to(jnp.sum(other * zmask[role], axis=0, keepdims=True), (8, 128))
                    fz[role, p] = fz[role, p] + cells[1][role][p] + halo

    for k in range(SWEEPS):
        row = row_of(first_pass() if k == 0 else residual_pass(), 16 * core)
        row_send[k, first_row] = row + fixed_row if k == 0 else row
        if k == 0:
            jacobi(k)
            pack_halo(k)
            pl.semaphore_wait(barrier, count)
            pair_copy(k).start()
            for_info(lambda copy: copy.start())
        else:
            pair_copy(k).start()
            jacobi(k)
            pack_halo(k)
        for_halo(k, lambda copy: copy.start())
        pair_copy(k).wait_recv()
        gather_start(k)
        if k == 0:
            for_info(lambda copy: copy.wait_recv(), True)
            setup_rounds()
        pair_copy(k).wait_send()
        for_halo(k, lambda copy: copy.wait_recv(), True)
        cells = sides_rounds(k)
        for_halo(k, lambda copy: copy.wait_send())
        main_rounds(k)
        if k == 0:
            for_info(lambda copy: copy.wait_send())
        gather_every(k).wait_recv()
        if k == 0:
            setup_aggregates()
        coarse_values(k)
        update(k, cells)
        gather_every(k).wait_send()


def solution(mesh):
    nx, ny = mesh.shape["gx"], mesh.shape["gy"]

    def step(adjoint_source, velocity, damping, face_rounds, aggregates):
        vmem = pl.BlockSpec(memory_space=pltpu.VMEM)
        hbm = pl.BlockSpec(memory_space=pltpu.MemorySpace.HBM)
        smem = pl.BlockSpec(memory_space=pltpu.SMEM)
        dma = pltpu.SemaphoreType.DMA
        tile = (8, 128)
        block = (CX, CY, CZ)
        return pl.pallas_call(
            functools.partial(kernel, nx, ny),
            out_shape=jax.ShapeDtypeStruct((2,) + block, F32),
            in_specs=[hbm, hbm, hbm, smem, smem],
            out_specs=vmem,
            scratch_shapes=[
                pltpu.VMEM((2,) + block, F32), pltpu.VMEM(block, F32), pltpu.VMEM(block, F32), dma((3,)),
                pltpu.VMEM(block, F32), pltpu.VMEM(block, F32), pltpu.VMEM(block, F32), pltpu.VMEM(block, F32),
                pltpu.VMEM((2,) + block, F32),
                pltpu.VMEM((2, CX * PY, CZ), F32), pltpu.VMEM((2, CX * PY, CZ), F32),
                pltpu.VMEM((SWEEPS, 2, 10 * PY, CZ), F32),
                pltpu.VMEM((2, 10 * PY, CZ), F32),
                pltpu.VMEM((4, 2) + tile, F32),
                pltpu.VMEM((12,) + tile, F32), pltpu.VMEM((4, 4, 128), F32),
                pltpu.VMEM((1024, 128), BF16), pltpu.VMEM((2, 64, 128), F32), pltpu.VMEM((2, 64, 128), F32),
                pltpu.VMEM((4, 24, 128), F32),
                pltpu.VMEM(tile, F32), pltpu.VMEM((2, 9) + tile, F32),
                pltpu.VMEM((SWEEPS, 7) + tile, F32), pltpu.VMEM((SWEEPS, 2, 9) + tile, F32),
                pltpu.VMEM((SWEEPS, 2, 3) + tile, F32), pltpu.VMEM((SWEEPS, 4, 2) + tile, F32),
                pltpu.VMEM((SWEEPS,) + tile, F32), pltpu.VMEM((SWEEPS,) + tile, F32), pltpu.VMEM((SWEEPS,) + tile, F32),
                pltpu.VMEM((SWEEPS, 128, 128), F32),
                dma((18,)), dma((18,)), dma((SWEEPS, 18)), dma((SWEEPS, 18)),
                dma((SWEEPS, 2)), dma((SWEEPS, 2)), dma((SWEEPS,)), dma((SWEEPS,)), dma((SWEEPS,)), dma((SWEEPS,)),
            ],
            compiler_params=pltpu.CompilerParams(
                collective_id=0, has_side_effects=True, vmem_limit_bytes=64 * 1024 * 1024
            ),
        )(adjoint_source, velocity, damping, face_rounds, jnp.transpose(aggregates, (0, 2, 1)))

    placed = (
        P(None, "gx", "gy", "gz"),
        P("gx", "gy", "gz"),
        P("gx", "gy", "gz"),
        P("gx", "gy", "gz", None),
        P("gx", "gy", "gz"),
    )
    return jax.shard_map(
        step, mesh=mesh, in_specs=placed, out_specs=P(None, "gx", "gy", "gz"), check_vma=False
    )
```

```python
import functools

import jax
import jax.numpy as jnp
from jax import lax
from jax.experimental import pallas as pl
from jax.experimental.pallas import tpu as pltpu
from jax.sharding import PartitionSpec as P

MESH = pl.DeviceIdType.MESH
F32 = jnp.float32
BF16 = jnp.bfloat16

CX, CY, CZ = 8, 32, 128
PY = 48
TILES = CY // 8
SWEEPS = 3
SMOOTH = 4
GAMMA_RE = 0.6
GAMMA_IM = 0.25
RELAX = 0.8
OMEGA_SQ = 9.0

OFFSETS = [(ox, oy) for ox in (-1, 0, 1) for oy in (-1, 0, 1)]
OFFSETS.sort(key=lambda o: -abs(o[0]) - abs(o[1]))


def slot_of(ox, oy):
    return (ox + 1) * 3 + (oy + 1)


def corner_of(ox, oy):
    return (1 if ox > 0 else 0) * 2 + (1 if oy > 0 else 0)


def iota(dim, shape=(8, 128)):
    return lax.broadcasted_iota(jnp.int32, shape, dim)


def roll(v, lanes, subs=0):
    if isinstance(lanes, int):
        lanes = lanes % 128
    if not isinstance(lanes, int) or lanes:
        v = pltpu.roll(v, lanes, 1)
    if subs % 8:
        v = pltpu.roll(v, subs % 8, 0)
    return v


def blend(a, b, mask):
    d_re = b[0] - a[0]
    d_im = b[1] - a[1]
    t_re = GAMMA_RE * d_re - GAMMA_IM * d_im
    t_im = GAMMA_RE * d_im + GAMMA_IM * d_re
    if mask is not None:
        t_re = jnp.where(mask, t_re, 0.0)
        t_im = jnp.where(mask, t_im, 0.0)
    return (a[0] + t_re, a[1] + t_im), (b[0] - t_re, b[1] - t_im)


def kernel(
    nx, ny,
    src_in, vel_in, dmp_in, rounds, aggs, out,
    src, vel, dmp, in_sem,
    kap, kdm, mre, mim, res, ping, pong, cor, fld, fz,
    coltile, edgecol, onehot, ksum, cval, zmask,
    info_send, info_recv, stage, corners, rz, ry, rd, row_send, pair_recv, chip_send, gath,
    info_ss, info_rs, h_ss, h_rs, x_ss, x_rs, pair_ss, pair_rs, ga_ss, ga_rs,
):
    ix, iy, iz = lax.axis_index("gx"), lax.axis_index("gy"), lax.axis_index("gz")
    lane, sub = iota(1), iota(0)
    lx, lt = lane % 8, (lane // 8) % TILES
    zf = jnp.where(iz == 0, 127, 0).astype(jnp.int32)
    at_face = lane == zf
    first_lane, last_lane = lane == 0, lane == 127
    lane32 = iota(1, (32, 128))
    first32, last32 = lane32 == 0, lane32 == 127

    has_x = {-1: ix > 0, 1: ix < nx - 1}
    has_y = {-1: iy > 0, 1: iy < ny - 1}

    def exists(ox, oy):
        if ox and oy:
            return jnp.logical_and(has_x[ox], has_y[oy])
        if ox:
            return has_x[ox]
        if oy:
            return has_y[oy]
        return None

    def guarded(cond, fn):
        if cond is None:
            fn()
        else:
            pl.when(cond)(fn)

    def device(ox, oy, oz):
        return (ix + ox, iy + oy, (1 - iz) if oz else iz)

    core = lax.rem(iy, 2)
    at_x, at_y, at_z = lax.rem(ix, 4), ix // 4, iz * (ny // 2) + iy // 2
    nz = ny
    pair = (ix, iy + 1 - 2 * core, iz)
    across = sorted(((dx, dy) for dx in range(4) for dy in range(4)), key=lambda d: -min(d[0], 4 - d[0]) - min(d[1], 4 - d[1]))
    across_x = [lax.rem(at_y + dy, 4) * 4 + lax.rem(at_x + dx, 4) for dx, dy in across]

    def for_chips(fn):
        def layer(i, carry):
            step = (i + 1) // 2
            there = lax.rem(at_z + nz // 2 + jnp.where(lax.rem(i, 2) == 1, nz - step, step), nz)
            ty, tz = lax.rem(there, ny // 2) * 2 + core, there // (ny // 2)
            for j in range(16):
                fn(i * 16 + j, (across_x[j], ty, tz))
            return carry
        lax.fori_loop(0, nz - 1, layer, 0)
        for j in range(15):
            fn((nz - 1) * 16 + j, (across_x[j], iy, iz))

    loads = [pltpu.make_async_copy(whole, local, in_sem.at[i])
             for i, (whole, local) in enumerate(((vel_in, vel), (dmp_in, dmp), (src_in, src)))]
    for load in loads:
        load.start()

    zero = jnp.zeros((8, 128), F32)
    for k in range(SWEEPS):
        for p in range(2):
            for x in range(10):
                tiles = range(6) if x in (0, 9) else (0, 5)
                for t in tiles:
                    cor[k, p, pl.ds(x * PY + 8 * t, 8), :] = zero
        for s in range(2):
            for o in range(9):
                rz[k, s, o] = zero
        for o in range(2):
            for j in range(3):
                ry[k, o, j] = zero
        for o in range(4):
            rd[k, o] = zero
    for s in range(2):
        for o in range(9):
            info_recv[s, o] = zero - 1.0

    barrier = pltpu.get_barrier_semaphore()
    count = jnp.int32(16 * nz - 1 + 1)
    for ox, oy in OFFSETS:
        if oy:
            def tell(ox=ox, oy=oy):
                for oz in (1, 0):
                    pl.semaphore_signal(barrier, inc=1, device_id=device(ox, oy, oz), device_id_type=MESH)
            guarded(exists(ox, oy), tell)
            count = count + jnp.where(exists(ox, oy), 2, 0)

    def tell_chip(slot, target):
        pl.semaphore_signal(barrier, inc=1, device_id=target, device_id_type=MESH)

    for_chips(tell_chip)
    tell_chip(0, pair)

    for buf in (ping, pong):
        for p in range(2):
            for x in range(8):
                buf[p, pl.ds(x * PY, 8), :] = zero
                buf[p, pl.ds(x * PY + 40, 8), :] = zero
    for p in range(2):
        for x in range(10):
            for t in range(6):
                fld[p, pl.ds(x * PY + 8 * t, 8), :] = zero
        for role in range(4):
            fz[role, p] = zero

    for load in loads:
        load.wait()
    for x in range(CX):
        v = vel[x]
        kappa = OMEGA_SQ / (v * v)
        damp = kappa * dmp[x]
        d_re = 14.0 - kappa
        scale = RELAX / (d_re * d_re + damp * damp)
        kap[x] = 16.0 - kappa
        kdm[x] = damp
        mre[x] = d_re * scale
        mim[x] = -damp * scale

    def face(i, inside):
        return jnp.where(inside, rounds[0, 0, 0, i].astype(F32), -1.0)

    low_x, high_x = face(0, ix > 0), face(1, ix < nx - 1)
    low_y, high_y = face(2, iy > 0), face(3, iy < ny - 1)
    depth = jnp.where(iz == 0, rounds[0, 0, 0, 5].astype(F32), rounds[0, 0, 0, 4].astype(F32))
    ids = [[aggs[qx, 0, qy].astype(F32) for qy in range(TILES)] for qx in range(2)]
    info = jnp.where(lx == 0, low_x, jnp.where(lx == 7, high_x, -1.0))
    col_y = jnp.where((lt == 0) & (sub == 0), low_y, jnp.where((lt == TILES - 1) & (sub == 7), high_y, -1.0))
    info = jnp.where(lane >= 32, col_y, info)
    info = jnp.where(lane >= 64, depth, info)
    for qx in range(2):
        for qy in range(TILES):
            info = jnp.where((lane >= 96) & (lx // 4 == qx) & (lt == qy), ids[qx][qy], info)
    info_send[...] = info

    low_rows = sub < 4
    lane1 = iota(1, (1, 128))

    def row_of(sums, first):
        rows = [jnp.sum(sums[p][qx][t], axis=0, keepdims=True) for p in range(2) for qx in range(2) for t in range(TILES)]
        total = jnp.sum(jnp.concatenate(rows, axis=0), axis=1, keepdims=True)
        spread = jnp.where(iota(1, (16, 128)) == iota(0, (16, 128)) + first, jnp.broadcast_to(total, (16, 128)), 0.0)
        return jnp.sum(spread, axis=0, keepdims=True)

    def rows_of(v, t):
        return v[8 * t:8 * t + 8]

    sums = [[[zero] * TILES for _ in range(2)] for _ in range(2)]
    for x in range(CX):
        kappa, damp = 16.0 - kap[x], kdm[x]
        for t in range(TILES):
            sums[0][x // 4][t] = sums[0][x // 4][t] + rows_of(kappa, t)
            sums[1][x // 4][t] = sums[1][x // 4][t] + rows_of(damp, t)
    fixed_row = row_of(sums, 32 + 16 * core)
    for qx in range(2):
        for t in range(TILES):
            fixed_row = fixed_row + jnp.where(lane1 == 64 + 8 * core + qx * TILES + t, ids[qx][t], 0.0)

    def assemble(tiles, default):
        def pick(parts):
            value = jnp.full((8, 128), default, F32)
            for mask, tile in parts:
                value = jnp.where(mask, tile, value)
            return value
        t0, t3 = (lt == 0) & (sub == 0), (lt == TILES - 1) & (sub == 7)
        x0, x7 = lx == 0, lx == 7
        across_x = pick([(x0, roll(tiles[(-1, 0)], -7)), (x7, roll(tiles[(1, 0)], 7))])
        across_y = pick([(t0, roll(tiles[(0, -1)], -24, 1)), (t3, roll(tiles[(0, 1)], 24, -1))])
        across_xy = pick([
            (x0 & t0, roll(tiles[(-1, -1)], -31, 1)),
            (x0 & t3, roll(tiles[(-1, 1)], 17, -1)),
            (x7 & t0, roll(tiles[(1, -1)], -17, 1)),
            (x7 & t3, roll(tiles[(1, 1)], 31, -1)),
        ])
        return [tiles[(0, 0)], across_x, across_y, across_xy]

    def smooth_z(v):
        return 2.0 * v + jnp.where(first32, 0.0, pltpu.roll(v, 1, 1)) + jnp.where(last32, 0.0, pltpu.roll(v, 127, 1))

    def residual_pass():
        lefts = []
        for p in range(2):
            c0, px, py, pxy = (fz[role, p] for role in range(4))
            t0, t3 = (lt == 0) & (sub == 0), (lt == TILES - 1) & (sub == 7)

            def smooth_y(v, across):
                up = pltpu.roll(v, 1, 0)
                up = jnp.where(sub == 0, roll(up, 8), up)
                up = jnp.where(t0, across, up)
                down = pltpu.roll(v, 7, 0)
                down = jnp.where(sub == 7, roll(down, -8), down)
                down = jnp.where(t3, across, down)
                return up + 2.0 * v + down

            yc, yx = smooth_y(c0, py), smooth_y(px, pxy)
            w = 2.0 * yc + jnp.where(lx == 0, yx, roll(yc, 1)) + jnp.where(lx == 7, yx, roll(yc, -1))
            lefts.append(pltpu.roll(w, zf, 1))
        sums = [[[zero] * TILES for _ in range(2)] for _ in range(2)]
        ys = [[None] * 10 for _ in range(2)]

        def y_smoothed(p, x):
            if ys[p][x] is None:
                base = x * PY
                ys[p][x] = (fld[p, pl.ds(base + 7, 32), :] + fld[p, pl.ds(base + 9, 32), :]
                            + 2.0 * fld[p, pl.ds(base + 8, 32), :])
            return ys[p][x]

        for x in range(CX):
            smoothed = []
            for p in range(2):
                v = y_smoothed(p, x) + 2.0 * y_smoothed(p, x + 1) + y_smoothed(p, x + 2)
                halo = jnp.concatenate([roll(lefts[p], -(8 * t + x)) for t in range(TILES)], axis=0)
                smoothed.append(smooth_z(v) + jnp.where(lane32 == zf, halo, 0.0))
            f_re = fld[0, pl.ds((x + 1) * PY + 8, 32), :]
            f_im = fld[1, pl.ds((x + 1) * PY + 8, 32), :]
            a, b = kap[x], kdm[x]
            r_re = src[0, x] + 0.25 * smoothed[0] - a * f_re + b * f_im
            r_im = src[1, x] + 0.25 * smoothed[1] - a * f_im - b * f_re
            res[0, x] = r_re
            res[1, x] = r_im
            for t in range(TILES):
                sums[0][x // 4][t] = sums[0][x // 4][t] + rows_of(r_re, t)
                sums[1][x // 4][t] = sums[1][x // 4][t] + rows_of(r_im, t)
        return sums

    def first_pass():
        sums = [[[zero] * TILES for _ in range(2)] for _ in range(2)]
        for x in range(CX):
            for p in range(2):
                v = src[p, x]
                res[p, x] = v
                for t in range(TILES):
                    sums[p][x // 4][t] = sums[p][x // 4][t] + rows_of(v, t)
        return sums

    def jacobi(k):
        for x in range(CX):
            a, b = mre[x], mim[x]
            r_re, r_im = res[0, x], res[1, x]
            ping[0, pl.ds(x * PY + 8, 32), :] = a * r_re - b * r_im
            ping[1, pl.ds(x * PY + 8, 32), :] = a * r_im + b * r_re
        buffers = [ping, pong]
        for step in range(1, SMOOTH):
            now, later = buffers[(step - 1) % 2], buffers[step % 2]
            last = step == SMOOTH - 1
            ys = [[None] * CX for _ in range(2)]

            def y_smoothed(p, x):
                if x < 0 or x >= CX:
                    return None
                if ys[p][x] is None:
                    base = x * PY
                    ys[p][x] = (now[p, pl.ds(base + 7, 32), :] + now[p, pl.ds(base + 9, 32), :]
                                + 2.0 * now[p, pl.ds(base + 8, 32), :])
                return ys[p][x]

            for x in range(CX):
                misfit, old = [], []
                for p in range(2):
                    v = 2.0 * y_smoothed(p, x)
                    for near in (y_smoothed(p, x - 1), y_smoothed(p, x + 1)):
                        if near is not None:
                            v = v + near
                    c = now[p, pl.ds(x * PY + 8, 32), :]
                    old.append(c)
                    misfit.append(res[p, x] + 0.25 * smooth_z(v) - 2.0 * c)
                a, b = mre[x], mim[x]
                new_re = 0.2 * old[0] + (a * misfit[0] - b * misfit[1])
                new_im = 0.2 * old[1] + (a * misfit[1] + b * misfit[0])
                if last:
                    cor[k, 0, pl.ds((x + 1) * PY + 8, 32), :] = new_re
                    cor[k, 1, pl.ds((x + 1) * PY + 8, 32), :] = new_im
                else:
                    later[0, pl.ds(x * PY + 8, 32), :] = new_re
                    later[1, pl.ds(x * PY + 8, 32), :] = new_im

    def remote(src_ref, dst_ref, ssem, rsem, target):
        return pltpu.make_async_remote_copy(
            src_ref=src_ref, dst_ref=dst_ref, send_sem=ssem, recv_sem=rsem,
            device_id=target, device_id_type=MESH)

    def halo_copies(k, ox, oy, oz, incoming):
        mine, theirs = oz * 9 + slot_of(ox, oy), oz * 9 + slot_of(-ox, -oy)
        target = device(ox, oy, oz)
        if oz == 0 and ox and oy:
            part = corners.at[k, corner_of(ox, oy), pl.ds(0, 3)]
            there, at_home = rd.at[k, corner_of(-ox, -oy), pl.ds(0, 3)], rd.at[k, corner_of(ox, oy), pl.ds(0, 3)]
        elif oz == 0 and oy:
            part = stage.at[k, pl.ds(0, 3)] if oy < 0 else stage.at[k, pl.ds(2, 3)]
            there, at_home = ry.at[k, 1 if oy < 0 else 0], ry.at[k, 0 if oy < 0 else 1]
        elif oy:
            leaving, coming = (pl.ds(0, 1), pl.ds(7, 1)) if oy < 0 else (pl.ds(7, 1), pl.ds(0, 1))
            part = stage.at[k, 2, leaving]
            there, at_home = rz.at[k, 1, slot_of(-ox, -oy), leaving], rz.at[k, 1, slot_of(ox, oy), coming]
        else:
            part = stage.at[k, 2]
            there, at_home = rz.at[k, oz, slot_of(-ox, -oy)], rz.at[k, oz, slot_of(ox, oy)]
        if incoming:
            return remote(part, at_home, h_ss.at[k, mine], h_rs.at[k, mine], target)
        return remote(part, there, h_ss.at[k, mine], h_rs.at[k, theirs], target)

    def plane_copies(k, ox, incoming):
        own, halo = (1, 9) if ox < 0 else (8, 0)
        part = cor.at[k, :, pl.ds(own * PY + 8, 32), :]
        there = cor.at[k, :, pl.ds(halo * PY + 8, 32), :]
        at_home = cor.at[k, :, pl.ds((0 if ox < 0 else 9) * PY + 8, 32), :]
        mine, theirs = (0, 1) if ox < 0 else (1, 0)
        if incoming:
            return remote(part, at_home, x_ss.at[k, mine], x_rs.at[k, mine], device(ox, 0, 0))
        return remote(part, there, x_ss.at[k, mine], x_rs.at[k, theirs], device(ox, 0, 0))

    def for_offsets(fn):
        for ox, oy in OFFSETS:
            guarded(exists(ox, oy), functools.partial(fn, ox, oy))

    def far_halo(k, fn, incoming=False):
        for_offsets(lambda ox, oy: fn(halo_copies(k, ox, oy, 1, incoming)))

    def near_halo(k, fn, incoming=False, planes=True):
        def each(ox, oy):
            if (ox, oy) == (0, 0):
                return
            if planes and oy == 0:
                fn(plane_copies(k, ox, incoming))
            fn(halo_copies(k, ox, oy, 0, incoming))
        for_offsets(each)

    def all_halo(k, fn, incoming=False, planes=True):
        def each(ox, oy):
            fn(halo_copies(k, ox, oy, 1, incoming))
            if (ox, oy) != (0, 0):
                fn(halo_copies(k, ox, oy, 0, incoming))
                if planes and oy == 0:
                    fn(plane_copies(k, ox, incoming))
        for_offsets(each)

    def for_planes(k, fn):
        for ox in (-1, 1):
            guarded(exists(ox, 0), functools.partial(lambda ox: fn(plane_copies(k, ox, False)), ox))

    def info_copies(ox, oy, oz, incoming):
        mine, theirs = oz * 9 + slot_of(ox, oy), oz * 9 + slot_of(-ox, -oy)
        target = device(ox, oy, oz)
        leaving = coming = pl.ds(0, 8)
        if oy:
            leaving, coming = (pl.ds(0, 1), pl.ds(7, 1)) if oy < 0 else (pl.ds(7, 1), pl.ds(0, 1))
        part = info_send.at[leaving]
        if incoming:
            return remote(part, info_recv.at[oz, slot_of(ox, oy), coming], info_ss.at[mine], info_rs.at[mine], target)
        return remote(part, info_recv.at[oz, slot_of(-ox, -oy), leaving], info_ss.at[mine], info_rs.at[theirs], target)

    def for_info(fn, incoming=False):
        def each(ox, oy):
            fn(info_copies(ox, oy, 1, incoming))
            if (ox, oy) != (0, 0):
                fn(info_copies(ox, oy, 0, incoming))
        for_offsets(each)

    def pack_halo(k):
        packed = zero
        for p in range(2):
            for x in range(CX):
                for t in range(TILES):
                    v = cor[k, p, pl.ds((x + 1) * PY + 8 + 8 * t, 8), :]
                    to = p * 32 + t * 8 + x
                    packed = jnp.where(lane == to, pltpu.roll(v, jnp.where(iz == 0, to + 1, to), 1), packed)
        stage[k, 2] = packed
        for p in range(2):
            stage[k, p] = cor[k, p, pl.ds(PY + 8, 8, stride=PY), :]
            stage[k, 3 + p] = cor[k, p, pl.ds(PY + 39, 8, stride=PY), :]
        for c in range(4):
            x, y, row = (1, 8)[c // 2], (8, 39)[c % 2], (0, 7)[c % 2]
            for p in range(2):
                corners[k, c, pl.ds(p, 1), :] = cor[k, p, pl.ds(x * PY + y, 1), :]
            corners[k, c, pl.ds(2, 1), :] = packed[row:row + 1]

    first_row = pl.ds(0, 1)
    others = pl.ds(0, 16 * nz - 1)

    def pair_copy(k):
        return remote(row_send.at[k, first_row], pair_recv.at[k, first_row], pair_ss.at[k], pair_rs.at[k], pair)

    def gather_start(k):
        chip = row_send[k, first_row] + pair_recv[k, first_row]
        chip_send[k, first_row] = chip
        gath[k, pl.ds(16 * nz - 1, 1)] = chip
        for_chips(lambda slot, target: remote(
            chip_send.at[k, first_row], gath.at[k, pl.ds(slot, 1)], ga_ss.at[k], ga_rs.at[k], target).start())

    def gather_every(k):
        return remote(gath.at[k, others], gath.at[k, others], ga_ss.at[k], ga_rs.at[k], pair)

    lane_n = iota(1, (128, 128))

    def by_aggregate(values):
        whole = jnp.where(lane_n < 32, values, 0.0)
        high = whole.astype(BF16).astype(F32)
        rest = whole - high
        middle = rest.astype(BF16).astype(F32)
        split = high + pltpu.roll(middle, 32, 1) + pltpu.roll(rest - middle, 64, 1)
        found = jnp.dot(onehot[...], split.astype(BF16), preferred_element_type=F32)
        lane64 = iota(1, (64, 128))
        total = jnp.zeros((64, 128), F32)
        for b in range(16):
            mine = (lane64 % 8 == b % 8) & ((lane64 // 16) % 2 == b // 8)
            total = jnp.where(mine, found[64 * b:64 * b + 64], total)
        total = jnp.where(lane64 < 96, total, 0.0)
        real = (lane64 // 8) % 2 == 0
        return (jnp.sum(jnp.where(real, total, 0.0), axis=1, keepdims=True),
                jnp.sum(jnp.where(real, 0.0, total), axis=1, keepdims=True))

    row64 = iota(0, (64, 128))

    def place_of(row):
        return row // 24, (row % 24) // 6, row % 6

    def setup_rounds():
        found = jnp.full((64, 128), -1.0, F32)
        for s in range(2):
            tiles = {o: info_recv[s, slot_of(*o)] for o in OFFSETS}
            if s == 0:
                tiles[(0, 0)] = info_send[...]
            roles = assemble(tiles, -1.0)
            coltile[4 * s + 0] = roles[0]
            coltile[4 * s + 1] = roles[2]
            coltile[4 * s + 2] = roll(roles[0], -32)
            coltile[4 * s + 3] = roll(roles[1], -32)
            if s == 0:
                for role in range(4):
                    coltile[8 + role] = roll(roles[role], -64)
                corner = [jnp.full((4, 128), -1.0, F32) for _ in range(4)]
                row4 = iota(0, (4, 128))
                for j, tile in enumerate((roles[0], roles[2], roll(roles[0], -32), roll(roles[1], -32))):
                    for c in range(4):
                        sx, sy = c // 2, c % 2
                        spot = (lane == (3 * sy) * 8 + 7 * sx) & (sub == 7 * sy)
                        value = jnp.max(jnp.max(jnp.where(spot, tile, -1.0), axis=1, keepdims=True), axis=0, keepdims=True)
                        corner[j] = jnp.where(row4 == c, value, corner[j])
                    edgecol[j] = corner[j]
            lane64 = iota(1, (64, 128))
            side, at_qx, at_qy = place_of(row64)
            role_at = jnp.where((at_qx == 0) | (at_qx == 3), 1, 0) + jnp.where((at_qy == 0) | (at_qy == 5), 2, 0)
            x_at = jnp.where(at_qx == 2, 4, jnp.where(at_qx == 3, 7, 0))
            spot = 96 + 8 * jnp.clip(at_qy - 1, 0, TILES - 1) + x_at
            for role in range(4):
                spread = jnp.broadcast_to(jnp.max(roles[role], axis=0, keepdims=True), (64, 128))
                found = jnp.where((side == s) & (role_at == role) & (lane64 == spot), spread, found)
        wanted = jnp.broadcast_to(jnp.max(found, axis=1, keepdims=True), (64, 128))
        cval[0] = wanted
        row24 = iota(0, (24, 128))
        lane24 = iota(1, (24, 128))
        x24, t24 = lane24 % 8, (lane24 // 8) % TILES
        for role in range(4):
            if role % 2:
                want_x = jnp.where(x24 == 0, 0, jnp.where(x24 == 7, 3, -1))
            else:
                want_x = 1 + x24 // 4
            if role // 2:
                want_y = jnp.where(t24 == 0, 0, jnp.where(t24 == TILES - 1, 5, -1))
            else:
                want_y = 1 + t24
            zmask[role] = jnp.where((row24 // 6 == want_x) & (row24 % 6 == want_y), 1.0, 0.0)

    def setup_aggregates():
        wanted = cval[0]
        cells = jnp.transpose(gath[0])
        for b in range(16):
            row = jnp.broadcast_to(cells[64 + b:65 + b], (64, 128))
            onehot[pl.ds(64 * b, 64), :] = jnp.where(wanted == row, 1.0, 0.0).astype(BF16)
        for p, total in enumerate(by_aggregate(pltpu.roll(gath[0], 96, 1))):
            ksum[p] = jnp.broadcast_to(total, (64, 128))

    def coarse_values(k):
        r_re, r_im = by_aggregate(gath[k])
        k_re, k_im = ksum[0], ksum[1]
        norm = k_re * k_re + k_im * k_im
        norm = jnp.where(norm > 0.0, norm, 1.0)
        cval[0] = (r_im * k_im - r_re * k_re) / norm
        cval[1] = (-r_re * k_im - r_im * k_re) / norm

    def sides_rounds(k):
        cells = []
        for s in range(2):
            tiles = {}
            for ox, oy in OFFSETS:
                if s == 0 and ox == 0 and oy == 0:
                    tiles[(ox, oy)] = stage[k, 2]
                elif s == 0 and ox and oy:
                    tiles[(ox, oy)] = jnp.broadcast_to(rd[k, corner_of(ox, oy), pl.ds(2, 1), :], (8, 128))
                elif s == 0 and oy:
                    tiles[(ox, oy)] = ry[k, 0, 0] if oy < 0 else ry[k, 1, 2]
                else:
                    tiles[(ox, oy)] = rz[k, s, slot_of(ox, oy)]
            roles = assemble(tiles, 0.0)
            cells.append([(role, roll(role, -32)) for role in roles])
        for r in range(6):
            now = float(r)
            for s in range(2):
                c = cells[s]
                c[0], c[1] = blend(c[0], c[1], coltile[4 * s + 0] == now)
                c[2], c[3] = blend(c[2], c[3], coltile[4 * s + 1] == now)
                c[0], c[2] = blend(c[0], c[2], coltile[4 * s + 2] == now)
                c[1], c[3] = blend(c[1], c[3], coltile[4 * s + 3] == now)
            for role in range(4):
                cells[0][role], cells[1][role] = blend(cells[0][role], cells[1][role], coltile[8 + role] == now)
        return cells

    def main_rounds(k):
        def lines(planes, rows):
            return tuple(
                jnp.concatenate([cor[k, p, pl.ds(x * PY + y, 1), :] for x in planes for y in rows], axis=0) for p in range(2))

        c0 = lines((1, 8), (8, 39))
        px = lines((0, 9), (8, 39))
        halo_rows = []
        for p in range(2):
            parts = []
            for x_at in (0, 7):
                parts += [ry[k, 0, 1 + p, pl.ds(x_at, 1), :], ry[k, 1, p, pl.ds(x_at, 1), :]]
            halo_rows.append(jnp.concatenate(parts, axis=0))
        py = tuple(halo_rows)
        diagonal = []
        for p in range(2):
            parts = []
            for c in range(4):
                parts.append(rd[k, c, pl.ds(p, 1), :])
            diagonal.append(jnp.concatenate(parts, axis=0))
        pxy = tuple(diagonal)
        for r in range(6):
            now = float(r)
            c0, px = blend(c0, px, edgecol[0] == now)
            py, pxy = blend(py, pxy, edgecol[1] == now)
            c0, py = blend(c0, py, edgecol[2] == now)
            px, pxy = blend(px, pxy, edgecol[3] == now)
        for own, halo, ox in ((1, 0, -1), (8, 9, 1)):
            a = tuple(cor[k, p, pl.ds(own * PY + 8, 32), :] for p in range(2))
            b = tuple(cor[k, p, pl.ds(halo * PY + 8, 32), :] for p in range(2))
            a, b = blend(a, b, jnp.broadcast_to(has_x[ox], (32, 128)))
            for p in range(2):
                cor[k, p, pl.ds(own * PY + 8, 32), :] = a[p]
                cor[k, p, pl.ds(halo * PY + 8, 32), :] = b[p]
        for own, halo, oy in ((8, 7, -1), (39, 40, 1)):
            a = tuple(stage[k, p if oy < 0 else 3 + p] for p in range(2))
            b = tuple(ry[k, 0, 1 + p] if oy < 0 else ry[k, 1, p] for p in range(2))
            a, b = blend(a, b, jnp.broadcast_to(has_y[oy], (8, 128)))
            for p in range(2):
                cor[k, p, pl.ds(PY + own, 8, stride=PY), :] = a[p]
                cor[k, p, pl.ds(PY + halo, 8, stride=PY), :] = b[p]
        for c in range(4):
            sx, sy = c // 2, c % 2
            own_x, halo_x = (1, 8)[sx], (0, 9)[sx]
            own_y, halo_y = (8, 39)[sy], (7, 40)[sy]
            for p in range(2):
                cor[k, p, pl.ds(own_x * PY + own_y, 1), :] = c0[p][c:c + 1]
                cor[k, p, pl.ds(halo_x * PY + own_y, 1), :] = px[p][c:c + 1]
                cor[k, p, pl.ds(own_x * PY + halo_y, 1), :] = py[p][c:c + 1]
                cor[k, p, pl.ds(halo_x * PY + halo_y, 1), :] = pxy[p][c:c + 1]

    def update(k, cells):
        last = k == SWEEPS - 1
        for p in range(2):
            turned = [pltpu.roll(cells[0][role][p], zf, 1) for role in range(4)]

            def term(role, t, x):
                at_qx = (0 if x == 0 else 3) if role % 2 else 1 + x // 4
                at_qy = (0 if t == 0 else 5) if role // 2 else 1 + t
                return jnp.broadcast_to(cval[p, pl.ds(at_qx * 6 + at_qy, 1), :], (8, 128))

            for x in range(10):
                if last and x in (0, 9):
                    continue
                role = 1 if x in (0, 9) else 0
                near = min(max(x - 1, 0), 7)
                for t in range(TILES):
                    value = term(role, t, (near // 4) * 4 if role == 0 else near)
                    column = roll(turned[role], -(8 * t + near))
                    rows = pl.ds(x * PY + 8 + 8 * t, 8)
                    value = value + fld[p, rows, :] + jnp.where(at_face, column, cor[k, p, rows, :])
                    if last:
                        out[p, x - 1, pl.ds(8 * t, 8), :] = value
                    else:
                        fld[p, rows, :] = value
                if last:
                    continue
                for t, at, y in ((0, 0, 7), (TILES - 1, 7, 40)):
                    column = roll(turned[2 + role], -(8 * t + near))[at:at + 1]
                    place = pl.ds(x * PY + y, 1)
                    value = term(2 + role, t, near)[0:1] + fld[p, place, :]
                    fld[p, place, :] = value + jnp.where(at_face[0:1], column, cor[k, p, place, :])
            if not last:
                other = cval[p, pl.ds(24, 24), :]
                for role in range(4):
                    halo = jnp.broadcast_to(jnp.sum(other * zmask[role], axis=0, keepdims=True), (8, 128))
                    fz[role, p] = fz[role, p] + cells[1][role][p] + halo

    for k in range(SWEEPS):
        row = row_of(first_pass() if k == 0 else residual_pass(), 16 * core)
        row_send[k, first_row] = row + fixed_row if k == 0 else row
        if k == 0:
            jacobi(k)
            pack_halo(k)
            pl.semaphore_wait(barrier, count)
            pair_copy(k).start()
            for_info(lambda copy: copy.start())
        else:
            pair_copy(k).start()
            jacobi(k)
            pack_halo(k)
        far_halo(k, lambda copy: copy.start())
        near_halo(k, lambda copy: copy.start())
        pair_copy(k).wait_recv()
        gather_start(k)
        if k == 0:
            for_info(lambda copy: copy.wait_recv(), True)
            setup_rounds()
        pair_copy(k).wait_send()
        for_planes(k, lambda copy: copy.wait_send())
        all_halo(k, lambda copy: copy.wait_recv(), True)
        cells = sides_rounds(k)
        main_rounds(k)
        all_halo(k, lambda copy: copy.wait_send(), planes=False)
        if k == 0:
            for_info(lambda copy: copy.wait_send())
        gather_every(k).wait_recv()
        if k == 0:
            setup_aggregates()
        coarse_values(k)
        update(k, cells)
        gather_every(k).wait_send()


def solution(mesh):
    nx, ny = mesh.shape["gx"], mesh.shape["gy"]

    def step(adjoint_source, velocity, damping, face_rounds, aggregates):
        vmem = pl.BlockSpec(memory_space=pltpu.VMEM)
        hbm = pl.BlockSpec(memory_space=pltpu.MemorySpace.HBM)
        smem = pl.BlockSpec(memory_space=pltpu.SMEM)
        dma = pltpu.SemaphoreType.DMA
        tile = (8, 128)
        block = (CX, CY, CZ)
        return pl.pallas_call(
            functools.partial(kernel, nx, ny),
            out_shape=pltpu.VMEM((2,) + block, F32),
            in_specs=[hbm, hbm, hbm, smem, smem],
            out_specs=vmem,
            scratch_shapes=[
                pltpu.VMEM((2,) + block, F32), pltpu.VMEM(block, F32), pltpu.VMEM(block, F32), dma((3,)),
                pltpu.VMEM(block, F32), pltpu.VMEM(block, F32), pltpu.VMEM(block, F32), pltpu.VMEM(block, F32),
                pltpu.VMEM((2,) + block, F32),
                pltpu.VMEM((2, CX * PY, CZ), F32), pltpu.VMEM((2, CX * PY, CZ), F32),
                pltpu.VMEM((SWEEPS, 2, 10 * PY, CZ), F32),
                pltpu.VMEM((2, 10 * PY, CZ), F32),
                pltpu.VMEM((4, 2) + tile, F32),
                pltpu.VMEM((12,) + tile, F32), pltpu.VMEM((4, 4, 128), F32),
                pltpu.VMEM((1024, 128), BF16), pltpu.VMEM((2, 64, 128), F32), pltpu.VMEM((2, 64, 128), F32),
                pltpu.VMEM((4, 24, 128), F32),
                pltpu.VMEM(tile, F32), pltpu.VMEM((2, 9) + tile, F32),
                pltpu.VMEM((SWEEPS, 5) + tile, F32), pltpu.VMEM((SWEEPS, 4) + tile, F32), pltpu.VMEM((SWEEPS, 2, 9) + tile, F32),
                pltpu.VMEM((SWEEPS, 2, 3) + tile, F32), pltpu.VMEM((SWEEPS, 4) + tile, F32),
                pltpu.VMEM((SWEEPS,) + tile, F32), pltpu.VMEM((SWEEPS,) + tile, F32), pltpu.VMEM((SWEEPS,) + tile, F32),
                pltpu.VMEM((SWEEPS, 128, 128), F32),
                dma((18,)), dma((18,)), dma((SWEEPS, 18)), dma((SWEEPS, 18)),
                dma((SWEEPS, 2)), dma((SWEEPS, 2)), dma((SWEEPS,)), dma((SWEEPS,)), dma((SWEEPS,)), dma((SWEEPS,)),
            ],
            compiler_params=pltpu.CompilerParams(
                collective_id=0, has_side_effects=True, vmem_limit_bytes=56 * 1024 * 1024
            ),
        )(adjoint_source, velocity, damping, face_rounds, jnp.transpose(aggregates, (0, 2, 1)))

    placed = (
        P(None, "gx", "gy", "gz"),
        P("gx", "gy", "gz"),
        P("gx", "gy", "gz"),
        P("gx", "gy", "gz", None),
        P("gx", "gy", "gz"),
    )
    return jax.shard_map(
        step, mesh=mesh, in_specs=placed, out_specs=P(None, "gx", "gy", "gz"), check_vma=False
    )
```

```python
import functools

import jax
import jax.numpy as jnp
from jax import lax
from jax.experimental import pallas as pl
from jax.experimental.pallas import tpu as pltpu
from jax.sharding import PartitionSpec as P

MESH = pl.DeviceIdType.MESH
F32 = jnp.float32
BF16 = jnp.bfloat16

CX, CY, CZ = 8, 32, 128
PY = 48
TILES = CY // 8
SWEEPS = 3
SMOOTH = 4
GAMMA_RE = 0.6
GAMMA_IM = 0.25
RELAX = 0.8
OMEGA_SQ = 9.0

OFFSETS = [(ox, oy) for ox in (-1, 0, 1) for oy in (-1, 0, 1)]
OFFSETS.sort(key=lambda o: -abs(o[0]) - abs(o[1]))


def slot_of(ox, oy):
    return (ox + 1) * 3 + (oy + 1)


def corner_of(ox, oy):
    return (1 if ox > 0 else 0) * 2 + (1 if oy > 0 else 0)


def iota(dim, shape=(8, 128)):
    return lax.broadcasted_iota(jnp.int32, shape, dim)


def roll(v, lanes, subs=0):
    if isinstance(lanes, int):
        lanes = lanes % 128
    if not isinstance(lanes, int) or lanes:
        v = pltpu.roll(v, lanes, 1)
    if subs % 8:
        v = pltpu.roll(v, subs % 8, 0)
    return v


def blend(a, b, mask):
    d_re = b[0] - a[0]
    d_im = b[1] - a[1]
    t_re = GAMMA_RE * d_re - GAMMA_IM * d_im
    t_im = GAMMA_RE * d_im + GAMMA_IM * d_re
    if mask is not None:
        t_re = jnp.where(mask, t_re, 0.0)
        t_im = jnp.where(mask, t_im, 0.0)
    return (a[0] + t_re, a[1] + t_im), (b[0] - t_re, b[1] - t_im)


def kernel(
    nx, ny,
    src_in, vel_in, dmp_in, rounds, aggs, out,
    src, vel, dmp, in_sem,
    kap, kdm, mre, mim, res, ping, pong, cor, fld, fz,
    coltile, edgecol, onehot, ksum, cval, zmask, coa, coz, own_k,
    info_send, info_recv, stage, corners, rz, ry, rd, row_send, pair_recv, chip_send, gath,
    info_ss, info_rs, h_ss, h_rs, x_ss, x_rs, pair_ss, pair_rs, ga_ss, ga_rs,
):
    ix, iy, iz = lax.axis_index("gx"), lax.axis_index("gy"), lax.axis_index("gz")
    lane, sub = iota(1), iota(0)
    lx, lt = lane % 8, (lane // 8) % TILES
    zf = jnp.where(iz == 0, 127, 0).astype(jnp.int32)
    at_face = lane == zf
    first_lane, last_lane = lane == 0, lane == 127
    lane32 = iota(1, (32, 128))
    first32, last32 = lane32 == 0, lane32 == 127

    has_x = {-1: ix > 0, 1: ix < nx - 1}
    has_y = {-1: iy > 0, 1: iy < ny - 1}

    def exists(ox, oy):
        if ox and oy:
            return jnp.logical_and(has_x[ox], has_y[oy])
        if ox:
            return has_x[ox]
        if oy:
            return has_y[oy]
        return None

    def guarded(cond, fn):
        if cond is None:
            fn()
        else:
            pl.when(cond)(fn)

    def device(ox, oy, oz):
        return (ix + ox, iy + oy, (1 - iz) if oz else iz)

    core = lax.rem(iy, 2)
    at_x, at_y, at_z = lax.rem(ix, 4), ix // 4, iz * (ny // 2) + iy // 2
    nz = ny
    pair = (ix, iy + 1 - 2 * core, iz)
    across = sorted(((dx, dy) for dx in range(4) for dy in range(4)), key=lambda d: -min(d[0], 4 - d[0]) - min(d[1], 4 - d[1]))
    across_x = [lax.rem(at_y + dy, 4) * 4 + lax.rem(at_x + dx, 4) for dx, dy in across]

    def for_chips(fn):
        def layer(i, carry):
            step = (i + 1) // 2
            there = lax.rem(at_z + nz // 2 + jnp.where(lax.rem(i, 2) == 1, nz - step, step), nz)
            ty, tz = lax.rem(there, ny // 2) * 2 + core, there // (ny // 2)
            for j in range(16):
                fn(i * 16 + j, (across_x[j], ty, tz))
            return carry
        lax.fori_loop(0, nz - 1, layer, 0)
        for j in range(15):
            fn((nz - 1) * 16 + j, (across_x[j], iy, iz))

    loads = [pltpu.make_async_copy(whole, local, in_sem.at[i])
             for i, (whole, local) in enumerate(((vel_in, vel), (dmp_in, dmp), (src_in, src)))]
    for load in loads:
        load.start()

    zero = jnp.zeros((8, 128), F32)
    for k in range(SWEEPS):
        for p in range(2):
            for x in range(10):
                tiles = range(6) if x in (0, 9) else (0, 5)
                for t in tiles:
                    cor[k, p, pl.ds(x * PY + 8 * t, 8), :] = zero
        for s in range(2):
            for o in range(9):
                rz[k, s, o] = zero
        for o in range(2):
            for j in range(3):
                ry[k, o, j] = zero
        for o in range(4):
            rd[k, o] = zero
    for s in range(2):
        for o in range(9):
            info_recv[s, o] = zero - 1.0

    barrier = pltpu.get_barrier_semaphore()
    count = jnp.int32(16 * nz - 1 + 1)
    def tell_chip(slot, target):
        pl.semaphore_signal(barrier, inc=1, device_id=target, device_id_type=MESH)

    for_chips(tell_chip)
    tell_chip(0, pair)
    for ox, oy in OFFSETS:
        if oy:
            def tell(ox=ox, oy=oy):
                for oz in (1, 0):
                    pl.semaphore_signal(barrier, inc=1, device_id=device(ox, oy, oz), device_id_type=MESH)
            guarded(exists(ox, oy), tell)
            count = count + jnp.where(exists(ox, oy), 2, 0)


    for buf in (ping, pong):
        for p in range(2):
            for x in range(8):
                buf[p, pl.ds(x * PY, 8), :] = zero
                buf[p, pl.ds(x * PY + 40, 8), :] = zero
    for p in range(2):
        for x in range(10):
            for t in range(6):
                fld[p, pl.ds(x * PY + 8 * t, 8), :] = zero
        for role in range(4):
            fz[role, p] = zero

    for load in loads:
        load.wait()
    for x in range(CX):
        v = vel[x]
        kappa = OMEGA_SQ / (v * v)
        damp = kappa * dmp[x]
        d_re = 14.0 - kappa
        scale = RELAX / (d_re * d_re + damp * damp)
        kap[x] = 16.0 - kappa
        kdm[x] = damp
        mre[x] = d_re * scale
        mim[x] = -damp * scale

    def face(i, inside):
        return jnp.where(inside, rounds[0, 0, 0, i].astype(F32), -1.0)

    low_x, high_x = face(0, ix > 0), face(1, ix < nx - 1)
    low_y, high_y = face(2, iy > 0), face(3, iy < ny - 1)
    depth = jnp.where(iz == 0, rounds[0, 0, 0, 5].astype(F32), rounds[0, 0, 0, 4].astype(F32))
    ids = [[aggs[qx, 0, qy].astype(F32) for qy in range(TILES)] for qx in range(2)]
    info = jnp.where(lx == 0, low_x, jnp.where(lx == 7, high_x, -1.0))
    col_y = jnp.where((lt == 0) & (sub == 0), low_y, jnp.where((lt == TILES - 1) & (sub == 7), high_y, -1.0))
    info = jnp.where(lane >= 32, col_y, info)
    info = jnp.where(lane >= 64, depth, info)
    for qx in range(2):
        for qy in range(TILES):
            info = jnp.where((lane >= 96) & (lx // 4 == qx) & (lt == qy), ids[qx][qy], info)
    info_send[...] = info

    low_rows = sub < 4
    lane1 = iota(1, (1, 128))

    def row_of(sums, first):
        rows = [jnp.sum(sums[p][qx][t], axis=0, keepdims=True) for p in range(2) for qx in range(2) for t in range(TILES)]
        return lanes_of(jnp.sum(jnp.concatenate(rows, axis=0), axis=1, keepdims=True), first)

    def lanes_of(total, first):
        spread = jnp.where(iota(1, (16, 128)) == iota(0, (16, 128)) + first, jnp.broadcast_to(total, (16, 128)), 0.0)
        return jnp.sum(spread, axis=0, keepdims=True)

    def rows_of(v, t):
        return v[8 * t:8 * t + 8]

    sums = [[[zero] * TILES for _ in range(2)] for _ in range(2)]
    for x in range(CX):
        kappa, damp = 16.0 - kap[x], kdm[x]
        for t in range(TILES):
            sums[0][x // 4][t] = sums[0][x // 4][t] + rows_of(kappa, t)
            sums[1][x // 4][t] = sums[1][x // 4][t] + rows_of(damp, t)
    fixed_row = row_of(sums, 32 + 16 * core)
    for p in range(2):
        for qx in range(2):
            for t in range(TILES):
                total = jnp.sum(jnp.sum(sums[p][qx][t], axis=0, keepdims=True), axis=1, keepdims=True)
                own_k[pl.ds(8 * p + TILES * qx + t, 1), :] = jnp.broadcast_to(total, (1, 128))
    for qx in range(2):
        for t in range(TILES):
            fixed_row = fixed_row + jnp.where(lane1 == 64 + 8 * core + qx * TILES + t, ids[qx][t], 0.0)

    def assemble(tiles, default):
        def pick(parts):
            value = jnp.full((8, 128), default, F32)
            for mask, tile in parts:
                value = jnp.where(mask, tile, value)
            return value
        t0, t3 = (lt == 0) & (sub == 0), (lt == TILES - 1) & (sub == 7)
        x0, x7 = lx == 0, lx == 7
        across_x = pick([(x0, roll(tiles[(-1, 0)], -7)), (x7, roll(tiles[(1, 0)], 7))])
        across_y = pick([(t0, roll(tiles[(0, -1)], -24, 1)), (t3, roll(tiles[(0, 1)], 24, -1))])
        across_xy = pick([
            (x0 & t0, roll(tiles[(-1, -1)], -31, 1)),
            (x0 & t3, roll(tiles[(-1, 1)], 17, -1)),
            (x7 & t0, roll(tiles[(1, -1)], -17, 1)),
            (x7 & t3, roll(tiles[(1, 1)], 31, -1)),
        ])
        return [tiles[(0, 0)], across_x, across_y, across_xy]

    def smooth_z(v):
        return 2.0 * v + jnp.where(first32, 0.0, pltpu.roll(v, 1, 1)) + jnp.where(last32, 0.0, pltpu.roll(v, 127, 1))

    def residual_pass(field, zone, source):
        lefts = []
        for p in range(2):
            c0, px, py, pxy = (zone[role, p] for role in range(4))
            t0, t3 = (lt == 0) & (sub == 0), (lt == TILES - 1) & (sub == 7)

            def smooth_y(v, across):
                up = pltpu.roll(v, 1, 0)
                up = jnp.where(sub == 0, roll(up, 8), up)
                up = jnp.where(t0, across, up)
                down = pltpu.roll(v, 7, 0)
                down = jnp.where(sub == 7, roll(down, -8), down)
                down = jnp.where(t3, across, down)
                return up + 2.0 * v + down

            yc, yx = smooth_y(c0, py), smooth_y(px, pxy)
            w = 2.0 * yc + jnp.where(lx == 0, yx, roll(yc, 1)) + jnp.where(lx == 7, yx, roll(yc, -1))
            lefts.append(pltpu.roll(w, zf, 1))
        sums = [[[zero] * TILES for _ in range(2)] for _ in range(2)]
        ys = [[None] * 10 for _ in range(2)]

        def y_smoothed(p, x):
            if ys[p][x] is None:
                base = x * PY
                ys[p][x] = (field[p, pl.ds(base + 7, 32), :] + field[p, pl.ds(base + 9, 32), :]
                            + 2.0 * field[p, pl.ds(base + 8, 32), :])
            return ys[p][x]

        for x in range(CX):
            smoothed = []
            for p in range(2):
                v = y_smoothed(p, x) + 2.0 * y_smoothed(p, x + 1) + y_smoothed(p, x + 2)
                halo = jnp.concatenate([roll(lefts[p], -(8 * t + x)) for t in range(TILES)], axis=0)
                smoothed.append(smooth_z(v) + jnp.where(lane32 == zf, halo, 0.0))
            f_re = field[0, pl.ds((x + 1) * PY + 8, 32), :]
            f_im = field[1, pl.ds((x + 1) * PY + 8, 32), :]
            a, b = kap[x], kdm[x]
            r_re = source[0, x] + 0.25 * smoothed[0] - a * f_re + b * f_im
            r_im = source[1, x] + 0.25 * smoothed[1] - a * f_im - b * f_re
            res[0, x] = r_re
            res[1, x] = r_im
            for t in range(TILES):
                sums[0][x // 4][t] = sums[0][x // 4][t] + rows_of(r_re, t)
                sums[1][x // 4][t] = sums[1][x // 4][t] + rows_of(r_im, t)
        return sums

    def first_pass():
        sums = [[[zero] * TILES for _ in range(2)] for _ in range(2)]
        for x in range(CX):
            for p in range(2):
                v = src[p, x]
                res[p, x] = v
                for t in range(TILES):
                    sums[p][x // 4][t] = sums[p][x // 4][t] + rows_of(v, t)
        return sums

    def jacobi(k):
        for x in range(CX):
            a, b = mre[x], mim[x]
            r_re, r_im = res[0, x], res[1, x]
            ping[0, pl.ds(x * PY + 8, 32), :] = a * r_re - b * r_im
            ping[1, pl.ds(x * PY + 8, 32), :] = a * r_im + b * r_re
        buffers = [ping, pong]
        for step in range(1, SMOOTH):
            now, later = buffers[(step - 1) % 2], buffers[step % 2]
            last = step == SMOOTH - 1
            ys = [[None] * CX for _ in range(2)]

            def y_smoothed(p, x):
                if x < 0 or x >= CX:
                    return None
                if ys[p][x] is None:
                    base = x * PY
                    ys[p][x] = (now[p, pl.ds(base + 7, 32), :] + now[p, pl.ds(base + 9, 32), :]
                                + 2.0 * now[p, pl.ds(base + 8, 32), :])
                return ys[p][x]

            for x in range(CX):
                misfit, old = [], []
                for p in range(2):
                    v = 2.0 * y_smoothed(p, x)
                    for near in (y_smoothed(p, x - 1), y_smoothed(p, x + 1)):
                        if near is not None:
                            v = v + near
                    c = now[p, pl.ds(x * PY + 8, 32), :]
                    old.append(c)
                    misfit.append(res[p, x] + 0.25 * smooth_z(v) - 2.0 * c)
                a, b = mre[x], mim[x]
                new_re = 0.2 * old[0] + (a * misfit[0] - b * misfit[1])
                new_im = 0.2 * old[1] + (a * misfit[1] + b * misfit[0])
                if last:
                    cor[k, 0, pl.ds((x + 1) * PY + 8, 32), :] = new_re
                    cor[k, 1, pl.ds((x + 1) * PY + 8, 32), :] = new_im
                else:
                    later[0, pl.ds(x * PY + 8, 32), :] = new_re
                    later[1, pl.ds(x * PY + 8, 32), :] = new_im

    def remote(src_ref, dst_ref, ssem, rsem, target):
        return pltpu.make_async_remote_copy(
            src_ref=src_ref, dst_ref=dst_ref, send_sem=ssem, recv_sem=rsem,
            device_id=target, device_id_type=MESH)

    def halo_copies(k, ox, oy, oz, incoming):
        mine, theirs = oz * 9 + slot_of(ox, oy), oz * 9 + slot_of(-ox, -oy)
        target = device(ox, oy, oz)
        if oz == 0 and ox and oy:
            part = corners.at[k, corner_of(ox, oy), pl.ds(0, 3)]
            there, at_home = rd.at[k, corner_of(-ox, -oy), pl.ds(0, 3)], rd.at[k, corner_of(ox, oy), pl.ds(0, 3)]
        elif oz == 0 and oy:
            part = stage.at[k, pl.ds(0, 3)] if oy < 0 else stage.at[k, pl.ds(2, 3)]
            there, at_home = ry.at[k, 1 if oy < 0 else 0], ry.at[k, 0 if oy < 0 else 1]
        elif oy:
            leaving, coming = (pl.ds(0, 1), pl.ds(7, 1)) if oy < 0 else (pl.ds(7, 1), pl.ds(0, 1))
            part = stage.at[k, 2, leaving]
            there, at_home = rz.at[k, 1, slot_of(-ox, -oy), leaving], rz.at[k, 1, slot_of(ox, oy), coming]
        else:
            half = pl.ds(0, 4)
            part = stage.at[k, 5, half]
            there, at_home = rz.at[k, oz, slot_of(-ox, -oy), half], rz.at[k, oz, slot_of(ox, oy), half]
        if incoming:
            return remote(part, at_home, h_ss.at[k, mine], h_rs.at[k, mine], target)
        return remote(part, there, h_ss.at[k, mine], h_rs.at[k, theirs], target)

    def plane_copies(k, ox, incoming):
        own, halo = (1, 9) if ox < 0 else (8, 0)
        part = cor.at[k, :, pl.ds(own * PY + 8, 32), :]
        there = cor.at[k, :, pl.ds(halo * PY + 8, 32), :]
        at_home = cor.at[k, :, pl.ds((0 if ox < 0 else 9) * PY + 8, 32), :]
        mine, theirs = (0, 1) if ox < 0 else (1, 0)
        if incoming:
            return remote(part, at_home, x_ss.at[k, mine], x_rs.at[k, mine], device(ox, 0, 0))
        return remote(part, there, x_ss.at[k, mine], x_rs.at[k, theirs], device(ox, 0, 0))

    def for_offsets(fn):
        for ox, oy in OFFSETS:
            guarded(exists(ox, oy), functools.partial(fn, ox, oy))

    def far_halo(k, fn, incoming=False):
        for_offsets(lambda ox, oy: fn(halo_copies(k, ox, oy, 1, incoming)))

    def near_halo(k, fn, incoming=False, planes=True):
        def each(ox, oy):
            if (ox, oy) == (0, 0):
                return
            if planes and oy == 0:
                fn(plane_copies(k, ox, incoming))
            fn(halo_copies(k, ox, oy, 0, incoming))
        for_offsets(each)

    def all_halo(k, fn, incoming=False, planes=True):
        def each(ox, oy):
            fn(halo_copies(k, ox, oy, 1, incoming))
            if (ox, oy) != (0, 0):
                fn(halo_copies(k, ox, oy, 0, incoming))
                if planes and oy == 0:
                    fn(plane_copies(k, ox, incoming))
        for_offsets(each)

    def for_planes(k, fn):
        for ox in (-1, 1):
            guarded(exists(ox, 0), functools.partial(lambda ox: fn(plane_copies(k, ox, False)), ox))

    def info_copies(ox, oy, oz, incoming):
        mine, theirs = oz * 9 + slot_of(ox, oy), oz * 9 + slot_of(-ox, -oy)
        target = device(ox, oy, oz)
        leaving = coming = pl.ds(0, 8)
        if oy:
            leaving, coming = (pl.ds(0, 1), pl.ds(7, 1)) if oy < 0 else (pl.ds(7, 1), pl.ds(0, 1))
        part = info_send.at[leaving]
        if incoming:
            return remote(part, info_recv.at[oz, slot_of(ox, oy), coming], info_ss.at[mine], info_rs.at[mine], target)
        return remote(part, info_recv.at[oz, slot_of(-ox, -oy), leaving], info_ss.at[mine], info_rs.at[theirs], target)

    def for_info(fn, incoming=False):
        def each(ox, oy):
            fn(info_copies(ox, oy, 1, incoming))
            if (ox, oy) != (0, 0):
                fn(info_copies(ox, oy, 0, incoming))
        for_offsets(each)

    def pack_halo(k):
        packed = zero
        for p in range(2):
            for x in range(CX):
                for t in range(TILES):
                    v = cor[k, p, pl.ds((x + 1) * PY + 8 + 8 * t, 8), :]
                    to = p * 32 + t * 8 + x
                    packed = jnp.where(lane == to, pltpu.roll(v, jnp.where(iz == 0, to + 1, to), 1), packed)
        stage[k, 2] = packed
        stage[k, 5] = jnp.where(lane < 64, packed, roll(packed, 64, 4))
        for p in range(2):
            stage[k, p] = cor[k, p, pl.ds(PY + 8, 8, stride=PY), :]
            stage[k, 3 + p] = cor[k, p, pl.ds(PY + 39, 8, stride=PY), :]
        for c in range(4):
            x, y, row = (1, 8)[c // 2], (8, 39)[c % 2], (0, 7)[c % 2]
            for p in range(2):
                corners[k, c, pl.ds(p, 1), :] = cor[k, p, pl.ds(x * PY + y, 1), :]
            corners[k, c, pl.ds(2, 1), :] = packed[row:row + 1]

    first_row = pl.ds(0, 1)
    others = pl.ds(0, 16 * nz - 1)

    def pair_copy(k):
        return remote(row_send.at[k, first_row], pair_recv.at[k, first_row], pair_ss.at[k], pair_rs.at[k], pair)

    def gather_start(k):
        chip = row_send[k, first_row] + pair_recv[k, first_row]
        chip_send[k, first_row] = chip
        gath[k, pl.ds(16 * nz - 1, 1)] = chip
        for_chips(lambda slot, target: remote(
            chip_send.at[k, first_row], gath.at[k, pl.ds(slot, 1)], ga_ss.at[k], ga_rs.at[k], target).start())

    def gather_every(k):
        return remote(gath.at[k, others], gath.at[k, others], ga_ss.at[k], ga_rs.at[k], pair)

    lane_n = iota(1, (128, 128))

    def by_aggregate(values):
        whole = jnp.where(lane_n < 32, values, 0.0)
        high = whole.astype(BF16).astype(F32)
        rest = whole - high
        middle = rest.astype(BF16).astype(F32)
        split = high + pltpu.roll(middle, 32, 1) + pltpu.roll(rest - middle, 64, 1)
        found = jnp.dot(onehot[...], split.astype(BF16), preferred_element_type=F32)
        lane64 = iota(1, (64, 128))
        total = jnp.zeros((64, 128), F32)
        for b in range(16):
            mine = (lane64 % 8 == b % 8) & ((lane64 // 16) % 2 == b // 8)
            total = jnp.where(mine, found[64 * b:64 * b + 64], total)
        total = jnp.where(lane64 < 96, total, 0.0)
        real = (lane64 // 8) % 2 == 0
        return (jnp.sum(jnp.where(real, total, 0.0), axis=1, keepdims=True),
                jnp.sum(jnp.where(real, 0.0, total), axis=1, keepdims=True))

    row64 = iota(0, (64, 128))

    def place_of(row):
        return row // 24, (row % 24) // 6, row % 6

    def setup_rounds():
        found = jnp.full((64, 128), -1.0, F32)
        for s in range(2):
            tiles = {o: info_recv[s, slot_of(*o)] for o in OFFSETS}
            if s == 0:
                tiles[(0, 0)] = info_send[...]
            roles = assemble(tiles, -1.0)
            coltile[4 * s + 0] = roles[0]
            coltile[4 * s + 1] = roles[2]
            coltile[4 * s + 2] = roll(roles[0], -32)
            coltile[4 * s + 3] = roll(roles[1], -32)
            if s == 0:
                for role in range(4):
                    coltile[8 + role] = roll(roles[role], -64)
                corner = [jnp.full((4, 128), -1.0, F32) for _ in range(4)]
                row4 = iota(0, (4, 128))
                for j, tile in enumerate((roles[0], roles[2], roll(roles[0], -32), roll(roles[1], -32))):
                    for c in range(4):
                        sx, sy = c // 2, c % 2
                        spot = (lane == (3 * sy) * 8 + 7 * sx) & (sub == 7 * sy)
                        value = jnp.max(jnp.max(jnp.where(spot, tile, -1.0), axis=1, keepdims=True), axis=0, keepdims=True)
                        corner[j] = jnp.where(row4 == c, value, corner[j])
                    edgecol[j] = corner[j]
            lane64 = iota(1, (64, 128))
            side, at_qx, at_qy = place_of(row64)
            role_at = jnp.where((at_qx == 0) | (at_qx == 3), 1, 0) + jnp.where((at_qy == 0) | (at_qy == 5), 2, 0)
            x_at = jnp.where(at_qx == 2, 4, jnp.where(at_qx == 3, 7, 0))
            spot = 96 + 8 * jnp.clip(at_qy - 1, 0, TILES - 1) + x_at
            for role in range(4):
                spread = jnp.broadcast_to(jnp.max(roles[role], axis=0, keepdims=True), (64, 128))
                found = jnp.where((side == s) & (role_at == role) & (lane64 == spot), spread, found)
        wanted = jnp.broadcast_to(jnp.max(found, axis=1, keepdims=True), (64, 128))
        cval[0] = wanted
        row24 = iota(0, (24, 128))
        lane24 = iota(1, (24, 128))
        x24, t24 = lane24 % 8, (lane24 // 8) % TILES
        for role in range(4):
            if role % 2:
                want_x = jnp.where(x24 == 0, 0, jnp.where(x24 == 7, 3, -1))
            else:
                want_x = 1 + x24 // 4
            if role // 2:
                want_y = jnp.where(t24 == 0, 0, jnp.where(t24 == TILES - 1, 5, -1))
            else:
                want_y = 1 + t24
            zmask[role] = jnp.where((row24 // 6 == want_x) & (row24 % 6 == want_y), 1.0, 0.0)

    def setup_aggregates():
        wanted = cval[0]
        cells = jnp.transpose(gath[0])
        for b in range(16):
            row = jnp.broadcast_to(cells[64 + b:65 + b], (64, 128))
            onehot[pl.ds(64 * b, 64), :] = jnp.where(wanted == row, 1.0, 0.0).astype(BF16)
        for p, total in enumerate(by_aggregate(pltpu.roll(gath[0], 96, 1))):
            ksum[p] = jnp.broadcast_to(total, (64, 128))

    def coarse_values(k):
        r_re, r_im = by_aggregate(gath[k])
        k_re, k_im = ksum[0], ksum[1]
        norm = k_re * k_re + k_im * k_im
        norm = jnp.where(norm > 0.0, norm, 1.0)
        cval[0] = (r_im * k_im - r_re * k_re) / norm
        cval[1] = (-r_re * k_im - r_im * k_re) / norm

    def sides_rounds(k):
        cells = []
        for s in range(2):
            tiles = {}
            for ox, oy in OFFSETS:
                if s == 0 and ox == 0 and oy == 0:
                    tiles[(ox, oy)] = stage[k, 2]
                elif s == 0 and ox and oy:
                    tiles[(ox, oy)] = jnp.broadcast_to(rd[k, corner_of(ox, oy), pl.ds(2, 1), :], (8, 128))
                elif s == 0 and oy:
                    tiles[(ox, oy)] = ry[k, 0, 0] if oy < 0 else ry[k, 1, 2]
                elif oy:
                    tiles[(ox, oy)] = rz[k, s, slot_of(ox, oy)]
                else:
                    folded = rz[k, s, slot_of(ox, oy)]
                    tiles[(ox, oy)] = jnp.where(sub < 4, folded, roll(folded, 64, 4))
            roles = assemble(tiles, 0.0)
            cells.append([(role, roll(role, -32)) for role in roles])
        for r in range(6):
            now = float(r)
            for s in range(2):
                c = cells[s]
                c[0], c[1] = blend(c[0], c[1], coltile[4 * s + 0] == now)
                c[2], c[3] = blend(c[2], c[3], coltile[4 * s + 1] == now)
                c[0], c[2] = blend(c[0], c[2], coltile[4 * s + 2] == now)
                c[1], c[3] = blend(c[1], c[3], coltile[4 * s + 3] == now)
            for role in range(4):
                cells[0][role], cells[1][role] = blend(cells[0][role], cells[1][role], coltile[8 + role] == now)
        return cells

    def main_rounds(k):
        def lines(planes, rows):
            return tuple(
                jnp.concatenate([cor[k, p, pl.ds(x * PY + y, 1), :] for x in planes for y in rows], axis=0) for p in range(2))

        c0 = lines((1, 8), (8, 39))
        px = lines((0, 9), (8, 39))
        halo_rows = []
        for p in range(2):
            parts = []
            for x_at in (0, 7):
                parts += [ry[k, 0, 1 + p, pl.ds(x_at, 1), :], ry[k, 1, p, pl.ds(x_at, 1), :]]
            halo_rows.append(jnp.concatenate(parts, axis=0))
        py = tuple(halo_rows)
        diagonal = []
        for p in range(2):
            parts = []
            for c in range(4):
                parts.append(rd[k, c, pl.ds(p, 1), :])
            diagonal.append(jnp.concatenate(parts, axis=0))
        pxy = tuple(diagonal)
        for r in range(6):
            now = float(r)
            c0, px = blend(c0, px, edgecol[0] == now)
            py, pxy = blend(py, pxy, edgecol[1] == now)
            c0, py = blend(c0, py, edgecol[2] == now)
            px, pxy = blend(px, pxy, edgecol[3] == now)
        for own, halo, ox in ((1, 0, -1), (8, 9, 1)):
            a = tuple(cor[k, p, pl.ds(own * PY + 8, 32), :] for p in range(2))
            b = tuple(cor[k, p, pl.ds(halo * PY + 8, 32), :] for p in range(2))
            a, b = blend(a, b, jnp.broadcast_to(has_x[ox], (32, 128)))
            for p in range(2):
                cor[k, p, pl.ds(own * PY + 8, 32), :] = a[p]
                cor[k, p, pl.ds(halo * PY + 8, 32), :] = b[p]
        for own, halo, oy in ((8, 7, -1), (39, 40, 1)):
            a = tuple(stage[k, p if oy < 0 else 3 + p] for p in range(2))
            b = tuple(ry[k, 0, 1 + p] if oy < 0 else ry[k, 1, p] for p in range(2))
            a, b = blend(a, b, jnp.broadcast_to(has_y[oy], (8, 128)))
            for p in range(2):
                cor[k, p, pl.ds(PY + own, 8, stride=PY), :] = a[p]
                cor[k, p, pl.ds(PY + halo, 8, stride=PY), :] = b[p]
        for c in range(4):
            sx, sy = c // 2, c % 2
            own_x, halo_x = (1, 8)[sx], (0, 9)[sx]
            own_y, halo_y = (8, 39)[sy], (7, 40)[sy]
            for p in range(2):
                cor[k, p, pl.ds(own_x * PY + own_y, 1), :] = c0[p][c:c + 1]
                cor[k, p, pl.ds(halo_x * PY + own_y, 1), :] = px[p][c:c + 1]
                cor[k, p, pl.ds(own_x * PY + halo_y, 1), :] = py[p][c:c + 1]
                cor[k, p, pl.ds(halo_x * PY + halo_y, 1), :] = pxy[p][c:c + 1]

    def add_correction(k, cells):
        last = k == SWEEPS - 1
        for p in range(2):
            turned = [pltpu.roll(cells[0][role][p], zf, 1) for role in range(4)]
            for x in range(10):
                if last and x in (0, 9):
                    continue
                role = 1 if x in (0, 9) else 0
                near = min(max(x - 1, 0), 7)
                for t in range(TILES):
                    column = roll(turned[role], -(8 * t + near))
                    rows = pl.ds(x * PY + 8 + 8 * t, 8)
                    fld[p, rows, :] = fld[p, rows, :] + jnp.where(at_face, column, cor[k, p, rows, :])
                if last:
                    continue
                for t, at, y in ((0, 0, 7), (TILES - 1, 7, 40)):
                    column = roll(turned[2 + role], -(8 * t + near))[at:at + 1]
                    place = pl.ds(x * PY + y, 1)
                    fld[p, place, :] = fld[p, place, :] + jnp.where(at_face[0:1], column, cor[k, p, place, :])
            if not last:
                for role in range(4):
                    fz[role, p] = fz[role, p] + cells[1][role][p]

    def term(p, role, t, x, height=8):
        at_qx = (0 if x == 0 else 3) if role % 2 else 1 + x // 4
        at_qy = (0 if t == 0 else 5) if role // 2 else 1 + t
        return jnp.broadcast_to(cval[p, pl.ds(at_qx * 6 + at_qy, 1), :], (height, 128))

    def add_coarse(last):
        for p in range(2):
            for x in range(10):
                if last and x in (0, 9):
                    continue
                role = 1 if x in (0, 9) else 0
                near = min(max(x - 1, 0), 7)
                for t in range(TILES):
                    value = term(p, role, t, near)
                    rows = pl.ds(x * PY + 8 + 8 * t, 8)
                    if last:
                        out[p, x - 1, pl.ds(8 * t, 8), :] = fld[p, rows, :] + value
                    else:
                        coa[p, rows, :] = value
                        fld[p, rows, :] = fld[p, rows, :] + value
                if last:
                    continue
                for t, y in ((0, 7), (TILES - 1, 40)):
                    place = pl.ds(x * PY + y, 1)
                    value = term(p, 2 + role, t, near, 1)
                    coa[p, place, :] = value
                    fld[p, place, :] = fld[p, place, :] + value
            if not last:
                other = cval[p, pl.ds(24, 24), :]
                for role in range(4):
                    halo = jnp.broadcast_to(jnp.sum(other * zmask[role], axis=0, keepdims=True), (8, 128))
                    coz[role, p] = halo
                    fz[role, p] = fz[role, p] + halo

    def coarse_row():
        values, smooth = [], []
        for p in range(2):
            c = cval[p]
            v = (2.0 * CZ - 1.0) * c[0:24] + 0.5 * c[24:48]
            for at in (1, 2):
                u = 7.0 * v[6 * at:6 * at + 6] + 0.5 * (v[6 * at - 6:6 * at] + v[6 * at + 6:6 * at + 12])
                smooth.append(15.0 * u[1:5] + 0.5 * (u[0:4] + u[2:6]))
                values.append(c[6 * at + 1:6 * at + 5])
        c_re, c_im = jnp.concatenate(values[0:2], axis=0), jnp.concatenate(values[2:4], axis=0)
        s_re, s_im = jnp.concatenate(smooth[0:2], axis=0), jnp.concatenate(smooth[2:4], axis=0)
        a, b = 16.0 * (4 * 8 * CZ) - own_k[0:8], own_k[8:16]
        total = jnp.concatenate([a * c_re - b * c_im - 2.0 * s_re, a * c_im + b * c_re - 2.0 * s_im], axis=0)
        return lanes_of(total, 16 * core)

    for k in range(SWEEPS):
        if k == 0:
            row_send[k, first_row] = row_of(first_pass(), 16 * core) + fixed_row
        else:
            row_send[k, first_row] = row - coarse_row()
        if k == 0:
            jacobi(k)
            pack_halo(k)
            pl.semaphore_wait(barrier, count)
            pair_copy(k).start()
            for_info(lambda copy: copy.start())
        else:
            pair_copy(k).start()
            add_coarse(False)
            residual_pass(coa, coz, res)
            jacobi(k)
            for_planes(k, lambda copy: copy.start())
            pack_halo(k)
        far_halo(k, lambda copy: copy.start())
        near_halo(k, lambda copy: copy.start(), planes=k == 0)
        pair_copy(k).wait_recv()
        gather_start(k)
        if k == 0:
            for_info(lambda copy: copy.wait_recv(), True)
            setup_rounds()
        pair_copy(k).wait_send()
        all_halo(k, lambda copy: copy.wait_send())
        if k == 0:
            for_info(lambda copy: copy.wait_send())
        all_halo(k, lambda copy: copy.wait_recv(), True)
        cells = sides_rounds(k)
        main_rounds(k)
        add_correction(k, cells)
        if k < SWEEPS - 1:
            row = row_of(residual_pass(fld, fz, src), 16 * core)
        gather_every(k).wait_recv()
        if k == 0:
            setup_aggregates()
        coarse_values(k)
        if k == SWEEPS - 1:
            add_coarse(True)
        gather_every(k).wait_send()


def solution(mesh):
    nx, ny = mesh.shape["gx"], mesh.shape["gy"]

    def step(adjoint_source, velocity, damping, face_rounds, aggregates):
        vmem = pl.BlockSpec(memory_space=pltpu.VMEM)
        hbm = pl.BlockSpec(memory_space=pltpu.MemorySpace.HBM)
        smem = pl.BlockSpec(memory_space=pltpu.SMEM)
        dma = pltpu.SemaphoreType.DMA
        tile = (8, 128)
        block = (CX, CY, CZ)
        return pl.pallas_call(
            functools.partial(kernel, nx, ny),
            out_shape=pltpu.VMEM((2,) + block, F32),
            in_specs=[hbm, hbm, hbm, smem, smem],
            out_specs=vmem,
            scratch_shapes=[
                pltpu.VMEM((2,) + block, F32), pltpu.VMEM(block, F32), pltpu.VMEM(block, F32), dma((3,)),
                pltpu.VMEM(block, F32), pltpu.VMEM(block, F32), pltpu.VMEM(block, F32), pltpu.VMEM(block, F32),
                pltpu.VMEM((2,) + block, F32),
                pltpu.VMEM((2, CX * PY, CZ), F32), pltpu.VMEM((2, CX * PY, CZ), F32),
                pltpu.VMEM((SWEEPS, 2, 10 * PY, CZ), F32),
                pltpu.VMEM((2, 10 * PY, CZ), F32),
                pltpu.VMEM((4, 2) + tile, F32),
                pltpu.VMEM((12,) + tile, F32), pltpu.VMEM((4, 4, 128), F32),
                pltpu.VMEM((1024, 128), BF16), pltpu.VMEM((2, 64, 128), F32), pltpu.VMEM((2, 64, 128), F32),
                pltpu.VMEM((4, 24, 128), F32), pltpu.VMEM((2, 10 * PY, CZ), F32), pltpu.VMEM((4, 2) + tile, F32),
                pltpu.VMEM((16, 128), F32),
                pltpu.VMEM(tile, F32), pltpu.VMEM((2, 9) + tile, F32),
                pltpu.VMEM((SWEEPS, 6) + tile, F32), pltpu.VMEM((SWEEPS, 4) + tile, F32), pltpu.VMEM((SWEEPS, 2, 9) + tile, F32),
                pltpu.VMEM((SWEEPS, 2, 3) + tile, F32), pltpu.VMEM((SWEEPS, 4) + tile, F32),
                pltpu.VMEM((SWEEPS,) + tile, F32), pltpu.VMEM((SWEEPS,) + tile, F32), pltpu.VMEM((SWEEPS,) + tile, F32),
                pltpu.VMEM((SWEEPS, 128, 128), F32),
                dma((18,)), dma((18,)), dma((SWEEPS, 18)), dma((SWEEPS, 18)),
                dma((SWEEPS, 2)), dma((SWEEPS, 2)), dma((SWEEPS,)), dma((SWEEPS,)), dma((SWEEPS,)), dma((SWEEPS,)),
            ],
            compiler_params=pltpu.CompilerParams(
                collective_id=0, has_side_effects=True, vmem_limit_bytes=56 * 1024 * 1024
            ),
        )(adjoint_source, velocity, damping, face_rounds, jnp.transpose(aggregates, (0, 2, 1)))

    placed = (
        P(None, "gx", "gy", "gz"),
        P("gx", "gy", "gz"),
        P("gx", "gy", "gz"),
        P("gx", "gy", "gz", None),
        P("gx", "gy", "gz"),
    )
    return jax.shard_map(
        step, mesh=mesh, in_specs=placed, out_specs=P(None, "gx", "gy", "gz"), check_vma=False
    )
```

```python
import functools

import jax
import jax.numpy as jnp
from jax import lax
from jax.experimental import pallas as pl
from jax.experimental.pallas import tpu as pltpu
from jax.sharding import PartitionSpec as P

MESH = pl.DeviceIdType.MESH
F32 = jnp.float32
BF16 = jnp.bfloat16

CX, CY, CZ = 8, 32, 128
PY = 48
TILES = CY // 8
SWEEPS = 3
SMOOTH = 4
GAMMA_RE = 0.6
GAMMA_IM = 0.25
RELAX = 0.8
OMEGA_SQ = 9.0

OFFSETS = [(ox, oy) for ox in (-1, 0, 1) for oy in (-1, 0, 1)]
OFFSETS.sort(key=lambda o: -abs(o[0]) - abs(o[1]))


def slot_of(ox, oy):
    return (ox + 1) * 3 + (oy + 1)


def corner_of(ox, oy):
    return (1 if ox > 0 else 0) * 2 + (1 if oy > 0 else 0)


def iota(dim, shape=(8, 128)):
    return lax.broadcasted_iota(jnp.int32, shape, dim)


def roll(v, lanes, subs=0):
    if isinstance(lanes, int):
        lanes = lanes % 128
    if not isinstance(lanes, int) or lanes:
        v = pltpu.roll(v, lanes, 1)
    if subs % 8:
        v = pltpu.roll(v, subs % 8, 0)
    return v


def blend(a, b, mask):
    d_re = b[0] - a[0]
    d_im = b[1] - a[1]
    t_re = GAMMA_RE * d_re - GAMMA_IM * d_im
    t_im = GAMMA_RE * d_im + GAMMA_IM * d_re
    if mask is not None:
        t_re = jnp.where(mask, t_re, 0.0)
        t_im = jnp.where(mask, t_im, 0.0)
    return (a[0] + t_re, a[1] + t_im), (b[0] - t_re, b[1] - t_im)


def kernel(
    nx, ny,
    src_in, vel_in, dmp_in, rounds, aggs, out,
    src, vel, dmp, in_sem,
    kap, kdm, mre, mim, res, ping, pong, cor, fld, fz,
    coltile, edgecol, onehot, ksum, cval, zmask, coa, coz, own_k,
    info_send, info_recv, stage, corners, rz, ry, rd, row_send, pair_recv, chip_send, gath,
    info_ss, info_rs, h_ss, h_rs, x_ss, x_rs, pair_ss, pair_rs, ga_ss, ga_rs,
):
    ix, iy, iz = lax.axis_index("gx"), lax.axis_index("gy"), lax.axis_index("gz")
    lane, sub = iota(1), iota(0)
    lx, lt = lane % 8, (lane // 8) % TILES
    zf = jnp.where(iz == 0, 127, 0).astype(jnp.int32)
    at_face = lane == zf
    first_lane, last_lane = lane == 0, lane == 127
    lane32 = iota(1, (32, 128))
    first32, last32 = lane32 == 0, lane32 == 127

    has_x = {-1: ix > 0, 1: ix < nx - 1}
    has_y = {-1: iy > 0, 1: iy < ny - 1}

    def exists(ox, oy):
        if ox and oy:
            return jnp.logical_and(has_x[ox], has_y[oy])
        if ox:
            return has_x[ox]
        if oy:
            return has_y[oy]
        return None

    def guarded(cond, fn):
        if cond is None:
            fn()
        else:
            pl.when(cond)(fn)

    def device(ox, oy, oz):
        return (ix + ox, iy + oy, (1 - iz) if oz else iz)

    core = lax.rem(iy, 2)
    at_x, at_y, at_z = lax.rem(ix, 4), ix // 4, iz * (ny // 2) + iy // 2
    nz = ny
    pair = (ix, iy + 1 - 2 * core, iz)
    across = sorted(((dx, dy) for dx in range(4) for dy in range(4)), key=lambda d: -min(d[0], 4 - d[0]) - min(d[1], 4 - d[1]))
    across_x = [lax.rem(at_y + dy, 4) * 4 + lax.rem(at_x + dx, 4) for dx, dy in across]

    def for_chips(fn, first=0, last=nz - 1, rest=True):
        def layer(i, carry):
            step = (i + 1) // 2
            there = lax.rem(at_z + nz // 2 + jnp.where(lax.rem(i, 2) == 1, nz - step, step), nz)
            ty, tz = lax.rem(there, ny // 2) * 2 + core, there // (ny // 2)
            for j in range(16):
                fn(i * 16 + j, (across_x[j], ty, tz))
            return carry
        lax.fori_loop(first, last, layer, 0)
        for j in range(15 if rest else 0):
            fn((nz - 1) * 16 + j, (across_x[j], iy, iz))

    loads = [pltpu.make_async_copy(whole, local, in_sem.at[i])
             for i, (whole, local) in enumerate(((vel_in, vel), (dmp_in, dmp), (src_in, src)))]
    for load in loads:
        load.start()

    zero = jnp.zeros((8, 128), F32)
    for k in range(SWEEPS):
        for p in range(2):
            for x in range(10):
                tiles = range(6) if x in (0, 9) else (0, 5)
                for t in tiles:
                    cor[k, p, pl.ds(x * PY + 8 * t, 8), :] = zero
        for s in range(2):
            for o in range(9):
                rz[k, s, o] = zero
        for o in range(2):
            for j in range(3):
                ry[k, o, j] = zero
        for o in range(4):
            rd[k, o] = zero
    for s in range(2):
        for o in range(9):
            info_recv[s, o] = zero - 1.0

    barrier = pltpu.get_barrier_semaphore()
    count = jnp.int32(16 * nz - 1 + 1)
    def tell_chip(slot, target):
        pl.semaphore_signal(barrier, inc=1, device_id=target, device_id_type=MESH)

    for_chips(tell_chip)
    tell_chip(0, pair)
    for ox, oy in OFFSETS:
        if oy:
            def tell(ox=ox, oy=oy):
                for oz in (1, 0):
                    pl.semaphore_signal(barrier, inc=1, device_id=device(ox, oy, oz), device_id_type=MESH)
            guarded(exists(ox, oy), tell)
            count = count + jnp.where(exists(ox, oy), 2, 0)


    for buf in (ping, pong):
        for p in range(2):
            for x in range(8):
                buf[p, pl.ds(x * PY, 8), :] = zero
                buf[p, pl.ds(x * PY + 40, 8), :] = zero
    for p in range(2):
        for x in range(10):
            for t in range(6):
                fld[p, pl.ds(x * PY + 8 * t, 8), :] = zero
        for role in range(4):
            fz[role, p] = zero

    for load in loads:
        load.wait()
    for x in range(CX):
        v = vel[x]
        kappa = OMEGA_SQ / (v * v)
        damp = kappa * dmp[x]
        d_re = 14.0 - kappa
        scale = RELAX / (d_re * d_re + damp * damp)
        kap[x] = 16.0 - kappa
        kdm[x] = damp
        mre[x] = d_re * scale
        mim[x] = -damp * scale

    def face(i, inside):
        return jnp.where(inside, rounds[0, 0, 0, i].astype(F32), -1.0)

    low_x, high_x = face(0, ix > 0), face(1, ix < nx - 1)
    low_y, high_y = face(2, iy > 0), face(3, iy < ny - 1)
    depth = jnp.where(iz == 0, rounds[0, 0, 0, 5].astype(F32), rounds[0, 0, 0, 4].astype(F32))
    ids = [[aggs[qx, 0, qy].astype(F32) for qy in range(TILES)] for qx in range(2)]
    info = jnp.where(lx == 0, low_x, jnp.where(lx == 7, high_x, -1.0))
    col_y = jnp.where((lt == 0) & (sub == 0), low_y, jnp.where((lt == TILES - 1) & (sub == 7), high_y, -1.0))
    info = jnp.where(lane >= 32, col_y, info)
    info = jnp.where(lane >= 64, depth, info)
    for qx in range(2):
        for qy in range(TILES):
            info = jnp.where((lane >= 96) & (lx // 4 == qx) & (lt == qy), ids[qx][qy], info)
    info_send[...] = info

    low_rows = sub < 4
    lane1 = iota(1, (1, 128))

    def row_of(sums, first):
        rows = [jnp.sum(sums[p][qx][t], axis=0, keepdims=True) for p in range(2) for qx in range(2) for t in range(TILES)]
        return lanes_of(jnp.sum(jnp.concatenate(rows, axis=0), axis=1, keepdims=True), first)

    def lanes_of(total, first):
        spread = jnp.where(iota(1, (16, 128)) == iota(0, (16, 128)) + first, jnp.broadcast_to(total, (16, 128)), 0.0)
        return jnp.sum(spread, axis=0, keepdims=True)

    def rows_of(v, t):
        return v[8 * t:8 * t + 8]

    sums = [[[zero] * TILES for _ in range(2)] for _ in range(2)]
    for x in range(CX):
        kappa, damp = 16.0 - kap[x], kdm[x]
        for t in range(TILES):
            sums[0][x // 4][t] = sums[0][x // 4][t] + rows_of(kappa, t)
            sums[1][x // 4][t] = sums[1][x // 4][t] + rows_of(damp, t)
    fixed_row = row_of(sums, 32 + 16 * core)
    for p in range(2):
        for qx in range(2):
            for t in range(TILES):
                total = jnp.sum(jnp.sum(sums[p][qx][t], axis=0, keepdims=True), axis=1, keepdims=True)
                own_k[pl.ds(8 * p + TILES * qx + t, 1), :] = jnp.broadcast_to(total, (1, 128))
    for qx in range(2):
        for t in range(TILES):
            fixed_row = fixed_row + jnp.where(lane1 == 64 + 8 * core + qx * TILES + t, ids[qx][t], 0.0)

    def assemble(tiles, default):
        def pick(parts):
            value = jnp.full((8, 128), default, F32)
            for mask, tile in parts:
                value = jnp.where(mask, tile, value)
            return value
        t0, t3 = (lt == 0) & (sub == 0), (lt == TILES - 1) & (sub == 7)
        x0, x7 = lx == 0, lx == 7
        across_x = pick([(x0, roll(tiles[(-1, 0)], -7)), (x7, roll(tiles[(1, 0)], 7))])
        across_y = pick([(t0, roll(tiles[(0, -1)], -24, 1)), (t3, roll(tiles[(0, 1)], 24, -1))])
        across_xy = pick([
            (x0 & t0, roll(tiles[(-1, -1)], -31, 1)),
            (x0 & t3, roll(tiles[(-1, 1)], 17, -1)),
            (x7 & t0, roll(tiles[(1, -1)], -17, 1)),
            (x7 & t3, roll(tiles[(1, 1)], 31, -1)),
        ])
        return [tiles[(0, 0)], across_x, across_y, across_xy]

    def smooth_z(v):
        return 2.0 * v + jnp.where(first32, 0.0, pltpu.roll(v, 1, 1)) + jnp.where(last32, 0.0, pltpu.roll(v, 127, 1))

    def residual_pass(field, zone, source):
        lefts = []
        for p in range(2):
            c0, px, py, pxy = (zone[role, p] for role in range(4))
            t0, t3 = (lt == 0) & (sub == 0), (lt == TILES - 1) & (sub == 7)

            def smooth_y(v, across):
                up = pltpu.roll(v, 1, 0)
                up = jnp.where(sub == 0, roll(up, 8), up)
                up = jnp.where(t0, across, up)
                down = pltpu.roll(v, 7, 0)
                down = jnp.where(sub == 7, roll(down, -8), down)
                down = jnp.where(t3, across, down)
                return up + 2.0 * v + down

            yc, yx = smooth_y(c0, py), smooth_y(px, pxy)
            w = 2.0 * yc + jnp.where(lx == 0, yx, roll(yc, 1)) + jnp.where(lx == 7, yx, roll(yc, -1))
            lefts.append(pltpu.roll(w, zf, 1))
        sums = [[[zero] * TILES for _ in range(2)] for _ in range(2)]
        ys = [[None] * 10 for _ in range(2)]

        def y_smoothed(p, x):
            if ys[p][x] is None:
                base = x * PY
                ys[p][x] = (field[p, pl.ds(base + 7, 32), :] + field[p, pl.ds(base + 9, 32), :]
                            + 2.0 * field[p, pl.ds(base + 8, 32), :])
            return ys[p][x]

        for x in range(CX):
            smoothed = []
            for p in range(2):
                v = y_smoothed(p, x) + 2.0 * y_smoothed(p, x + 1) + y_smoothed(p, x + 2)
                halo = jnp.concatenate([roll(lefts[p], -(8 * t + x)) for t in range(TILES)], axis=0)
                smoothed.append(smooth_z(v) + jnp.where(lane32 == zf, halo, 0.0))
            f_re = field[0, pl.ds((x + 1) * PY + 8, 32), :]
            f_im = field[1, pl.ds((x + 1) * PY + 8, 32), :]
            a, b = kap[x], kdm[x]
            r_re = source[0, x] + 0.25 * smoothed[0] - a * f_re + b * f_im
            r_im = source[1, x] + 0.25 * smoothed[1] - a * f_im - b * f_re
            res[0, x] = r_re
            res[1, x] = r_im
            for t in range(TILES):
                sums[0][x // 4][t] = sums[0][x // 4][t] + rows_of(r_re, t)
                sums[1][x // 4][t] = sums[1][x // 4][t] + rows_of(r_im, t)
        return sums

    def first_pass():
        sums = [[[zero] * TILES for _ in range(2)] for _ in range(2)]
        for x in range(CX):
            for p in range(2):
                v = src[p, x]
                res[p, x] = v
                for t in range(TILES):
                    sums[p][x // 4][t] = sums[p][x // 4][t] + rows_of(v, t)
        return sums

    def jacobi(k):
        for x in range(CX):
            a, b = mre[x], mim[x]
            r_re, r_im = res[0, x], res[1, x]
            ping[0, pl.ds(x * PY + 8, 32), :] = a * r_re - b * r_im
            ping[1, pl.ds(x * PY + 8, 32), :] = a * r_im + b * r_re
        buffers = [ping, pong]
        for step in range(1, SMOOTH):
            now, later = buffers[(step - 1) % 2], buffers[step % 2]
            last = step == SMOOTH - 1
            ys = [[None] * CX for _ in range(2)]

            def y_smoothed(p, x):
                if x < 0 or x >= CX:
                    return None
                if ys[p][x] is None:
                    base = x * PY
                    ys[p][x] = (now[p, pl.ds(base + 7, 32), :] + now[p, pl.ds(base + 9, 32), :]
                                + 2.0 * now[p, pl.ds(base + 8, 32), :])
                return ys[p][x]

            for x in range(CX):
                misfit, old = [], []
                for p in range(2):
                    v = 2.0 * y_smoothed(p, x)
                    for near in (y_smoothed(p, x - 1), y_smoothed(p, x + 1)):
                        if near is not None:
                            v = v + near
                    c = now[p, pl.ds(x * PY + 8, 32), :]
                    old.append(c)
                    misfit.append(res[p, x] + 0.25 * smooth_z(v) - 2.0 * c)
                a, b = mre[x], mim[x]
                new_re = 0.2 * old[0] + (a * misfit[0] - b * misfit[1])
                new_im = 0.2 * old[1] + (a * misfit[1] + b * misfit[0])
                if last:
                    cor[k, 0, pl.ds((x + 1) * PY + 8, 32), :] = new_re
                    cor[k, 1, pl.ds((x + 1) * PY + 8, 32), :] = new_im
                else:
                    later[0, pl.ds(x * PY + 8, 32), :] = new_re
                    later[1, pl.ds(x * PY + 8, 32), :] = new_im

    def remote(src_ref, dst_ref, ssem, rsem, target):
        return pltpu.make_async_remote_copy(
            src_ref=src_ref, dst_ref=dst_ref, send_sem=ssem, recv_sem=rsem,
            device_id=target, device_id_type=MESH)

    def halo_copies(k, ox, oy, oz, incoming):
        mine, theirs = oz * 9 + slot_of(ox, oy), oz * 9 + slot_of(-ox, -oy)
        target = device(ox, oy, oz)
        if oz == 0 and ox and oy:
            part = corners.at[k, corner_of(ox, oy), pl.ds(0, 3)]
            there, at_home = rd.at[k, corner_of(-ox, -oy), pl.ds(0, 3)], rd.at[k, corner_of(ox, oy), pl.ds(0, 3)]
        elif oz == 0 and oy:
            part = stage.at[k, pl.ds(0, 3)] if oy < 0 else stage.at[k, pl.ds(2, 3)]
            there, at_home = ry.at[k, 1 if oy < 0 else 0], ry.at[k, 0 if oy < 0 else 1]
        elif oy:
            leaving, coming = (pl.ds(0, 1), pl.ds(7, 1)) if oy < 0 else (pl.ds(7, 1), pl.ds(0, 1))
            part = stage.at[k, 2, leaving]
            there, at_home = rz.at[k, 1, slot_of(-ox, -oy), leaving], rz.at[k, 1, slot_of(ox, oy), coming]
        else:
            half = pl.ds(0, 4)
            part = stage.at[k, 5, half]
            there, at_home = rz.at[k, oz, slot_of(-ox, -oy), half], rz.at[k, oz, slot_of(ox, oy), half]
        if incoming:
            return remote(part, at_home, h_ss.at[k, mine], h_rs.at[k, mine], target)
        return remote(part, there, h_ss.at[k, mine], h_rs.at[k, theirs], target)

    def plane_copies(k, ox, incoming):
        own, halo = (1, 9) if ox < 0 else (8, 0)
        part = cor.at[k, :, pl.ds(own * PY + 8, 32), :]
        there = cor.at[k, :, pl.ds(halo * PY + 8, 32), :]
        at_home = cor.at[k, :, pl.ds((0 if ox < 0 else 9) * PY + 8, 32), :]
        mine, theirs = (0, 1) if ox < 0 else (1, 0)
        if incoming:
            return remote(part, at_home, x_ss.at[k, mine], x_rs.at[k, mine], device(ox, 0, 0))
        return remote(part, there, x_ss.at[k, mine], x_rs.at[k, theirs], device(ox, 0, 0))

    def for_offsets(fn):
        for ox, oy in OFFSETS:
            guarded(exists(ox, oy), functools.partial(fn, ox, oy))

    def far_halo(k, fn, incoming=False):
        for_offsets(lambda ox, oy: fn(halo_copies(k, ox, oy, 1, incoming)))

    def near_halo(k, fn, incoming=False, planes=True):
        def each(ox, oy):
            if (ox, oy) == (0, 0):
                return
            if planes and oy == 0:
                fn(plane_copies(k, ox, incoming))
            fn(halo_copies(k, ox, oy, 0, incoming))
        for_offsets(each)

    def all_halo(k, fn, incoming=False, planes=True):
        def each(ox, oy):
            fn(halo_copies(k, ox, oy, 1, incoming))
            if (ox, oy) != (0, 0):
                fn(halo_copies(k, ox, oy, 0, incoming))
                if planes and oy == 0:
                    fn(plane_copies(k, ox, incoming))
        for_offsets(each)

    def for_planes(k, fn):
        for ox in (-1, 1):
            guarded(exists(ox, 0), functools.partial(lambda ox: fn(plane_copies(k, ox, False)), ox))

    def info_copies(ox, oy, oz, incoming):
        mine, theirs = oz * 9 + slot_of(ox, oy), oz * 9 + slot_of(-ox, -oy)
        target = device(ox, oy, oz)
        leaving = coming = pl.ds(0, 8)
        if oy:
            leaving, coming = (pl.ds(0, 1), pl.ds(7, 1)) if oy < 0 else (pl.ds(7, 1), pl.ds(0, 1))
        part = info_send.at[leaving]
        if incoming:
            return remote(part, info_recv.at[oz, slot_of(ox, oy), coming], info_ss.at[mine], info_rs.at[mine], target)
        return remote(part, info_recv.at[oz, slot_of(-ox, -oy), leaving], info_ss.at[mine], info_rs.at[theirs], target)

    def for_info(fn, incoming=False):
        def each(ox, oy):
            fn(info_copies(ox, oy, 1, incoming))
            if (ox, oy) != (0, 0):
                fn(info_copies(ox, oy, 0, incoming))
        for_offsets(each)

    def pack_halo(k):
        packed = zero
        for p in range(2):
            for x in range(CX):
                for t in range(TILES):
                    v = cor[k, p, pl.ds((x + 1) * PY + 8 + 8 * t, 8), :]
                    to = p * 32 + t * 8 + x
                    packed = jnp.where(lane == to, pltpu.roll(v, jnp.where(iz == 0, to + 1, to), 1), packed)
        stage[k, 2] = packed
        stage[k, 5] = jnp.where(lane < 64, packed, roll(packed, 64, 4))
        for p in range(2):
            stage[k, p] = cor[k, p, pl.ds(PY + 8, 8, stride=PY), :]
            stage[k, 3 + p] = cor[k, p, pl.ds(PY + 39, 8, stride=PY), :]
        for c in range(4):
            x, y, row = (1, 8)[c // 2], (8, 39)[c % 2], (0, 7)[c % 2]
            for p in range(2):
                corners[k, c, pl.ds(p, 1), :] = cor[k, p, pl.ds(x * PY + y, 1), :]
            corners[k, c, pl.ds(2, 1), :] = packed[row:row + 1]

    first_row = pl.ds(0, 1)
    others = pl.ds(0, 16 * nz - 1)

    def pair_copy(k):
        return remote(row_send.at[k, first_row], pair_recv.at[k, first_row], pair_ss.at[k], pair_rs.at[k], pair)

    def chip_row(k):
        pair_copy(k).wait_recv()
        chip = row_send[k, first_row] + pair_recv[k, first_row]
        chip_send[k, first_row] = chip
        gath[k, pl.ds(16 * nz - 1, 1)] = chip

    def gather_start(k, *layers):
        for_chips(lambda slot, target: remote(
            chip_send.at[k, first_row], gath.at[k, pl.ds(slot, 1)], ga_ss.at[k], ga_rs.at[k], target).start(), *layers)

    def gather_every(k):
        return remote(gath.at[k, others], gath.at[k, others], ga_ss.at[k], ga_rs.at[k], pair)

    lane_n = iota(1, (128, 128))

    def by_aggregate(values):
        whole = jnp.where(lane_n < 32, values, 0.0)
        high = whole.astype(BF16).astype(F32)
        rest = whole - high
        middle = rest.astype(BF16).astype(F32)
        split = high + pltpu.roll(middle, 32, 1) + pltpu.roll(rest - middle, 64, 1)
        found = jnp.dot(onehot[...], split.astype(BF16), preferred_element_type=F32)
        lane64 = iota(1, (64, 128))
        total = jnp.zeros((64, 128), F32)
        for b in range(16):
            mine = (lane64 % 8 == b % 8) & ((lane64 // 16) % 2 == b // 8)
            total = jnp.where(mine, found[64 * b:64 * b + 64], total)
        total = jnp.where(lane64 < 96, total, 0.0)
        real = (lane64 // 8) % 2 == 0
        return (jnp.sum(jnp.where(real, total, 0.0), axis=1, keepdims=True),
                jnp.sum(jnp.where(real, 0.0, total), axis=1, keepdims=True))

    row64 = iota(0, (64, 128))

    def place_of(row):
        return row // 24, (row % 24) // 6, row % 6

    def setup_rounds():
        found = jnp.full((64, 128), -1.0, F32)
        for s in range(2):
            tiles = {o: info_recv[s, slot_of(*o)] for o in OFFSETS}
            if s == 0:
                tiles[(0, 0)] = info_send[...]
            roles = assemble(tiles, -1.0)
            coltile[4 * s + 0] = roles[0]
            coltile[4 * s + 1] = roles[2]
            coltile[4 * s + 2] = roll(roles[0], -32)
            coltile[4 * s + 3] = roll(roles[1], -32)
            if s == 0:
                for role in range(4):
                    coltile[8 + role] = roll(roles[role], -64)
                corner = [jnp.full((4, 128), -1.0, F32) for _ in range(4)]
                row4 = iota(0, (4, 128))
                for j, tile in enumerate((roles[0], roles[2], roll(roles[0], -32), roll(roles[1], -32))):
                    for c in range(4):
                        sx, sy = c // 2, c % 2
                        spot = (lane == (3 * sy) * 8 + 7 * sx) & (sub == 7 * sy)
                        value = jnp.max(jnp.max(jnp.where(spot, tile, -1.0), axis=1, keepdims=True), axis=0, keepdims=True)
                        corner[j] = jnp.where(row4 == c, value, corner[j])
                    edgecol[j] = corner[j]
            lane64 = iota(1, (64, 128))
            side, at_qx, at_qy = place_of(row64)
            role_at = jnp.where((at_qx == 0) | (at_qx == 3), 1, 0) + jnp.where((at_qy == 0) | (at_qy == 5), 2, 0)
            x_at = jnp.where(at_qx == 2, 4, jnp.where(at_qx == 3, 7, 0))
            spot = 96 + 8 * jnp.clip(at_qy - 1, 0, TILES - 1) + x_at
            for role in range(4):
                spread = jnp.broadcast_to(jnp.max(roles[role], axis=0, keepdims=True), (64, 128))
                found = jnp.where((side == s) & (role_at == role) & (lane64 == spot), spread, found)
        wanted = jnp.broadcast_to(jnp.max(found, axis=1, keepdims=True), (64, 128))
        cval[0] = wanted
        row24 = iota(0, (24, 128))
        lane24 = iota(1, (24, 128))
        x24, t24 = lane24 % 8, (lane24 // 8) % TILES
        for role in range(4):
            if role % 2:
                want_x = jnp.where(x24 == 0, 0, jnp.where(x24 == 7, 3, -1))
            else:
                want_x = 1 + x24 // 4
            if role // 2:
                want_y = jnp.where(t24 == 0, 0, jnp.where(t24 == TILES - 1, 5, -1))
            else:
                want_y = 1 + t24
            zmask[role] = jnp.where((row24 // 6 == want_x) & (row24 % 6 == want_y), 1.0, 0.0)

    def setup_aggregates():
        wanted = cval[0]
        cells = jnp.transpose(gath[0])
        for b in range(16):
            row = jnp.broadcast_to(cells[64 + b:65 + b], (64, 128))
            onehot[pl.ds(64 * b, 64), :] = jnp.where(wanted == row, 1.0, 0.0).astype(BF16)
        for p, total in enumerate(by_aggregate(pltpu.roll(gath[0], 96, 1))):
            ksum[p] = jnp.broadcast_to(total, (64, 128))

    def coarse_values(k):
        r_re, r_im = by_aggregate(gath[k])
        k_re, k_im = ksum[0], ksum[1]
        norm = k_re * k_re + k_im * k_im
        norm = jnp.where(norm > 0.0, norm, 1.0)
        cval[0] = (r_im * k_im - r_re * k_re) / norm
        cval[1] = (-r_re * k_im - r_im * k_re) / norm

    def sides_rounds(k):
        cells = []
        for s in range(2):
            tiles = {}
            for ox, oy in OFFSETS:
                if s == 0 and ox == 0 and oy == 0:
                    tiles[(ox, oy)] = stage[k, 2]
                elif s == 0 and ox and oy:
                    tiles[(ox, oy)] = jnp.broadcast_to(rd[k, corner_of(ox, oy), pl.ds(2, 1), :], (8, 128))
                elif s == 0 and oy:
                    tiles[(ox, oy)] = ry[k, 0, 0] if oy < 0 else ry[k, 1, 2]
                elif oy:
                    tiles[(ox, oy)] = rz[k, s, slot_of(ox, oy)]
                else:
                    folded = rz[k, s, slot_of(ox, oy)]
                    tiles[(ox, oy)] = jnp.where(sub < 4, folded, roll(folded, 64, 4))
            roles = assemble(tiles, 0.0)
            cells.append([(role, roll(role, -32)) for role in roles])
        for r in range(6):
            now = float(r)
            for s in range(2):
                c = cells[s]
                c[0], c[1] = blend(c[0], c[1], coltile[4 * s + 0] == now)
                c[2], c[3] = blend(c[2], c[3], coltile[4 * s + 1] == now)
                c[0], c[2] = blend(c[0], c[2], coltile[4 * s + 2] == now)
                c[1], c[3] = blend(c[1], c[3], coltile[4 * s + 3] == now)
            for role in range(4):
                cells[0][role], cells[1][role] = blend(cells[0][role], cells[1][role], coltile[8 + role] == now)
        return cells

    def main_rounds(k):
        def lines(planes, rows):
            return tuple(
                jnp.concatenate([cor[k, p, pl.ds(x * PY + y, 1), :] for x in planes for y in rows], axis=0) for p in range(2))

        c0 = lines((1, 8), (8, 39))
        px = lines((0, 9), (8, 39))
        halo_rows = []
        for p in range(2):
            parts = []
            for x_at in (0, 7):
                parts += [ry[k, 0, 1 + p, pl.ds(x_at, 1), :], ry[k, 1, p, pl.ds(x_at, 1), :]]
            halo_rows.append(jnp.concatenate(parts, axis=0))
        py = tuple(halo_rows)
        diagonal = []
        for p in range(2):
            parts = []
            for c in range(4):
                parts.append(rd[k, c, pl.ds(p, 1), :])
            diagonal.append(jnp.concatenate(parts, axis=0))
        pxy = tuple(diagonal)
        for r in range(6):
            now = float(r)
            c0, px = blend(c0, px, edgecol[0] == now)
            py, pxy = blend(py, pxy, edgecol[1] == now)
            c0, py = blend(c0, py, edgecol[2] == now)
            px, pxy = blend(px, pxy, edgecol[3] == now)
        for own, halo, ox in ((1, 0, -1), (8, 9, 1)):
            a = tuple(cor[k, p, pl.ds(own * PY + 8, 32), :] for p in range(2))
            b = tuple(cor[k, p, pl.ds(halo * PY + 8, 32), :] for p in range(2))
            a, b = blend(a, b, jnp.broadcast_to(has_x[ox], (32, 128)))
            for p in range(2):
                cor[k, p, pl.ds(own * PY + 8, 32), :] = a[p]
                cor[k, p, pl.ds(halo * PY + 8, 32), :] = b[p]
        for own, halo, oy in ((8, 7, -1), (39, 40, 1)):
            a = tuple(stage[k, p if oy < 0 else 3 + p] for p in range(2))
            b = tuple(ry[k, 0, 1 + p] if oy < 0 else ry[k, 1, p] for p in range(2))
            a, b = blend(a, b, jnp.broadcast_to(has_y[oy], (8, 128)))
            for p in range(2):
                cor[k, p, pl.ds(PY + own, 8, stride=PY), :] = a[p]
                cor[k, p, pl.ds(PY + halo, 8, stride=PY), :] = b[p]
        for c in range(4):
            sx, sy = c // 2, c % 2
            own_x, halo_x = (1, 8)[sx], (0, 9)[sx]
            own_y, halo_y = (8, 39)[sy], (7, 40)[sy]
            for p in range(2):
                cor[k, p, pl.ds(own_x * PY + own_y, 1), :] = c0[p][c:c + 1]
                cor[k, p, pl.ds(halo_x * PY + own_y, 1), :] = px[p][c:c + 1]
                cor[k, p, pl.ds(own_x * PY + halo_y, 1), :] = py[p][c:c + 1]
                cor[k, p, pl.ds(halo_x * PY + halo_y, 1), :] = pxy[p][c:c + 1]

    def add_correction(k, cells):
        last = k == SWEEPS - 1
        for p in range(2):
            turned = [pltpu.roll(cells[0][role][p], zf, 1) for role in range(4)]
            for x in range(10):
                if last and x in (0, 9):
                    continue
                role = 1 if x in (0, 9) else 0
                near = min(max(x - 1, 0), 7)
                for t in range(TILES):
                    column = roll(turned[role], -(8 * t + near))
                    rows = pl.ds(x * PY + 8 + 8 * t, 8)
                    fld[p, rows, :] = fld[p, rows, :] + jnp.where(at_face, column, cor[k, p, rows, :])
                if last:
                    continue
                for t, at, y in ((0, 0, 7), (TILES - 1, 7, 40)):
                    column = roll(turned[2 + role], -(8 * t + near))[at:at + 1]
                    place = pl.ds(x * PY + y, 1)
                    fld[p, place, :] = fld[p, place, :] + jnp.where(at_face[0:1], column, cor[k, p, place, :])
            if not last:
                for role in range(4):
                    fz[role, p] = fz[role, p] + cells[1][role][p]

    def term(p, role, t, x, height=8):
        at_qx = (0 if x == 0 else 3) if role % 2 else 1 + x // 4
        at_qy = (0 if t == 0 else 5) if role // 2 else 1 + t
        return jnp.broadcast_to(cval[p, pl.ds(at_qx * 6 + at_qy, 1), :], (height, 128))

    def add_coarse(last):
        for p in range(2):
            for x in range(10):
                if last and x in (0, 9):
                    continue
                role = 1 if x in (0, 9) else 0
                near = min(max(x - 1, 0), 7)
                for t in range(TILES):
                    value = term(p, role, t, near)
                    rows = pl.ds(x * PY + 8 + 8 * t, 8)
                    if last:
                        out[p, x - 1, pl.ds(8 * t, 8), :] = fld[p, rows, :] + value
                    else:
                        coa[p, rows, :] = value
                        fld[p, rows, :] = fld[p, rows, :] + value
                if last:
                    continue
                for t, y in ((0, 7), (TILES - 1, 40)):
                    place = pl.ds(x * PY + y, 1)
                    value = term(p, 2 + role, t, near, 1)
                    coa[p, place, :] = value
                    fld[p, place, :] = fld[p, place, :] + value
            if not last:
                other = cval[p, pl.ds(24, 24), :]
                for role in range(4):
                    halo = jnp.broadcast_to(jnp.sum(other * zmask[role], axis=0, keepdims=True), (8, 128))
                    coz[role, p] = halo
                    fz[role, p] = fz[role, p] + halo

    def coarse_row():
        values, smooth = [], []
        for p in range(2):
            c = cval[p]
            v = (2.0 * CZ - 1.0) * c[0:24] + 0.5 * c[24:48]
            for at in (1, 2):
                u = 7.0 * v[6 * at:6 * at + 6] + 0.5 * (v[6 * at - 6:6 * at] + v[6 * at + 6:6 * at + 12])
                smooth.append(15.0 * u[1:5] + 0.5 * (u[0:4] + u[2:6]))
                values.append(c[6 * at + 1:6 * at + 5])
        c_re, c_im = jnp.concatenate(values[0:2], axis=0), jnp.concatenate(values[2:4], axis=0)
        s_re, s_im = jnp.concatenate(smooth[0:2], axis=0), jnp.concatenate(smooth[2:4], axis=0)
        a, b = 16.0 * (4 * 8 * CZ) - own_k[0:8], own_k[8:16]
        total = jnp.concatenate([a * c_re - b * c_im - 2.0 * s_re, a * c_im + b * c_re - 2.0 * s_im], axis=0)
        return lanes_of(total, 16 * core)

    for k in range(SWEEPS):
        if k == 0:
            row_send[k, first_row] = row_of(first_pass(), 16 * core) + fixed_row
        else:
            row_send[k, first_row] = row - coarse_row()
        if k == 0:
            jacobi(k)
            pack_halo(k)
            pl.semaphore_wait(barrier, count)
            pair_copy(k).start()
            for_info(lambda copy: copy.start())
        else:
            pair_copy(k).start()
            add_coarse(False)
            residual_pass(coa, coz, res)
            chip_row(k)
            gather_start(k, 0, 1, False)
            jacobi(k)
            for_planes(k, lambda copy: copy.start())
            pack_halo(k)
        far_halo(k, lambda copy: copy.start())
        near_halo(k, lambda copy: copy.start(), planes=k == 0)
        if k == 0:
            chip_row(k)
        gather_start(k, 0 if k == 0 else 1)
        if k == 0:
            for_info(lambda copy: copy.wait_recv(), True)
            setup_rounds()
        pair_copy(k).wait_send()
        all_halo(k, lambda copy: copy.wait_send())
        if k == 0:
            for_info(lambda copy: copy.wait_send())
        all_halo(k, lambda copy: copy.wait_recv(), True)
        cells = sides_rounds(k)
        main_rounds(k)
        add_correction(k, cells)
        if k < SWEEPS - 1:
            row = row_of(residual_pass(fld, fz, src), 16 * core)
        gather_every(k).wait_recv()
        if k == 0:
            setup_aggregates()
        coarse_values(k)
        if k == SWEEPS - 1:
            add_coarse(True)
        gather_every(k).wait_send()


def solution(mesh):
    nx, ny = mesh.shape["gx"], mesh.shape["gy"]

    def step(adjoint_source, velocity, damping, face_rounds, aggregates):
        vmem = pl.BlockSpec(memory_space=pltpu.VMEM)
        hbm = pl.BlockSpec(memory_space=pltpu.MemorySpace.HBM)
        smem = pl.BlockSpec(memory_space=pltpu.SMEM)
        dma = pltpu.SemaphoreType.DMA
        tile = (8, 128)
        block = (CX, CY, CZ)
        return pl.pallas_call(
            functools.partial(kernel, nx, ny),
            out_shape=pltpu.VMEM((2,) + block, F32),
            in_specs=[hbm, hbm, hbm, smem, smem],
            out_specs=vmem,
            scratch_shapes=[
                pltpu.VMEM((2,) + block, F32), pltpu.VMEM(block, F32), pltpu.VMEM(block, F32), dma((3,)),
                pltpu.VMEM(block, F32), pltpu.VMEM(block, F32), pltpu.VMEM(block, F32), pltpu.VMEM(block, F32),
                pltpu.VMEM((2,) + block, F32),
                pltpu.VMEM((2, CX * PY, CZ), F32), pltpu.VMEM((2, CX * PY, CZ), F32),
                pltpu.VMEM((SWEEPS, 2, 10 * PY, CZ), F32),
                pltpu.VMEM((2, 10 * PY, CZ), F32),
                pltpu.VMEM((4, 2) + tile, F32),
                pltpu.VMEM((12,) + tile, F32), pltpu.VMEM((4, 4, 128), F32),
                pltpu.VMEM((1024, 128), BF16), pltpu.VMEM((2, 64, 128), F32), pltpu.VMEM((2, 64, 128), F32),
                pltpu.VMEM((4, 24, 128), F32), pltpu.VMEM((2, 10 * PY, CZ), F32), pltpu.VMEM((4, 2) + tile, F32),
                pltpu.VMEM((16, 128), F32),
                pltpu.VMEM(tile, F32), pltpu.VMEM((2, 9) + tile, F32),
                pltpu.VMEM((SWEEPS, 6) + tile, F32), pltpu.VMEM((SWEEPS, 4) + tile, F32), pltpu.VMEM((SWEEPS, 2, 9) + tile, F32),
                pltpu.VMEM((SWEEPS, 2, 3) + tile, F32), pltpu.VMEM((SWEEPS, 4) + tile, F32),
                pltpu.VMEM((SWEEPS,) + tile, F32), pltpu.VMEM((SWEEPS,) + tile, F32), pltpu.VMEM((SWEEPS,) + tile, F32),
                pltpu.VMEM((SWEEPS, 128, 128), F32),
                dma((18,)), dma((18,)), dma((SWEEPS, 18)), dma((SWEEPS, 18)),
                dma((SWEEPS, 2)), dma((SWEEPS, 2)), dma((SWEEPS,)), dma((SWEEPS,)), dma((SWEEPS,)), dma((SWEEPS,)),
            ],
            compiler_params=pltpu.CompilerParams(
                collective_id=0, has_side_effects=True, vmem_limit_bytes=56 * 1024 * 1024
            ),
        )(adjoint_source, velocity, damping, face_rounds, jnp.transpose(aggregates, (0, 2, 1)))

    placed = (
        P(None, "gx", "gy", "gz"),
        P("gx", "gy", "gz"),
        P("gx", "gy", "gz"),
        P("gx", "gy", "gz", None),
        P("gx", "gy", "gz"),
    )
    return jax.shard_map(
        step, mesh=mesh, in_specs=placed, out_specs=P(None, "gx", "gy", "gz"), check_vma=False
    )
```

```python
import functools

import jax
import jax.numpy as jnp
from jax import lax
from jax.experimental import pallas as pl
from jax.experimental.pallas import tpu as pltpu
from jax.sharding import PartitionSpec as P

MESH = pl.DeviceIdType.MESH
F32 = jnp.float32
BF16 = jnp.bfloat16

CX, CY, CZ = 8, 32, 128
PY = 48
TILES = CY // 8
SWEEPS = 3
SMOOTH = 4
GAMMA_RE = 0.6
GAMMA_IM = 0.25
RELAX = 0.8
OMEGA_SQ = 9.0

OFFSETS = [(ox, oy) for ox in (-1, 0, 1) for oy in (-1, 0, 1)]
OFFSETS.sort(key=lambda o: -abs(o[0]) - abs(o[1]))


def slot_of(ox, oy):
    return (ox + 1) * 3 + (oy + 1)


def corner_of(ox, oy):
    return (1 if ox > 0 else 0) * 2 + (1 if oy > 0 else 0)


def iota(dim, shape=(8, 128)):
    return lax.broadcasted_iota(jnp.int32, shape, dim)


def roll(v, lanes, subs=0):
    if isinstance(lanes, int):
        lanes = lanes % 128
    if not isinstance(lanes, int) or lanes:
        v = pltpu.roll(v, lanes, 1)
    if subs % 8:
        v = pltpu.roll(v, subs % 8, 0)
    return v


def blend(a, b, mask):
    d_re = b[0] - a[0]
    d_im = b[1] - a[1]
    t_re = GAMMA_RE * d_re - GAMMA_IM * d_im
    t_im = GAMMA_RE * d_im + GAMMA_IM * d_re
    if mask is not None:
        t_re = jnp.where(mask, t_re, 0.0)
        t_im = jnp.where(mask, t_im, 0.0)
    return (a[0] + t_re, a[1] + t_im), (b[0] - t_re, b[1] - t_im)


def kernel(
    nx, ny,
    src_in, vel_in, dmp_in, rounds, aggs, out,
    src, vel, dmp, in_sem,
    kap, kdm, mre, mim, res, ping, pong, cor, fld, fz,
    coltile, edgecol, onehot, ksum, cval, zmask, coa, coz, own_k,
    info_send, info_recv, stage, corners, rz, ry, rd, row_send, pair_recv, chip_send, gath,
    info_ss, info_rs, h_ss, h_rs, x_ss, x_rs, pair_ss, pair_rs, ga_ss, ga_rs,
):
    ix, iy, iz = lax.axis_index("gx"), lax.axis_index("gy"), lax.axis_index("gz")
    lane, sub = iota(1), iota(0)
    lx, lt = lane % 8, (lane // 8) % TILES
    zf = jnp.where(iz == 0, 127, 0).astype(jnp.int32)
    at_face = lane == zf
    first_lane, last_lane = lane == 0, lane == 127
    lane32 = iota(1, (32, 128))
    first32, last32 = lane32 == 0, lane32 == 127

    has_x = {-1: ix > 0, 1: ix < nx - 1}
    has_y = {-1: iy > 0, 1: iy < ny - 1}

    def exists(ox, oy):
        if ox and oy:
            return jnp.logical_and(has_x[ox], has_y[oy])
        if ox:
            return has_x[ox]
        if oy:
            return has_y[oy]
        return None

    def guarded(cond, fn):
        if cond is None:
            fn()
        else:
            pl.when(cond)(fn)

    def device(ox, oy, oz):
        return (ix + ox, iy + oy, (1 - iz) if oz else iz)

    core = lax.rem(iy, 2)
    at_x, at_y, at_z = lax.rem(ix, 4), ix // 4, iz * (ny // 2) + iy // 2
    nz = ny
    pair = (ix, iy + 1 - 2 * core, iz)
    across = sorted(((dx, dy) for dx in range(4) for dy in range(4)), key=lambda d: -min(d[0], 4 - d[0]) - min(d[1], 4 - d[1]))
    across_x = [lax.rem(at_y + dy, 4) * 4 + lax.rem(at_x + dx, 4) for dx, dy in across]

    def for_chips(fn):
        def layer(i, carry):
            step = (i + 1) // 2
            there = lax.rem(at_z + nz // 2 + jnp.where(lax.rem(i, 2) == 1, nz - step, step), nz)
            ty, tz = lax.rem(there, ny // 2) * 2 + core, there // (ny // 2)
            for j in range(16):
                fn(i * 16 + j, (across_x[j], ty, tz))
            return carry
        lax.fori_loop(0, nz - 1, layer, 0)
        for j in range(15):
            fn((nz - 1) * 16 + j, (across_x[j], iy, iz))

    loads = [pltpu.make_async_copy(whole, local, in_sem.at[i])
             for i, (whole, local) in enumerate(((vel_in, vel), (dmp_in, dmp), (src_in, src)))]
    for load in loads:
        load.start()

    zero = jnp.zeros((8, 128), F32)
    for k in range(SWEEPS):
        for p in range(2):
            for x in range(10):
                tiles = range(6) if x in (0, 9) else (0, 5)
                for t in tiles:
                    cor[k, p, pl.ds(x * PY + 8 * t, 8), :] = zero
        for s in range(2):
            for o in range(9):
                rz[k, s, o] = zero
        for o in range(2):
            for j in range(3):
                ry[k, o, j] = zero
        for o in range(4):
            rd[k, o] = zero
    for s in range(2):
        for o in range(9):
            info_recv[s, o] = zero - 1.0

    barrier = pltpu.get_barrier_semaphore()
    count = jnp.int32(16 * nz - 1 + 1)
    def tell_chip(slot, target):
        pl.semaphore_signal(barrier, inc=1, device_id=target, device_id_type=MESH)

    for_chips(tell_chip)
    tell_chip(0, pair)
    for ox, oy in OFFSETS:
        if oy:
            def tell(ox=ox, oy=oy):
                for oz in (1, 0):
                    pl.semaphore_signal(barrier, inc=1, device_id=device(ox, oy, oz), device_id_type=MESH)
            guarded(exists(ox, oy), tell)
            count = count + jnp.where(exists(ox, oy), 2, 0)


    for buf in (ping, pong):
        for p in range(2):
            for x in range(8):
                buf[p, pl.ds(x * PY, 8), :] = zero
                buf[p, pl.ds(x * PY + 40, 8), :] = zero
    for p in range(2):
        for x in range(10):
            for t in range(6):
                fld[p, pl.ds(x * PY + 8 * t, 8), :] = zero
        for role in range(4):
            fz[role, p] = zero

    for load in loads:
        load.wait()
    for x in range(CX):
        v = vel[x]
        kappa = OMEGA_SQ / (v * v)
        damp = kappa * dmp[x]
        d_re = 14.0 - kappa
        scale = RELAX / (d_re * d_re + damp * damp)
        kap[x] = 16.0 - kappa
        kdm[x] = damp
        mre[x] = d_re * scale
        mim[x] = -damp * scale

    def face(i, inside):
        return jnp.where(inside, rounds[0, 0, 0, i].astype(F32), -1.0)

    low_x, high_x = face(0, ix > 0), face(1, ix < nx - 1)
    low_y, high_y = face(2, iy > 0), face(3, iy < ny - 1)
    depth = jnp.where(iz == 0, rounds[0, 0, 0, 5].astype(F32), rounds[0, 0, 0, 4].astype(F32))
    ids = [[aggs[qx, 0, qy].astype(F32) for qy in range(TILES)] for qx in range(2)]
    info = jnp.where(lx == 0, low_x, jnp.where(lx == 7, high_x, -1.0))
    col_y = jnp.where((lt == 0) & (sub == 0), low_y, jnp.where((lt == TILES - 1) & (sub == 7), high_y, -1.0))
    info = jnp.where(lane >= 32, col_y, info)
    info = jnp.where(lane >= 64, depth, info)
    for qx in range(2):
        for qy in range(TILES):
            info = jnp.where((lane >= 96) & (lx // 4 == qx) & (lt == qy), ids[qx][qy], info)
    info_send[...] = info

    low_rows = sub < 4
    lane1 = iota(1, (1, 128))

    def row_of(sums, first):
        rows = [jnp.sum(sums[p][qx][t], axis=0, keepdims=True) for p in range(2) for qx in range(2) for t in range(TILES)]
        return lanes_of(jnp.sum(jnp.concatenate(rows, axis=0), axis=1, keepdims=True), first)

    def lanes_of(total, first):
        spread = jnp.where(iota(1, (16, 128)) == iota(0, (16, 128)) + first, jnp.broadcast_to(total, (16, 128)), 0.0)
        return jnp.sum(spread, axis=0, keepdims=True)

    def rows_of(v, t):
        return v[8 * t:8 * t + 8]

    sums = [[[zero] * TILES for _ in range(2)] for _ in range(2)]
    for x in range(CX):
        kappa, damp = 16.0 - kap[x], kdm[x]
        for t in range(TILES):
            sums[0][x // 4][t] = sums[0][x // 4][t] + rows_of(kappa, t)
            sums[1][x // 4][t] = sums[1][x // 4][t] + rows_of(damp, t)
    fixed_row = row_of(sums, 32 + 16 * core)
    for p in range(2):
        for qx in range(2):
            for t in range(TILES):
                total = jnp.sum(jnp.sum(sums[p][qx][t], axis=0, keepdims=True), axis=1, keepdims=True)
                own_k[pl.ds(8 * p + TILES * qx + t, 1), :] = jnp.broadcast_to(total, (1, 128))
    for qx in range(2):
        for t in range(TILES):
            fixed_row = fixed_row + jnp.where(lane1 == 64 + 8 * core + qx * TILES + t, ids[qx][t], 0.0)

    def assemble(tiles, default):
        def pick(parts):
            value = jnp.full((8, 128), default, F32)
            for mask, tile in parts:
                value = jnp.where(mask, tile, value)
            return value
        t0, t3 = (lt == 0) & (sub == 0), (lt == TILES - 1) & (sub == 7)
        x0, x7 = lx == 0, lx == 7
        across_x = pick([(x0, roll(tiles[(-1, 0)], -7)), (x7, roll(tiles[(1, 0)], 7))])
        across_y = pick([(t0, roll(tiles[(0, -1)], -24, 1)), (t3, roll(tiles[(0, 1)], 24, -1))])
        across_xy = pick([
            (x0 & t0, roll(tiles[(-1, -1)], -31, 1)),
            (x0 & t3, roll(tiles[(-1, 1)], 17, -1)),
            (x7 & t0, roll(tiles[(1, -1)], -17, 1)),
            (x7 & t3, roll(tiles[(1, 1)], 31, -1)),
        ])
        return [tiles[(0, 0)], across_x, across_y, across_xy]

    def smooth_z(v):
        return 2.0 * v + jnp.where(first32, 0.0, pltpu.roll(v, 1, 1)) + jnp.where(last32, 0.0, pltpu.roll(v, 127, 1))

    def residual_pass(field, zone, source, flat=False):
        lefts = []
        for p in range(2):
            c0, px, py, pxy = (zone[role, p] for role in range(4))
            t0, t3 = (lt == 0) & (sub == 0), (lt == TILES - 1) & (sub == 7)

            def smooth_y(v, across):
                up = pltpu.roll(v, 1, 0)
                up = jnp.where(sub == 0, roll(up, 8), up)
                up = jnp.where(t0, across, up)
                down = pltpu.roll(v, 7, 0)
                down = jnp.where(sub == 7, roll(down, -8), down)
                down = jnp.where(t3, across, down)
                return up + 2.0 * v + down

            yc, yx = smooth_y(c0, py), smooth_y(px, pxy)
            w = 2.0 * yc + jnp.where(lx == 0, yx, roll(yc, 1)) + jnp.where(lx == 7, yx, roll(yc, -1))
            lefts.append(pltpu.roll(w, zf, 1))
        sums = [[[zero] * TILES for _ in range(2)] for _ in range(2)]
        ys = [[None] * 10 for _ in range(2)]

        def y_smoothed(p, x):
            if ys[p][x] is None:
                base = x * PY
                ys[p][x] = (field[p, pl.ds(base + 7, 32), :] + field[p, pl.ds(base + 9, 32), :]
                            + 2.0 * field[p, pl.ds(base + 8, 32), :])
            return ys[p][x]

        for x in range(CX):
            smoothed = []
            for p in range(2):
                v = y_smoothed(p, x) + 2.0 * y_smoothed(p, x + 1) + y_smoothed(p, x + 2)
                halo = jnp.concatenate([roll(lefts[p], -(8 * t + x)) for t in range(TILES)], axis=0)
                along = 4.0 * v - jnp.where(first32 | last32, v, 0.0) if flat else smooth_z(v)
                smoothed.append(along + jnp.where(lane32 == zf, halo, 0.0))
            f_re = field[0, pl.ds((x + 1) * PY + 8, 32), :]
            f_im = field[1, pl.ds((x + 1) * PY + 8, 32), :]
            a, b = kap[x], kdm[x]
            r_re = source[0, x] + 0.25 * smoothed[0] - a * f_re + b * f_im
            r_im = source[1, x] + 0.25 * smoothed[1] - a * f_im - b * f_re
            res[0, x] = r_re
            res[1, x] = r_im
            for t in range(TILES):
                sums[0][x // 4][t] = sums[0][x // 4][t] + rows_of(r_re, t)
                sums[1][x // 4][t] = sums[1][x // 4][t] + rows_of(r_im, t)
        return sums

    def first_pass():
        sums = [[[zero] * TILES for _ in range(2)] for _ in range(2)]
        for x in range(CX):
            for p in range(2):
                v = src[p, x]
                res[p, x] = v
                for t in range(TILES):
                    sums[p][x // 4][t] = sums[p][x // 4][t] + rows_of(v, t)
        return sums

    def jacobi(k):
        for x in range(CX):
            a, b = mre[x], mim[x]
            r_re, r_im = res[0, x], res[1, x]
            ping[0, pl.ds(x * PY + 8, 32), :] = a * r_re - b * r_im
            ping[1, pl.ds(x * PY + 8, 32), :] = a * r_im + b * r_re
        buffers = [ping, pong]
        for step in range(1, SMOOTH):
            now, later = buffers[(step - 1) % 2], buffers[step % 2]
            last = step == SMOOTH - 1
            ys = [[None] * CX for _ in range(2)]

            def y_smoothed(p, x):
                if x < 0 or x >= CX:
                    return None
                if ys[p][x] is None:
                    base = x * PY
                    ys[p][x] = (now[p, pl.ds(base + 7, 32), :] + now[p, pl.ds(base + 9, 32), :]
                                + 2.0 * now[p, pl.ds(base + 8, 32), :])
                return ys[p][x]

            for x in range(CX):
                misfit, old = [], []
                for p in range(2):
                    v = 2.0 * y_smoothed(p, x)
                    for near in (y_smoothed(p, x - 1), y_smoothed(p, x + 1)):
                        if near is not None:
                            v = v + near
                    c = now[p, pl.ds(x * PY + 8, 32), :]
                    old.append(c)
                    misfit.append(res[p, x] + 0.25 * smooth_z(v) - 2.0 * c)
                a, b = mre[x], mim[x]
                new_re = 0.2 * old[0] + (a * misfit[0] - b * misfit[1])
                new_im = 0.2 * old[1] + (a * misfit[1] + b * misfit[0])
                if last:
                    cor[k, 0, pl.ds((x + 1) * PY + 8, 32), :] = new_re
                    cor[k, 1, pl.ds((x + 1) * PY + 8, 32), :] = new_im
                else:
                    later[0, pl.ds(x * PY + 8, 32), :] = new_re
                    later[1, pl.ds(x * PY + 8, 32), :] = new_im

    def remote(src_ref, dst_ref, ssem, rsem, target):
        return pltpu.make_async_remote_copy(
            src_ref=src_ref, dst_ref=dst_ref, send_sem=ssem, recv_sem=rsem,
            device_id=target, device_id_type=MESH)

    def halo_copies(k, ox, oy, oz, incoming):
        mine, theirs = oz * 9 + slot_of(ox, oy), oz * 9 + slot_of(-ox, -oy)
        target = device(ox, oy, oz)
        if oz == 0 and ox and oy:
            part = corners.at[k, corner_of(ox, oy), pl.ds(0, 3)]
            there, at_home = rd.at[k, corner_of(-ox, -oy), pl.ds(0, 3)], rd.at[k, corner_of(ox, oy), pl.ds(0, 3)]
        elif oz == 0 and oy:
            part = stage.at[k, pl.ds(0, 3)] if oy < 0 else stage.at[k, pl.ds(2, 3)]
            there, at_home = ry.at[k, 1 if oy < 0 else 0], ry.at[k, 0 if oy < 0 else 1]
        elif oy:
            leaving, coming = (pl.ds(0, 1), pl.ds(7, 1)) if oy < 0 else (pl.ds(7, 1), pl.ds(0, 1))
            part = stage.at[k, 2, leaving]
            there, at_home = rz.at[k, 1, slot_of(-ox, -oy), leaving], rz.at[k, 1, slot_of(ox, oy), coming]
        else:
            half = pl.ds(0, 4)
            part = stage.at[k, 5, half]
            there, at_home = rz.at[k, oz, slot_of(-ox, -oy), half], rz.at[k, oz, slot_of(ox, oy), half]
        if incoming:
            return remote(part, at_home, h_ss.at[k, mine], h_rs.at[k, mine], target)
        return remote(part, there, h_ss.at[k, mine], h_rs.at[k, theirs], target)

    def plane_copies(k, ox, incoming):
        own, halo = (1, 9) if ox < 0 else (8, 0)
        part = cor.at[k, :, pl.ds(own * PY + 8, 32), :]
        there = cor.at[k, :, pl.ds(halo * PY + 8, 32), :]
        at_home = cor.at[k, :, pl.ds((0 if ox < 0 else 9) * PY + 8, 32), :]
        mine, theirs = (0, 1) if ox < 0 else (1, 0)
        if incoming:
            return remote(part, at_home, x_ss.at[k, mine], x_rs.at[k, mine], device(ox, 0, 0))
        return remote(part, there, x_ss.at[k, mine], x_rs.at[k, theirs], device(ox, 0, 0))

    def for_offsets(fn):
        for ox, oy in OFFSETS:
            guarded(exists(ox, oy), functools.partial(fn, ox, oy))

    def far_halo(k, fn, incoming=False):
        for_offsets(lambda ox, oy: fn(halo_copies(k, ox, oy, 1, incoming)))

    def near_halo(k, fn, incoming=False, planes=True):
        def each(ox, oy):
            if (ox, oy) == (0, 0):
                return
            if planes and oy == 0:
                fn(plane_copies(k, ox, incoming))
            fn(halo_copies(k, ox, oy, 0, incoming))
        for_offsets(each)

    def all_halo(k, fn, incoming=False, planes=True):
        def each(ox, oy):
            fn(halo_copies(k, ox, oy, 1, incoming))
            if (ox, oy) != (0, 0):
                fn(halo_copies(k, ox, oy, 0, incoming))
                if planes and oy == 0:
                    fn(plane_copies(k, ox, incoming))
        for_offsets(each)

    def for_planes(k, fn):
        for ox in (-1, 1):
            guarded(exists(ox, 0), functools.partial(lambda ox: fn(plane_copies(k, ox, False)), ox))

    def info_copies(ox, oy, oz, incoming):
        mine, theirs = oz * 9 + slot_of(ox, oy), oz * 9 + slot_of(-ox, -oy)
        target = device(ox, oy, oz)
        leaving = coming = pl.ds(0, 8)
        if oy:
            leaving, coming = (pl.ds(0, 1), pl.ds(7, 1)) if oy < 0 else (pl.ds(7, 1), pl.ds(0, 1))
        part = info_send.at[leaving]
        if incoming:
            return remote(part, info_recv.at[oz, slot_of(ox, oy), coming], info_ss.at[mine], info_rs.at[mine], target)
        return remote(part, info_recv.at[oz, slot_of(-ox, -oy), leaving], info_ss.at[mine], info_rs.at[theirs], target)

    def for_info(fn, incoming=False):
        def each(ox, oy):
            fn(info_copies(ox, oy, 1, incoming))
            if (ox, oy) != (0, 0):
                fn(info_copies(ox, oy, 0, incoming))
        for_offsets(each)

    def pack_halo(k):
        packed = zero
        for p in range(2):
            for x in range(CX):
                for t in range(TILES):
                    v = cor[k, p, pl.ds((x + 1) * PY + 8 + 8 * t, 8), :]
                    to = p * 32 + t * 8 + x
                    packed = jnp.where(lane == to, pltpu.roll(v, jnp.where(iz == 0, to + 1, to), 1), packed)
        stage[k, 2] = packed
        stage[k, 5] = jnp.where(lane < 64, packed, roll(packed, 64, 4))
        for p in range(2):
            stage[k, p] = cor[k, p, pl.ds(PY + 8, 8, stride=PY), :]
            stage[k, 3 + p] = cor[k, p, pl.ds(PY + 39, 8, stride=PY), :]
        for c in range(4):
            x, y, row = (1, 8)[c // 2], (8, 39)[c % 2], (0, 7)[c % 2]
            for p in range(2):
                corners[k, c, pl.ds(p, 1), :] = cor[k, p, pl.ds(x * PY + y, 1), :]
            corners[k, c, pl.ds(2, 1), :] = packed[row:row + 1]

    first_row = pl.ds(0, 1)
    others = pl.ds(0, 16 * nz - 1)

    def pair_copy(k):
        return remote(row_send.at[k, first_row], pair_recv.at[k, first_row], pair_ss.at[k], pair_rs.at[k], pair)

    def gather_start(k):
        chip = row_send[k, first_row] + pair_recv[k, first_row]
        chip_send[k, first_row] = chip
        gath[k, pl.ds(16 * nz - 1, 1)] = chip
        for_chips(lambda slot, target: remote(
            chip_send.at[k, first_row], gath.at[k, pl.ds(slot, 1)], ga_ss.at[k], ga_rs.at[k], target).start())

    def gather_every(k):
        return remote(gath.at[k, others], gath.at[k, others], ga_ss.at[k], ga_rs.at[k], pair)

    lane_n = iota(1, (128, 128))

    def by_aggregate(values):
        whole = jnp.where(lane_n < 32, values, 0.0)
        high = whole.astype(BF16).astype(F32)
        rest = whole - high
        middle = rest.astype(BF16).astype(F32)
        split = high + pltpu.roll(middle, 32, 1) + pltpu.roll(rest - middle, 64, 1)
        found = jnp.dot(onehot[...], split.astype(BF16), preferred_element_type=F32)
        lane64 = iota(1, (64, 128))
        total = jnp.zeros((64, 128), F32)
        for b in range(16):
            mine = (lane64 % 8 == b % 8) & ((lane64 // 16) % 2 == b // 8)
            total = jnp.where(mine, found[64 * b:64 * b + 64], total)
        total = jnp.where(lane64 < 96, total, 0.0)
        real = (lane64 // 8) % 2 == 0
        return (jnp.sum(jnp.where(real, total, 0.0), axis=1, keepdims=True),
                jnp.sum(jnp.where(real, 0.0, total), axis=1, keepdims=True))

    row64 = iota(0, (64, 128))

    def place_of(row):
        return row // 24, (row % 24) // 6, row % 6

    def setup_rounds():
        found = jnp.full((64, 128), -1.0, F32)
        for s in range(2):
            tiles = {o: info_recv[s, slot_of(*o)] for o in OFFSETS}
            if s == 0:
                tiles[(0, 0)] = info_send[...]
            roles = assemble(tiles, -1.0)
            coltile[4 * s + 0] = roles[0]
            coltile[4 * s + 1] = roles[2]
            coltile[4 * s + 2] = roll(roles[0], -32)
            coltile[4 * s + 3] = roll(roles[1], -32)
            if s == 0:
                for role in range(4):
                    coltile[8 + role] = roll(roles[role], -64)
                corner = [jnp.full((4, 128), -1.0, F32) for _ in range(4)]
                row4 = iota(0, (4, 128))
                for j, tile in enumerate((roles[0], roles[2], roll(roles[0], -32), roll(roles[1], -32))):
                    for c in range(4):
                        sx, sy = c // 2, c % 2
                        spot = (lane == (3 * sy) * 8 + 7 * sx) & (sub == 7 * sy)
                        value = jnp.max(jnp.max(jnp.where(spot, tile, -1.0), axis=1, keepdims=True), axis=0, keepdims=True)
                        corner[j] = jnp.where(row4 == c, value, corner[j])
                    edgecol[j] = corner[j]
            lane64 = iota(1, (64, 128))
            side, at_qx, at_qy = place_of(row64)
            role_at = jnp.where((at_qx == 0) | (at_qx == 3), 1, 0) + jnp.where((at_qy == 0) | (at_qy == 5), 2, 0)
            x_at = jnp.where(at_qx == 2, 4, jnp.where(at_qx == 3, 7, 0))
            spot = 96 + 8 * jnp.clip(at_qy - 1, 0, TILES - 1) + x_at
            for role in range(4):
                spread = jnp.broadcast_to(jnp.max(roles[role], axis=0, keepdims=True), (64, 128))
                found = jnp.where((side == s) & (role_at == role) & (lane64 == spot), spread, found)
        wanted = jnp.broadcast_to(jnp.max(found, axis=1, keepdims=True), (64, 128))
        cval[0] = wanted
        row24 = iota(0, (24, 128))
        lane24 = iota(1, (24, 128))
        x24, t24 = lane24 % 8, (lane24 // 8) % TILES
        for role in range(4):
            if role % 2:
                want_x = jnp.where(x24 == 0, 0, jnp.where(x24 == 7, 3, -1))
            else:
                want_x = 1 + x24 // 4
            if role // 2:
                want_y = jnp.where(t24 == 0, 0, jnp.where(t24 == TILES - 1, 5, -1))
            else:
                want_y = 1 + t24
            zmask[role] = jnp.where((row24 // 6 == want_x) & (row24 % 6 == want_y), 1.0, 0.0)

    def setup_aggregates():
        wanted = cval[0]
        cells = jnp.transpose(gath[0])
        for b in range(16):
            row = jnp.broadcast_to(cells[64 + b:65 + b], (64, 128))
            onehot[pl.ds(64 * b, 64), :] = jnp.where(wanted == row, 1.0, 0.0).astype(BF16)
        for p, total in enumerate(by_aggregate(pltpu.roll(gath[0], 96, 1))):
            ksum[p] = jnp.broadcast_to(total, (64, 128))

    def coarse_values(k):
        r_re, r_im = by_aggregate(gath[k])
        k_re, k_im = ksum[0], ksum[1]
        norm = k_re * k_re + k_im * k_im
        norm = jnp.where(norm > 0.0, norm, 1.0)
        cval[0] = (r_im * k_im - r_re * k_re) / norm
        cval[1] = (-r_re * k_im - r_im * k_re) / norm

    def sides_rounds(k):
        cells = []
        for s in range(2):
            tiles = {}
            for ox, oy in OFFSETS:
                if s == 0 and ox == 0 and oy == 0:
                    tiles[(ox, oy)] = stage[k, 2]
                elif s == 0 and ox and oy:
                    tiles[(ox, oy)] = jnp.broadcast_to(rd[k, corner_of(ox, oy), pl.ds(2, 1), :], (8, 128))
                elif s == 0 and oy:
                    tiles[(ox, oy)] = ry[k, 0, 0] if oy < 0 else ry[k, 1, 2]
                elif oy:
                    tiles[(ox, oy)] = rz[k, s, slot_of(ox, oy)]
                else:
                    folded = rz[k, s, slot_of(ox, oy)]
                    tiles[(ox, oy)] = jnp.where(sub < 4, folded, roll(folded, 64, 4))
            roles = assemble(tiles, 0.0)
            cells.append([(role, roll(role, -32)) for role in roles])
        for r in range(6):
            now = float(r)
            for s in range(2):
                c = cells[s]
                c[0], c[1] = blend(c[0], c[1], coltile[4 * s + 0] == now)
                c[2], c[3] = blend(c[2], c[3], coltile[4 * s + 1] == now)
                c[0], c[2] = blend(c[0], c[2], coltile[4 * s + 2] == now)
                c[1], c[3] = blend(c[1], c[3], coltile[4 * s + 3] == now)
            for role in range(4):
                cells[0][role], cells[1][role] = blend(cells[0][role], cells[1][role], coltile[8 + role] == now)
        return cells

    def main_rounds(k):
        def lines(planes, rows):
            return tuple(
                jnp.concatenate([cor[k, p, pl.ds(x * PY + y, 1), :] for x in planes for y in rows], axis=0) for p in range(2))

        c0 = lines((1, 8), (8, 39))
        px = lines((0, 9), (8, 39))
        halo_rows = []
        for p in range(2):
            parts = []
            for x_at in (0, 7):
                parts += [ry[k, 0, 1 + p, pl.ds(x_at, 1), :], ry[k, 1, p, pl.ds(x_at, 1), :]]
            halo_rows.append(jnp.concatenate(parts, axis=0))
        py = tuple(halo_rows)
        diagonal = []
        for p in range(2):
            parts = []
            for c in range(4):
                parts.append(rd[k, c, pl.ds(p, 1), :])
            diagonal.append(jnp.concatenate(parts, axis=0))
        pxy = tuple(diagonal)
        for r in range(6):
            now = float(r)
            c0, px = blend(c0, px, edgecol[0] == now)
            py, pxy = blend(py, pxy, edgecol[1] == now)
            c0, py = blend(c0, py, edgecol[2] == now)
            px, pxy = blend(px, pxy, edgecol[3] == now)
        for own, halo, ox in ((1, 0, -1), (8, 9, 1)):
            a = tuple(cor[k, p, pl.ds(own * PY + 8, 32), :] for p in range(2))
            b = tuple(cor[k, p, pl.ds(halo * PY + 8, 32), :] for p in range(2))
            a, b = blend(a, b, jnp.broadcast_to(has_x[ox], (32, 128)))
            for p in range(2):
                cor[k, p, pl.ds(own * PY + 8, 32), :] = a[p]
                cor[k, p, pl.ds(halo * PY + 8, 32), :] = b[p]
        for own, halo, oy in ((8, 7, -1), (39, 40, 1)):
            a = tuple(stage[k, p if oy < 0 else 3 + p] for p in range(2))
            b = tuple(ry[k, 0, 1 + p] if oy < 0 else ry[k, 1, p] for p in range(2))
            a, b = blend(a, b, jnp.broadcast_to(has_y[oy], (8, 128)))
            for p in range(2):
                cor[k, p, pl.ds(PY + own, 8, stride=PY), :] = a[p]
                cor[k, p, pl.ds(PY + halo, 8, stride=PY), :] = b[p]
        for c in range(4):
            sx, sy = c // 2, c % 2
            own_x, halo_x = (1, 8)[sx], (0, 9)[sx]
            own_y, halo_y = (8, 39)[sy], (7, 40)[sy]
            for p in range(2):
                cor[k, p, pl.ds(own_x * PY + own_y, 1), :] = c0[p][c:c + 1]
                cor[k, p, pl.ds(halo_x * PY + own_y, 1), :] = px[p][c:c + 1]
                cor[k, p, pl.ds(own_x * PY + halo_y, 1), :] = py[p][c:c + 1]
                cor[k, p, pl.ds(halo_x * PY + halo_y, 1), :] = pxy[p][c:c + 1]

    def add_correction(k, cells):
        last = k == SWEEPS - 1
        for p in range(2):
            turned = [pltpu.roll(cells[0][role][p], zf, 1) for role in range(4)]
            for x in range(10):
                if last and x in (0, 9):
                    continue
                role = 1 if x in (0, 9) else 0
                near = min(max(x - 1, 0), 7)
                for t in range(TILES):
                    column = roll(turned[role], -(8 * t + near))
                    rows = pl.ds(x * PY + 8 + 8 * t, 8)
                    fld[p, rows, :] = fld[p, rows, :] + jnp.where(at_face, column, cor[k, p, rows, :])
                if last:
                    continue
                for t, at, y in ((0, 0, 7), (TILES - 1, 7, 40)):
                    column = roll(turned[2 + role], -(8 * t + near))[at:at + 1]
                    place = pl.ds(x * PY + y, 1)
                    fld[p, place, :] = fld[p, place, :] + jnp.where(at_face[0:1], column, cor[k, p, place, :])
            if not last:
                for role in range(4):
                    fz[role, p] = fz[role, p] + cells[1][role][p]

    def term(p, role, t, x, height=8):
        at_qx = (0 if x == 0 else 3) if role % 2 else 1 + x // 4
        at_qy = (0 if t == 0 else 5) if role // 2 else 1 + t
        return jnp.broadcast_to(cval[p, pl.ds(at_qx * 6 + at_qy, 1), :], (height, 128))

    def add_coarse(last):
        for p in range(2):
            for x in range(10):
                if last and x in (0, 9):
                    continue
                role = 1 if x in (0, 9) else 0
                near = min(max(x - 1, 0), 7)
                for t in range(TILES):
                    value = term(p, role, t, near)
                    rows = pl.ds(x * PY + 8 + 8 * t, 8)
                    if last:
                        out[p, x - 1, pl.ds(8 * t, 8), :] = fld[p, rows, :] + value
                    else:
                        coa[p, rows, :] = value
                if last:
                    continue
                for t, y in ((0, 7), (TILES - 1, 40)):
                    place = pl.ds(x * PY + y, 1)
                    value = term(p, 2 + role, t, near, 1)
                    coa[p, place, :] = value
            if not last:
                other = cval[p, pl.ds(24, 24), :]
                for role in range(4):
                    halo = jnp.broadcast_to(jnp.sum(other * zmask[role], axis=0, keepdims=True), (8, 128))
                    coz[role, p] = halo

    def keep_coarse():
        for p in range(2):
            for x in range(10):
                for y, height in ((7, 1), (8, 32), (40, 1)):
                    rows = pl.ds(x * PY + y, height)
                    fld[p, rows, :] = fld[p, rows, :] + coa[p, rows, :]
            for role in range(4):
                fz[role, p] = fz[role, p] + coz[role, p]

    def coarse_row():
        values, smooth = [], []
        for p in range(2):
            c = cval[p]
            v = (2.0 * CZ - 1.0) * c[0:24] + 0.5 * c[24:48]
            for at in (1, 2):
                u = 7.0 * v[6 * at:6 * at + 6] + 0.5 * (v[6 * at - 6:6 * at] + v[6 * at + 6:6 * at + 12])
                smooth.append(15.0 * u[1:5] + 0.5 * (u[0:4] + u[2:6]))
                values.append(c[6 * at + 1:6 * at + 5])
        c_re, c_im = jnp.concatenate(values[0:2], axis=0), jnp.concatenate(values[2:4], axis=0)
        s_re, s_im = jnp.concatenate(smooth[0:2], axis=0), jnp.concatenate(smooth[2:4], axis=0)
        a, b = 16.0 * (4 * 8 * CZ) - own_k[0:8], own_k[8:16]
        total = jnp.concatenate([a * c_re - b * c_im - 2.0 * s_re, a * c_im + b * c_re - 2.0 * s_im], axis=0)
        return lanes_of(total, 16 * core)

    for k in range(SWEEPS):
        if k == 0:
            row_send[k, first_row] = row_of(first_pass(), 16 * core) + fixed_row
        else:
            row_send[k, first_row] = row - coarse_row()
        if k == 0:
            jacobi(k)
            pack_halo(k)
            pl.semaphore_wait(barrier, count)
            pair_copy(k).start()
            for_info(lambda copy: copy.start())
        else:
            pair_copy(k).start()
            add_coarse(False)
            residual_pass(coa, coz, res, flat=True)
            jacobi(k)
            for_planes(k, lambda copy: copy.start())
            pack_halo(k)
        far_halo(k, lambda copy: copy.start())
        near_halo(k, lambda copy: copy.start(), planes=k == 0)
        pair_copy(k).wait_recv()
        gather_start(k)
        if k == 0:
            for_info(lambda copy: copy.wait_recv(), True)
            setup_rounds()
        if k > 0:
            keep_coarse()
        pair_copy(k).wait_send()
        all_halo(k, lambda copy: copy.wait_send())
        if k == 0:
            for_info(lambda copy: copy.wait_send())
        all_halo(k, lambda copy: copy.wait_recv(), True)
        cells = sides_rounds(k)
        main_rounds(k)
        add_correction(k, cells)
        if k < SWEEPS - 1:
            row = row_of(residual_pass(fld, fz, src), 16 * core)
        gather_every(k).wait_recv()
        if k == 0:
            setup_aggregates()
        coarse_values(k)
        if k == SWEEPS - 1:
            add_coarse(True)
        gather_every(k).wait_send()


def solution(mesh):
    nx, ny = mesh.shape["gx"], mesh.shape["gy"]

    def step(adjoint_source, velocity, damping, face_rounds, aggregates):
        vmem = pl.BlockSpec(memory_space=pltpu.VMEM)
        hbm = pl.BlockSpec(memory_space=pltpu.MemorySpace.HBM)
        smem = pl.BlockSpec(memory_space=pltpu.SMEM)
        dma = pltpu.SemaphoreType.DMA
        tile = (8, 128)
        block = (CX, CY, CZ)
        return pl.pallas_call(
            functools.partial(kernel, nx, ny),
            out_shape=pltpu.VMEM((2,) + block, F32),
            in_specs=[hbm, hbm, hbm, smem, smem],
            out_specs=vmem,
            scratch_shapes=[
                pltpu.VMEM((2,) + block, F32), pltpu.VMEM(block, F32), pltpu.VMEM(block, F32), dma((3,)),
                pltpu.VMEM(block, F32), pltpu.VMEM(block, F32), pltpu.VMEM(block, F32), pltpu.VMEM(block, F32),
                pltpu.VMEM((2,) + block, F32),
                pltpu.VMEM((2, CX * PY, CZ), F32), pltpu.VMEM((2, CX * PY, CZ), F32),
                pltpu.VMEM((SWEEPS, 2, 10 * PY, CZ), F32),
                pltpu.VMEM((2, 10 * PY, CZ), F32),
                pltpu.VMEM((4, 2) + tile, F32),
                pltpu.VMEM((12,) + tile, F32), pltpu.VMEM((4, 4, 128), F32),
                pltpu.VMEM((1024, 128), BF16), pltpu.VMEM((2, 64, 128), F32), pltpu.VMEM((2, 64, 128), F32),
                pltpu.VMEM((4, 24, 128), F32), pltpu.VMEM((2, 10 * PY, CZ), F32), pltpu.VMEM((4, 2) + tile, F32),
                pltpu.VMEM((16, 128), F32),
                pltpu.VMEM(tile, F32), pltpu.VMEM((2, 9) + tile, F32),
                pltpu.VMEM((SWEEPS, 6) + tile, F32), pltpu.VMEM((SWEEPS, 4) + tile, F32), pltpu.VMEM((SWEEPS, 2, 9) + tile, F32),
                pltpu.VMEM((SWEEPS, 2, 3) + tile, F32), pltpu.VMEM((SWEEPS, 4) + tile, F32),
                pltpu.VMEM((SWEEPS,) + tile, F32), pltpu.VMEM((SWEEPS,) + tile, F32), pltpu.VMEM((SWEEPS,) + tile, F32),
                pltpu.VMEM((SWEEPS, 128, 128), F32),
                dma((18,)), dma((18,)), dma((SWEEPS, 18)), dma((SWEEPS, 18)),
                dma((SWEEPS, 2)), dma((SWEEPS, 2)), dma((SWEEPS,)), dma((SWEEPS,)), dma((SWEEPS,)), dma((SWEEPS,)),
            ],
            compiler_params=pltpu.CompilerParams(
                collective_id=0, has_side_effects=True, vmem_limit_bytes=56 * 1024 * 1024
            ),
        )(adjoint_source, velocity, damping, face_rounds, jnp.transpose(aggregates, (0, 2, 1)))

    placed = (
        P(None, "gx", "gy", "gz"),
        P("gx", "gy", "gz"),
        P("gx", "gy", "gz"),
        P("gx", "gy", "gz", None),
        P("gx", "gy", "gz"),
    )
    return jax.shard_map(
        step, mesh=mesh, in_specs=placed, out_specs=P(None, "gx", "gy", "gz"), check_vma=False
    )
```
